32 devices in a mesh: batch: 16 (over z, y, x), seq: 2 (over core).
Axes of the slice: x: 2, y: 2, z: 4, core: 2. Of those that a mesh axis runs over, the one named last changes fastest.
Arguments:
- inputs: bfloat16 [16, 1024, 768], P('batch', 'seq'), may hold values from -6 to 6
- history: bfloat16 [12, 16, 1024, 768], P(None, 'batch', 'seq'), may hold values from -6 to 6
- segment_ids: int32 [16, 1024], P('batch'), may hold values from 0 to 7, as said below
- cotangent: bfloat16 [16, 1024, 768], P('batch', 'seq'), may hold values from -7 to 7
- mix_weights: float32 [13], replicated, may hold values from 0.2 to 0.8
- attn_gain: bfloat16 [768], P(('batch', 'seq')), may hold values from 0.5 to 1.5
- query_weight: bfloat16 [768, 768], P(('batch', 'seq')), may hold values from -0.21875 to 0.21875
- key_weight: bfloat16 [768, 768], P(('batch', 'seq')), may hold values from -0.21875 to 0.21875
- value_weight: bfloat16 [768, 768], P(('batch', 'seq')), may hold values from -0.21875 to 0.21875
- output_weight: bfloat16 [768, 768], P(('batch', 'seq')), may hold values from -1.5 to 1.5
- mlp_gain: bfloat16 [768], P(('batch', 'seq')), may hold values from 0.5 to 1.5
- up_weight: bfloat16 [768, 3072], P(('batch', 'seq')), may hold values from -0.21875 to 0.21875
- down_weight: bfloat16 [3072, 768], P(('batch', 'seq')), may hold values from -0.109375 to 0.109375
Outputs:
- output: bfloat16 [16, 1024, 768], P('batch', 'seq')
- grad_inputs: float32 [16, 1024, 768], P('batch', 'seq')
- grad_history: bfloat16 [12, 16, 1024, 768], P(None, 'batch', 'seq')
- grad_mix_weights: float32 [13], replicated
- grad_attn_gain: float32 [768], P(('batch', 'seq'))
- grad_query_weight: float32 [768, 768], P(('batch', 'seq'))
- grad_key_weight: float32 [768, 768], P(('batch', 'seq'))
- grad_value_weight: float32 [768, 768], P(('batch', 'seq'))
- grad_output_weight: float32 [768, 768], P(('batch', 'seq'))
- grad_mlp_gain: float32 [768], P(('batch', 'seq'))
- grad_up_weight: float32 [768, 3072], P(('batch', 'seq'))
- grad_down_weight: float32 [3072, 768], P(('batch', 'seq'))
The draws below stay inside these ranges and needn't reach their ends.
Inputs may be any that keep to these rules, and one draw needn't show every extreme that they name: `segment_ids`: within a row the ids start at 0, never fall, and each id holds one document; in every row one document has tokens on both sides of the row's middle.
All inputs are finite; a program needn't handle non-finite values.
Results may differ from the reference program's by a relative error of at most 0.013.
Values may be sent and summed in bfloat16 or wider, within the bound.
A program may use at most 256 MiB of HBM per device.

```python
import math
import jax
import jax.numpy as jnp
from jax import lax

D = 768
HD = 64
FF = 3072
HIST = 12
ROW_LEN = 1024
ROWS = 16


def draw_segment_ids(key, part):
    key = jax.random.fold_in(key, 11)
    key_count = jax.random.fold_in(key, 1)
    key_score = jax.random.fold_in(key, 2)
    key_row = jax.random.fold_in(key, 3)
    most_docs = max(2, ROW_LEN // 128)
    order = jnp.arange(ROW_LEN, dtype=jnp.int32)
    middle = (order > ROW_LEN // 2 - ROW_LEN // 8) & (order <= ROW_LEN // 2 + ROW_LEN // 8)
    barred = middle | (order == 0)
    docs = jax.random.randint(key_count, (ROWS,), 1, most_docs + 1)
    chosen = jax.random.randint(key_row, (), 0, ROWS)
    docs = jnp.where(jnp.arange(ROWS, dtype=jnp.int32) == chosen, most_docs, docs).astype(jnp.int32)
    score = jax.random.randint(key_score, (ROWS, ROW_LEN), 0, ROW_LEN) * ROW_LEN + order[None, :]
    score = jnp.where(barred[None, :], score + ROW_LEN * ROW_LEN, score)
    ranks = jnp.argsort(jnp.argsort(score, axis=1, stable=True), axis=1, stable=True).astype(jnp.int32)
    starts = (ranks < (docs - 1)[:, None]) & jnp.logical_not(barred)[None, :]
    starts = starts | (order == 0)[None, :]
    return (jnp.cumsum(starts.astype(jnp.int32), axis=1) - 1).astype(jnp.int32)


def draw_cotangent(key, part):
    key = jax.random.fold_in(key, 7)
    rows = jnp.arange(ROWS, dtype=jnp.float32)[:, None, None]
    noise = jnp.clip(jax.random.normal(key, (ROWS, ROW_LEN, D), jnp.float32), -4.0, 4.0)
    scale = jnp.power(3.0, rows / ROWS - 0.5)
    return (noise * scale).astype(jnp.bfloat16)


def levels(rng, shape, cuts, low, largest):
    def one(dim, shards_of):
        heights = jax.random.uniform(jax.random.fold_in(jax.random.fold_in(rng, 6), dim), (shards_of,), jnp.float32, low / len(cuts), largest / len(cuts))
        return jnp.repeat(jnp.exp(heights), shape[dim] // shards_of).reshape((-1,) + (1,) * (len(shape) - dim - 1))

    loudness = one(*cuts[0])
    for cut in cuts[1:]:
        loudness = loudness * one(*cut)
    return loudness


def normal_values(rng, dims, deviation, bound, cuts=(), held_as=jnp.bfloat16):
    drawn = jax.random.normal(rng, dims, jnp.float32) * deviation
    if len(cuts) > 0:
        drawn = levels(rng, dims, cuts, -0.22, 0.18) * drawn
    return jnp.clip(drawn, min=-bound, max=bound).astype(held_as)


def setup_inputs(seed: int = 0) -> dict:
    arg_keys = jax.random.split(jax.random.key(seed), 14)
    return {
        "inputs": normal_values(arg_keys[0], (ROWS, ROW_LEN, D), 1.0, 6.0, ((0, 16), (1, 2))),
        "history": normal_values(arg_keys[1], (HIST, ROWS, ROW_LEN, D), 1.0, 6.0, ((1, 16), (2, 2))),
        "segment_ids": draw_segment_ids(jax.random.fold_in(arg_keys[13], 71), 0),
        "cotangent": draw_cotangent(jax.random.fold_in(arg_keys[13], 71), 0),
        "mix_weights": jnp.clip(jax.random.uniform(arg_keys[4], (HIST + 1,), jnp.float32, 0.2, 0.8), 0.2, 0.8),
        "attn_gain": jnp.clip(1.0 + 0.1 * jax.random.normal(arg_keys[5], (D,), jnp.float32), 0.5, 1.5).astype(jnp.bfloat16),
        "query_weight": normal_values(arg_keys[6], (D, D), D ** -0.5, 0.21875, ((0, 32),)),
        "key_weight": normal_values(arg_keys[7], (D, D), D ** -0.5, 0.21875, ((0, 32),)),
        "value_weight": normal_values(arg_keys[8], (D, D), D ** -0.5, 0.21875, ((0, 32),)),
        "output_weight": normal_values(arg_keys[9], (D, D), (D // 48) ** -0.5, 1.5, ((0, 32),)),
        "mlp_gain": jnp.clip(1.0 + 0.1 * jax.random.normal(arg_keys[10], (D,), jnp.float32), 0.5, 1.5).astype(jnp.bfloat16),
        "up_weight": normal_values(arg_keys[11], (D, FF), D ** -0.5, 0.21875, ((0, 32),)),
        "down_weight": normal_values(arg_keys[12], (FF, D), FF ** -0.5, 0.109375, ((0, 32),)),
    }


EPSILON = 1e-05
MASKED = -1000000000.0
HIGHEST = lax.Precision.HIGHEST

@jax.custom_vjp
def low(v):
    return lax.optimization_barrier(v.astype(jnp.bfloat16)).astype(jnp.float32)

@jax.custom_vjp
def low_back(v):
    return v

def low_keep(v):
    return (low(v), None)

def low_pass(kept, grad):
    return (grad,)

def back_keep(v):
    return (v, None)

def back_low(kept, grad):
    return (low(grad),)
low.defvjp(low_keep, low_pass)
low_back.defvjp(back_keep, back_low)

def layer_norm(value, gain):
    mean = lax.optimization_barrier(jnp.mean(value, axis=-1, keepdims=True))
    centred = value - mean
    variance = lax.optimization_barrier(jnp.mean(centred * centred, axis=-1, keepdims=True))
    return centred * lax.rsqrt(variance + EPSILON) * gain

def rotate(value, angles):
    half = value.shape[-1] // 2
    cosine = jnp.cos(angles)[..., None, :]
    sine = jnp.sin(angles)[..., None, :]
    first = value[..., :half]
    second = value[..., half:]
    return jnp.concatenate([first * cosine - second * sine, second * cosine + first * sine], axis=-1)

def frequencies(size):
    return jnp.power(10000.0, -(2.0 / size) * jnp.arange(size // 2, dtype=jnp.float32))

def product(left, right):
    return jnp.dot(left, right, precision=HIGHEST, preferred_element_type=jnp.float32)

def row_positions(segment):
    order = jnp.arange(segment.shape[0], dtype=jnp.int32)
    before = lax.optimization_barrier(jnp.sum((segment[None, :] < segment[:, None]).astype(jnp.int32), axis=1))
    return order - before

def attend_row(packed):
    query, keys, values, segment = packed
    length = query.shape[0]
    order = jnp.arange(length)
    allowed = (segment[:, None] == segment[None, :]) & (order[None, :] <= order[:, None])
    scores = jnp.einsum('qhd,khd->hqk', query, keys, precision=HIGHEST) * HD ** (-0.5)
    scores = low_back(scores)
    scores = jnp.where(allowed[None], scores, MASKED)
    top = lax.optimization_barrier(jnp.max(scores, axis=-1, keepdims=True))
    raw = jnp.exp(scores - top)
    weights = raw / lax.optimization_barrier(jnp.sum(raw, axis=-1, keepdims=True))
    mixed = jnp.einsum('hqk,khd->qhd', low(weights), values, precision=HIGHEST)
    return low(low_back(mixed))

def block_forward(params, rows_in, history_in, segments):
    mixing, gain_one, query_weight, key_weight, value_weight, output_weight, gain_two, up_weight, down_weight = params
    groups, length, width = rows_in.shape
    heads = width // HD
    positions = jax.vmap(row_positions)(segments)
    angles = positions[..., None].astype(jnp.float32) * frequencies(HD)
    flat = rows_in.reshape(-1, width)
    normed = low(layer_norm(flat, gain_one))
    query = low_back(product(normed, query_weight)).reshape(groups, length, heads, HD)
    query = low(low_back(rotate(query, angles)))
    keys = low_back(product(normed, key_weight)).reshape(groups, length, heads, HD)
    keys = low(low_back(rotate(keys, angles)))
    values = low(low_back(product(normed, value_weight))).reshape(groups, length, heads, HD)
    mixed = lax.map(jax.checkpoint(attend_row), (query, keys, values, segments))
    attended = low_back(product(mixed.reshape(-1, width), output_weight))
    first = flat + attended
    second_in = low(layer_norm(first, gain_two))
    hidden_pre = low_back(product(second_in, up_weight))
    hidden = low(jax.nn.gelu(hidden_pre, approximate=True))
    block = first + low_back(product(hidden, down_weight))
    output = mixing[HIST] * block
    for index in range(HIST):
        output = output + mixing[index] * history_in[index].reshape(-1, width)
    return output.reshape(groups, length, width)

def reference(inputs, history, segment_ids, cotangent, mix_weights, attn_gain, query_weight, key_weight, value_weight, output_weight, mlp_gain, up_weight, down_weight):
    size = math.gcd(ROWS, max(1, 4096 // ROW_LEN))
    count = ROWS // size
    params = (mix_weights.astype(jnp.float32), attn_gain.astype(jnp.float32), query_weight.astype(jnp.float32), key_weight.astype(jnp.float32), value_weight.astype(jnp.float32), output_weight.astype(jnp.float32), mlp_gain.astype(jnp.float32), up_weight.astype(jnp.float32), down_weight.astype(jnp.float32))

    def split(value):
        return value.reshape((count, size) + value.shape[1:])
    stacked = (split(inputs), jnp.moveaxis(history.reshape(HIST, count, size, ROW_LEN, D), 1, 0), split(segment_ids), split(cotangent))
    zeros = tuple((jnp.zeros_like(param) for param in params))

    def one_group(totals, group):
        rows_in, history_in, segments, grad_out = group

        def forward(weights, rows_f, history_f):
            return block_forward(weights, rows_f, history_f, segments)
        output, pullback = jax.vjp(forward, params, rows_in.astype(jnp.float32), history_in.astype(jnp.float32))
        grad_params, grad_rows, grad_hist = pullback(grad_out.astype(jnp.float32))
        totals = tuple((left + right for left, right in zip(totals, grad_params)))
        return (totals, (output.astype(jnp.bfloat16), grad_rows, grad_hist.astype(jnp.bfloat16)))
    totals, outputs = lax.scan(one_group, zeros, stacked)
    output, grad_inputs, grad_history = outputs
    output = output.reshape(ROWS, ROW_LEN, D)
    grad_inputs = grad_inputs.reshape(ROWS, ROW_LEN, D)
    grad_history = jnp.moveaxis(grad_history, 0, 1).reshape(HIST, ROWS, ROW_LEN, D)
    return (output, grad_inputs, grad_history, totals[0], totals[1], totals[2], totals[3], totals[4], totals[5], totals[6], totals[7], totals[8])
```

```python
import functools

import jax
import jax.numpy as jnp
import numpy as np
from jax import lax
from jax.experimental import pallas as pl
from jax.experimental.pallas import tpu as pltpu
from jax.sharding import PartitionSpec as P

HD = 64
EPSILON = 1e-05
MASKED = -1000000000.0
MESH = pl.DeviceIdType.MESH
F32 = jnp.float32
BF16 = jnp.bfloat16
NZ, NY, NX = 4, 2, 2
GROUPS = NZ * NY * NX
COPIES = 224
BLOCK = 256


def mm(a, b):
    return lax.dot_general(a, b, (((1,), (0,)), ((), ())), preferred_element_type=F32)


def mm_nt(a, b):
    return lax.dot_general(a, b, (((1,), (1,)), ((), ())), preferred_element_type=F32)


def mm_tn(a, b):
    return lax.dot_general(a, b, (((0,), (0,)), ((), ())), preferred_element_type=F32)


def loop(count, body):
    def step(i, carry):
        body(i)
        return carry

    lax.fori_loop(0, count, step, 0)


def rows_of(i, size):
    return pl.ds(pl.multiple_of(i * size, size), size)


def lane_cut(start, size):
    return pl.ds(pl.multiple_of(start, 128), size)


def normalize(value):
    mean = jnp.mean(value, axis=-1, keepdims=True)
    centred = value - mean
    variance = jnp.mean(centred * centred, axis=-1, keepdims=True)
    root = lax.rsqrt(variance + EPSILON)
    return centred * root, root


def norm_back(xhat, root, gain, grad):
    g = grad * gain
    return root * (
        g - jnp.mean(g, axis=-1, keepdims=True) - xhat * jnp.mean(g * xhat, axis=-1, keepdims=True)
    )


def fold_rows(value):
    total = value[0:8]
    for r in range(8, value.shape[0], 8):
        total = total + value[r : r + 8]
    return total


class Place:
    def __init__(self, unit):
        batch = lax.axis_index("batch")
        self.k = lax.axis_index("seq")
        self.o = 1 - self.k
        group = batch // unit
        self.unit = unit
        self.u = batch % unit
        self.z = group // (NY * NX)
        self.y = (group // NX) % NY
        self.x = group % NX
        self.core = (batch, self.o)
        self.xn = self.device(self.z, self.y, 1 - self.x)
        self.yn = self.device(self.z, 1 - self.y, self.x)

    def device(self, z, y, x):
        return (((z * NY + y) * NX + x) * self.unit + self.u, self.k)

    def ahead(self, step):
        return (self.z + step) % NZ

    def behind(self, step):
        return (self.z + NZ - step) % NZ

    def zn(self, step):
        return self.device(self.ahead(step), self.y, self.x)


class Wire:
    def __init__(self, send, recv):
        self.send = send
        self.recv = recv
        self.open = []
        self.count = 0

    def copy(self, src, dst, device):
        i = self.count
        self.count += 1
        made = pltpu.make_async_remote_copy(
            src_ref=src,
            dst_ref=dst,
            send_sem=self.send.at[i],
            recv_sem=self.recv.at[i],
            device_id=device,
            device_id_type=MESH,
        )
        made.start()
        self.open.append(made)
        return made

    def sent(self, made):
        made.wait_send()
        self.open = [one for one in self.open if one is not made]

    def close(self):
        for made in self.open:
            made.wait_send()


class Gather:
    def __init__(self, wire, at, ref, cut):
        self.wire, self.at, self.ref, self.cut = wire, at, ref, cut
        self.z = {}
        self.mid = {}
        self.last = {}

    def start(self):
        at, ref = self.at, self.ref
        own = ref.at[at.z, at.y, at.x]
        for step in range(1, NZ):
            self.z[step] = self.wire.copy(own, own, at.zn(step))
        self.pass_mid(0)

    def pass_mid(self, step):
        at, ref, cut = self.at, self.ref, self.cut
        if step:
            self.z[step].wait_recv()
        zz = at.behind(step)
        left = ref.at[zz, at.y, at.x, :, :cut]
        right = ref.at[zz, at.y, at.x, :, cut:]
        self.mid[step] = (
            self.wire.copy(left, left, at.xn),
            self.wire.copy(right, right, at.yn),
        )

    def pass_last(self, step):
        at, ref, cut = self.at, self.ref, self.cut
        zz = at.behind(step)
        self.mid[step][0].wait_recv()
        left = ref.at[zz, at.y, :, :, :cut]
        one = self.wire.copy(left, left, at.yn)
        self.mid[step][1].wait_recv()
        right = ref.at[zz, :, at.x, :, cut:]
        self.last[step] = (one, self.wire.copy(right, right, at.xn))

    def finish(self):
        for step in range(NZ):
            for made in self.last[step]:
                made.wait_recv()

    def steps(self):
        return [
            self.start,
            lambda: (self.pass_mid(1), self.pass_last(0)),
            lambda: (self.pass_mid(2), self.pass_last(1)),
            lambda: (self.pass_mid(3), self.pass_last(2)),
            lambda: self.pass_last(3),
        ]


class Reduce:
    def __init__(self, wire, at, grad, cut, one_a, one_b, two, three):
        self.wire, self.at, self.grad, self.cut = wire, at, grad, cut
        self.one_a, self.one_b, self.two, self.three = one_a, one_b, two, three

    def first(self):
        at, grad, cut = self.at, self.grad, self.cut
        self.a = self.wire.copy(grad.at[:, 1 - at.y, :, :, :cut], self.one_a, at.yn)
        self.b = self.wire.copy(grad.at[:, :, 1 - at.x, :, cut:], self.one_b, at.xn)

    def second(self):
        at, grad, cut = self.at, self.grad, self.cut
        self.a.wait_recv()

        def add_a(xx):
            def body(zz):
                grad[zz, at.y, xx, :, :cut] = (
                    grad[zz, at.y, xx, :, :cut].astype(F32) + self.one_a[zz, xx].astype(F32)
                ).astype(BF16)

            loop(NZ, body)

        def add_b(yy):
            def body(zz):
                grad[zz, yy, at.x, :, cut:] = (
                    grad[zz, yy, at.x, :, cut:].astype(F32) + self.one_b[zz, yy].astype(F32)
                ).astype(BF16)

            loop(NZ, body)

        add_a(1 - at.x)
        self.aa = self.wire.copy(
            grad.at[:, at.y, 1 - at.x, :, :cut], self.two.at[:, :, :cut], at.xn
        )
        self.b.wait_recv()
        add_b(1 - at.y)
        self.bb = self.wire.copy(
            grad.at[:, 1 - at.y, at.x, :, cut:], self.two.at[:, :, cut:], at.yn
        )
        add_a(at.x)
        add_b(at.y)

    def third(self):
        at, grad = self.at, self.grad
        self.aa.wait_recv()
        self.bb.wait_recv()

        def body(zz):
            grad[zz, at.y, at.x] = (
                grad[zz, at.y, at.x].astype(F32) + self.two[zz].astype(F32)
            ).astype(BF16)

        loop(NZ, body)
        self.z = [
            self.wire.copy(grad.at[at.ahead(step), at.y, at.x], self.three.at[step - 1], at.zn(step))
            for step in range(1, NZ)
        ]

    def result(self):
        at = self.at
        total = self.grad[at.z, at.y, at.x].astype(F32)
        for step in range(1, NZ):
            self.z[step - 1].wait_recv()
            total = total + self.three[step - 1].astype(F32)
        return total


def layer(unit, names, *refs):
    (
        seg_ref, freq_ref, mix_ref, gains_ref, in_ref, cot_ref,
        q_ref, k_ref, v_ref, o_ref, up_ref, down_ref, hist_ref,
        out_ref, gin_ref, gq_ref, gk_ref, gv_ref, go_ref, gup_ref, gdown_ref, small_ref,
    ) = refs[:22]
    s = dict(zip(names, refs[22:]))
    tokens, width = in_ref.shape
    length = 2 * tokens
    half = width // 2
    ff_half = up_ref.shape[1] // 2
    pairs = half // 128
    share = q_ref.shape[0]
    down_rows = down_ref.shape[0]
    blocks = length // BLOCK
    hist = hist_ref.shape[0]
    at = Place(unit)
    k, o = at.k, at.o
    wire = Wire(s["send"], s["recv"])

    hist_rows = s["hbuf"].shape[2]
    hist_chunks = tokens // hist_rows

    def fetch(i):
        return pltpu.make_async_copy(
            hist_ref.at[:, pl.ds(i * hist_rows, hist_rows)], s["hbuf"].at[i % 2], s["hsem"].at[i % 2]
        )

    fetch(0).start()

    xs, xr = s["xs"], s["xr"]
    qkv_cols = 3 * half
    blk = down_rows
    for h in range(2):
        c = h * half
        for i in range(pairs):
            for j, ref in enumerate((q_ref, k_ref, v_ref)):
                xs[h, :, 384 * i + 128 * j : 384 * i + 128 * j + 128] = ref[
                    :, c + 128 * i : c + 128 * i + 128
                ].astype(F32)
        xs[h, :, qkv_cols : qkv_cols + half] = o_ref[:, c : c + half].astype(F32)
        wide = up_ref[...].astype(F32)
        xs[h, :, qkv_cols + half :] = jnp.concatenate(
            [
                wide[:, 2 * blk * i + blk * h : 2 * blk * i + blk * h + blk]
                for i in range(GROUPS)
            ],
            axis=1,
        )
    ga = s["ga"]
    ga[k, at.z, at.y, at.x] = gains_ref[...]

    barrier = pltpu.get_barrier_semaphore()
    for device in (at.core, at.xn, at.yn, at.zn(1), at.zn(2), at.zn(3)):
        pl.semaphore_signal(barrier, inc=1, device_id=device, device_id_type=MESH)
    pl.semaphore_wait(barrier, 6)

    swap = wire.copy(xs.at[o], xr, at.core)
    gain_z = [
        wire.copy(ga.at[k, at.z, at.y, at.x], ga.at[k, at.z, at.y, at.x], at.zn(step))
        for step in range(1, NZ)
    ]
    s["wdown"][at.z, at.y, at.x] = down_ref[...]

    own0 = pl.multiple_of(k * tokens, tokens)
    other0 = pl.multiple_of(o * tokens, tokens)

    def own(i, size):
        return pl.ds(pl.multiple_of(own0 + i * size, size), size)

    def other(i, size):
        return pl.ds(pl.multiple_of(other0 + i * size, size), size)

    mix_last = mix_ref[hist]
    gbl, norm, sec, gfl = s["gbl"], s["norm"], s["sec"], s["gfl"]

    swap.wait_recv()
    mine = xs[k]
    theirs = xr[...]
    upper = jnp.where(k == 0, mine, theirs)
    lower = jnp.where(k == 0, theirs, mine)
    block = jnp.concatenate([upper, lower], axis=0).astype(BF16)
    s["wqkv"][at.z, at.y, at.x] = block[:, :qkv_cols]
    s["wo"][at.z, at.y, at.x] = block[:, qkv_cols : qkv_cols + half]
    s["wup"][at.z, at.y, at.x] = block[:, qkv_cols + half :]

    gather_qkv = Gather(wire, at, s["wqkv"], 640)
    gather_o = Gather(wire, at, s["wo"], 128)
    gather_up = Gather(wire, at, s["wup"], ff_half // 2)
    gather_down = Gather(wire, at, s["wdown"], half)
    gather_qkv.start()
    todo = gather_qkv.steps()[1:]

    def pump(count=1):
        for _ in range(count):
            if todo:
                todo.pop(0)()

    seg = seg_ref[...].astype(F32)
    seg_col = jnp.transpose(jnp.broadcast_to(seg, (128, length)))
    start_row = jnp.zeros((1, length), F32)
    start_col = jnp.zeros((length, 128), F32)
    for d in range(7):
        count = jnp.sum(jnp.where(seg == d, 1.0, 0.0), axis=1, keepdims=True)
        start_row = start_row + jnp.where(seg > d, count, 0.0)
        start_col = start_col + jnp.where(seg_col > d, count, 0.0)
    s["start_row"][...] = jnp.broadcast_to(start_row, (8, length))
    s["start_col"][...] = start_col
    lane = lax.broadcasted_iota(jnp.int32, (1, 128), 1)
    first_half = (lane % HD) < (HD // 2)

    for step in range(1, NZ):
        gain_z[step - 1].wait_recv()
    gain_x = wire.copy(ga.at[k, :, at.y, at.x], ga.at[k, :, at.y, at.x], at.xn)

    def rope_tables(i):
        rows = rows_of(i, 64)
        order = (lax.broadcasted_iota(jnp.int32, (64, 128), 0) + i * 64).astype(F32)
        angles = (order - s["start_col"][rows, :]) * freq_ref[0:1, :]
        s["cos"][rows, :] = jnp.cos(angles)
        sine = jnp.sin(angles)
        s["sin"][rows, :] = jnp.where(first_half, -sine, sine)

    loop(length // 64, rope_tables)
    gain_x.wait_recv()
    gain_y = wire.copy(ga.at[k, :, at.y], ga.at[k, :, at.y], at.yn)
    pump()

    def low_block(i):
        gbl[own(i, 32), :] = (mix_last * cot_ref[rows_of(i, 32), :].astype(F32)).astype(BF16)

    loop(tokens // 32, low_block)
    send_gbl = wire.copy(
        gbl.at[pl.ds(own0, tokens)], gbl.at[pl.ds(own0, tokens)], at.core
    )
    gain_y.wait_recv()
    gain_c = wire.copy(ga.at[k], ga.at[k], at.core)

    def history_chunk(i):
        if i + 1 < hist_chunks:
            fetch(i + 1).start()
        fetch(i).wait()

        def group(r, sums):
            rows = rows_of(r, 16)
            whole = pl.ds(pl.multiple_of(i * hist_rows + r * 16, 16), 16)
            cot = cot_ref[whole, :].astype(F32)
            total = jnp.zeros((16, width), F32)
            out = []
            for j in range(hist):
                earlier = s["hbuf"][i % 2, j, rows, :].astype(F32)
                total = total + mix_ref[j] * earlier
                term = fold_rows(earlier * cot)
                part = sums[j]
                for c in range(0, width, 128):
                    part = part + term[:, c : c + 128]
                out.append(part)
            s["acc"][whole, :] = total
            return tuple(out)

        sums = lax.fori_loop(
            0, hist_rows // 16, group, tuple(s["mixacc"][j] for j in range(hist))
        )
        for j in range(hist):
            s["mixacc"][j] = sums[j]

    s["mixacc"][...] = jnp.zeros_like(s["mixacc"])
    history_chunk(0)
    gain_c.wait_recv()

    lanes = lax.broadcasted_iota(jnp.int32, (128, width), 1).astype(F32)
    rows_i = lax.broadcasted_iota(jnp.int32, (128, width), 0)
    owner = jnp.floor((lanes + 0.5) * (1.0 / share))
    spread = jnp.where(lanes - share * owner == rows_i.astype(F32), 1.0, 0.0).astype(BF16)
    gain_rows = [jnp.zeros((1, width), F32), jnp.zeros((1, width), F32)]
    for kk in range(2):
        tiles = ga[kk].reshape(GROUPS * 8, 128).astype(BF16)
        wide = mm(tiles, spread)
        for r in range(2):
            hit = ((rows_i % 8) == r) & (owner == (2 * (rows_i // 8) + kk).astype(F32))
            gain_rows[r] = gain_rows[r] + jnp.sum(
                jnp.where(hit, wide, 0.0), axis=0, keepdims=True
            )
    s["gain"][...] = jnp.concatenate([gain_rows[0], gain_rows[1], jnp.zeros((6, width), F32)], axis=0)

    def norm_one(i):
        xhat, _ = normalize(in_ref[rows_of(i, 32), :].astype(F32))
        norm[own(i, 32), :] = (xhat * s["gain"][0:1, :]).astype(BF16)

    loop(tokens // 32, norm_one)
    send_norm = wire.copy(norm.at[pl.ds(own0, tokens)], norm.at[pl.ds(own0, tokens)], at.core)
    pump()
    for i in range(1, hist_chunks):
        history_chunk(i)
        if i % 2 == 0:
            pump()
    pump(4)
    gather_o.start()
    gather_up.start()
    todo.extend(gather_o.steps()[1:4])
    todo.append(lambda: (gather_o.pass_last(3), gather_up.pass_mid(1), gather_up.pass_last(0)))
    todo.append(gather_down.start)
    todo.extend(gather_up.steps()[2:])
    todo.extend(gather_down.steps()[1:])
    send_norm.wait_recv()
    send_gbl.wait_recv()
    gather_qkv.finish()

    qs, ks, vs = s["q"], s["kk"], s["v"]

    def turn(value, rows, sign):
        partner = jnp.where(first_half, pltpu.roll(value, 96, 1), pltpu.roll(value, 32, 1))
        return value * s["cos"][rows, :] + (sign * partner) * s["sin"][rows, :]

    def project(i):
        rows = rows_of(i, BLOCK)
        left = norm[rows, :]
        for p in range(pairs):
            wide = mm(left, s["wqkv"][:, :, :, :, 384 * p : 384 * p + 384].reshape(width, 384))
            cols = slice(128 * p, 128 * p + 128)
            qs[rows, cols] = (turn(wide[:, :128], rows, 1.0).astype(BF16) * HD**-0.5).astype(BF16)
            ks[rows, cols] = turn(wide[:, 128:256], rows, 1.0).astype(BF16)
            vs[rows, cols] = wide[:, 256:].astype(BF16)

    loop(blocks, project)
    pump()

    lane_low = lane < HD
    ones = [
        jnp.where(lane_low, 1.0, 0.0).astype(BF16),
        jnp.where(lane_low, 0.0, 1.0).astype(BF16),
    ]

    def attend(p, b):
        cols = slice(128 * p, 128 * p + 128)
        r0 = b * BLOCK
        rows = slice(r0, r0 + BLOCK)
        here_q = lax.broadcasted_iota(jnp.int32, (BLOCK, BLOCK), 0)
        here_k = lax.broadcasted_iota(jnp.int32, (BLOCK, BLOCK), 1)
        start = s["start_col"][rows, 0:1]
        outs, tops = [], []
        for h in range(2):
            query = qs[rows, cols] * ones[h]
            near = mm_nt(query, ks[rows, cols])
            near = jnp.where(
                (here_k <= here_q) & ((here_k + r0).astype(F32) >= start), near, MASKED
            )
            top = jnp.max(near, axis=1, keepdims=True)
            if b:
                far = mm_nt(query, ks[0:r0, cols])
                far_k = lax.broadcasted_iota(jnp.int32, (1, r0), 1).astype(F32)
                far = jnp.where(far_k >= start, far, MASKED)
                top = jnp.maximum(top, jnp.max(far, axis=1, keepdims=True))
            raw = jnp.exp(near - top).astype(BF16)
            out = mm(raw, vs[rows, cols] * ones[h] + ones[1 - h])
            if b:
                raw = jnp.exp(far - top).astype(BF16)
                out = out + mm(raw, vs[0:r0, cols] * ones[h] + ones[1 - h])
            outs.append(out)
            tops.append(top)
        total = jnp.where(lane_low, pltpu.roll(outs[0], HD, 1), pltpu.roll(outs[1], HD, 1))
        mixed = jnp.where(lane_low, outs[0], outs[1]) / total
        s["mix"][rows, cols] = mixed.astype(BF16)
        s["mixf"][rows, cols] = mixed
        log_total = jnp.transpose(jnp.where(lane_low, tops[0], tops[1]) + jnp.log(total))
        s["lse"][p, 0:1, rows] = log_total[0:1]
        s["lse"][p, 1:2, rows] = log_total[HD : HD + 1]

    for p in range(pairs):
        for b in range(blocks):
            attend(p, b)
            if b in (1, 3):
                pump()

    gather_o.finish()
    wo, wox = s["wo"], s["wox"]
    swap_o = wire.copy(wo.at[pl.ds(2 * o, 2)], wox, at.core)
    swap_o.wait_recv()
    my_cols = lane_cut(k * half, half)
    other_cols = lane_cut(o * half, half)

    def output_weight():
        return (
            wo[pl.ds(2 * k, 2)].reshape(half, half),
            wox[...].reshape(half, half),
        )

    part_s, part_r = s["part_s"], s["part_r"]
    quarter = tokens // 2

    def send_parts(make, store, recv):
        made = []
        for i in range(2):
            make(other(i, quarter), rows_of(i, quarter), store)
            made.append(
                wire.copy(
                    store.at[pl.ds(i * quarter, quarter)], recv.at[pl.ds(i * quarter, quarter)], at.core
                )
            )
        return made

    def attended(rows, to, store):
        left = s["mix"][rows, :]
        one, two = output_weight()
        store[to, my_cols] = mm(left, one)
        store[to, other_cols] = mm(left, two)

    arrive = send_parts(attended, part_s, part_r)
    first = s["first"]
    for i in range(2):
        attended(own(i, quarter), rows_of(i, quarter), first)
    pump()
    send_sec = []
    for i in range(2):
        arrive[i].wait_recv()

        def norm_two(j):
            rows = pl.ds(pl.multiple_of(i * quarter + j * 32, 32), 32)
            value = in_ref[rows, :].astype(F32) + (first[rows, :] + part_r[rows, :])
            first[rows, :] = value
            xhat, _ = normalize(value)
            to = pl.ds(pl.multiple_of(own0 + i * quarter + j * 32, 32), 32)
            sec[to, :] = (xhat * s["gain"][1:2, :]).astype(BF16)

        loop(quarter // 32, norm_two)
        send_sec.append(wire.copy(sec.at[own(i, quarter)], sec.at[own(i, quarter)], at.core))
    pump(9)
    gather_up.finish()
    hid, dgelu = s["hid"], s["dgelu"]
    wup, wdown = s["wup"], s["wdown"]
    sqrt_2_over_pi = float(np.sqrt(2.0 / np.pi).astype(np.float32))

    def expand(rows):
        left = sec[rows, :]
        step = 512
        for c in range(0, ff_half, step):
            v = mm(left, wup[:, :, :, :, c : c + step].reshape(width, step))
            vv = v * v
            t = jnp.tanh(sqrt_2_over_pi * (v + 0.044715 * (vv * v)))
            hid[rows, c : c + step] = (0.5 * v * (1.0 + t)).astype(BF16)
            dgelu[rows, c : c + step] = (
                0.5 * (1.0 + t)
                + (0.5 * sqrt_2_over_pi) * v * (1.0 - t * t) * (1.0 + 3 * 0.044715 * vv)
            ).astype(BF16)

    loop(tokens // 128, lambda j: expand(own(j, 128)))
    for i in range(2):
        send_sec[i].wait_recv()
        loop(quarter // 128, lambda j: expand(
            pl.ds(pl.multiple_of(other0 + i * quarter + j * 128, 128), 128)
        ))

    gdown = s["gdown"]

    def grad_down(zz):
        left = hid[:, pl.ds(pl.multiple_of(zz * 384, 128), 384)]
        wide = mm_tn(left, gbl[...]).astype(BF16)
        for i in range(2):
            gdown[i][zz] = wide[:, i * half : (i + 1) * half].reshape(NY, NX, down_rows, half)

    loop(NZ, grad_down)
    reduce_down = [
        Reduce(wire, at, gdown[i], (256, 128)[i], *s["rdown"][i]) for i in range(2)
    ]
    for r in reduce_down:
        r.first()
    pump(9)
    gather_down.finish()

    def back_hidden(rows, to, store):
        for j in range(rows.size // 128):
            part = pl.ds(pl.multiple_of(rows.start + j * 128, 128), 128)
            for c in range(0, ff_half, 512):
                weight = wdown[:, :, :, :, :].reshape(ff_half, width)[c : c + 512]
                grad = mm_nt(gbl[part, :], weight)
                dgelu[part, c : c + 512] = (
                    grad * dgelu[part, c : c + 512].astype(F32)
                ).astype(BF16)
        store[to, :] = mm_nt(dgelu[rows, :], wup[...].reshape(width, ff_half))

    for made in arrive:
        wire.sent(made)
    arrive = send_parts(back_hidden, part_s, part_r)
    gsec = s["gfirst"]
    for i in range(2):
        back_hidden(own(i, quarter), rows_of(i, quarter), gsec)
    gup = s["gup"]

    def grad_up(j):
        left = sec[:, pl.ds(pl.multiple_of(j * 384, 128), 384)]
        for i in range(2):
            wide = mm_tn(left, dgelu[:, i * width : (i + 1) * width]).astype(BF16)
            gup[i][pl.ds(2 * j, 2)] = wide.reshape(2, NY, NX, 2 * share, width)

    small = s["small"]
    small[...] = jnp.zeros_like(small)

    def norm_two_back(i):
        arrive[i].wait_recv()

        def body(j, total):
            rows = pl.ds(pl.multiple_of(i * quarter + j * 32, 32), 32)
            grad = gsec[rows, :] + part_r[rows, :]
            xhat, root = normalize(first[rows, :])
            part = norm_back(xhat, root, s["gain"][1:2, :], grad)
            full = mix_last * cot_ref[rows, :].astype(F32) + part
            gsec[rows, :] = full
            to = pl.ds(pl.multiple_of(own0 + i * quarter + j * 32, 32), 32)
            gfl[to, :] = full.astype(BF16)
            return total + fold_rows(grad * xhat)

        total = lax.fori_loop(0, quarter // 32, body, jnp.zeros((8, width), F32))
        small[1:2, :] = small[1:2, :] + jnp.sum(total, axis=0, keepdims=True)
        return wire.copy(gfl.at[own(i, quarter)], gfl.at[own(i, quarter)], at.core)

    send_gfl = [norm_two_back(0), norm_two_back(1)]
    loop(2, grad_up)
    reduce_up = [
        Reduce(wire, at, gup[i], width // 2, *s["rup"][i]) for i in range(2)
    ]
    for r in reduce_up:
        r.first()
    for r in reduce_down:
        r.second()

    out_s, out_r = s["out_s"], s["out_r"]

    def contract(rows, to, store):
        store[to, :] = mm(hid[rows, :], wdown[...].reshape(ff_half, width))

    arrive_out = send_parts(contract, out_s, out_r)

    gm = s["gm"]

    def back_mixed(rows):
        one, two = output_weight()
        left = gfl[rows, my_cols]
        right = gfl[rows, other_cols]
        gm[rows, :] = (mm_nt(left, one) + mm_nt(right, two)).astype(BF16)

    back_mixed(own(0, tokens))
    for made in send_gfl:
        made.wait_recv()
    back_mixed(other(0, tokens))
    go = s["go"]
    left = s["mix"][...]
    go[pl.ds(2 * k, 2)] = mm_tn(left, gfl[:, my_cols]).astype(BF16).reshape(
        2, NY, NX, 2 * share, half
    )
    s["gox"][...] = mm_tn(left, gfl[:, other_cols]).astype(BF16).reshape(
        2, NY, NX, 2 * share, half
    )
    swap_go = wire.copy(s["gox"], go.at[pl.ds(2 * k, 2)], at.core)

    outb = s["outb"]
    block_sum = jnp.zeros((8, width), F32)
    for i in range(2):
        rows = pl.ds(i * quarter, quarter)
        mine_out = out_s
        wire.sent(arrive_out[i])
        contract(own(i, quarter), rows, mine_out)
        arrive_out[i].wait_recv()

        def finish_out(j, total):
            part = pl.ds(pl.multiple_of(i * quarter + j * 32, 32), 32)
            block = first[part, :] + (mine_out[part, :] + out_r[part, :])
            outb[part, :] = (s["acc"][part, :] + mix_last * block).astype(BF16)
            return total + fold_rows(block * cot_ref[part, :].astype(F32))

        block_sum = lax.fori_loop(0, quarter // 32, finish_out, block_sum)
    put_out = pltpu.make_async_copy(outb, out_ref, s["osem"].at[0])
    put_out.start()
    terms = jnp.zeros((1, width), F32)
    wide_lane = lax.broadcasted_iota(jnp.int32, (1, width), 1)
    for j in range(hist):
        terms = jnp.where(wide_lane == j, jnp.sum(s["mixacc"][j]), terms)
    terms = jnp.where(wide_lane == hist, jnp.sum(block_sum), terms)
    small[2:3, :] = terms
    swap_go.wait_recv()
    reduce_o = Reduce(wire, at, go, 128, *s["ro"])
    reduce_o.first()

    todo.extend([r.second for r in reduce_up])
    todo.extend([r.third for r in reduce_down])
    todo.append(reduce_o.second)
    todo.extend([r.third for r in reduce_up])
    todo.append(reduce_o.third)

    lse, delta = s["lse"], s["delta"]
    gqkv = s["hid"]
    gpair = s["gqkv"]
    grad_query = s["dq"]
    reduce_qkv = [
        Reduce(wire, at, gpair[p], (256, 128, 256)[p % 3], *s["rqkv"][p]) for p in range(pairs)
    ]

    def attend_back(p, b):
        cols = slice(128 * p, 128 * p + 128)
        r0 = b * BLOCK
        rows = slice(r0, r0 + BLOCK)
        after = slice(r0, length)
        count = length - r0
        here_k = lax.broadcasted_iota(jnp.int32, (BLOCK, count), 0)
        here_q = lax.broadcasted_iota(jnp.int32, (BLOCK, count), 1)
        allowed = (here_k <= here_q) & (
            (here_k + r0).astype(F32) >= s["start_row"][0:1, after]
        )
        key, value = ks[rows, cols], vs[rows, cols]
        query, grad = qs[after, cols], gm[after, cols]
        dk = jnp.zeros((BLOCK, 128), F32)
        dv = jnp.zeros((BLOCK, 128), F32)
        dq = jnp.zeros((count, 128), F32)
        for h in range(2):
            key_h = key * ones[h]
            scores = mm_nt(key_h, query)
            weights = jnp.exp(jnp.where(allowed, scores - lse[p, h : h + 1, after], MASKED))
            grad_w = mm_nt(value * ones[h], grad)
            grad_s = (weights * (grad_w - delta[p, h : h + 1, after])).astype(BF16)
            dv = dv + mm(weights.astype(BF16), grad * ones[h])
            dk = dk + mm(grad_s, query * ones[h])
            dq = dq + mm_tn(grad_s, key_h)
        base = 384 * p
        gqkv[rows, base + 256 : base + 384] = dv.astype(BF16)
        gqkv[rows, base + 128 : base + 256] = turn(
            dk.astype(BF16).astype(F32), rows, -1.0
        ).astype(BF16)
        if b == 0:
            grad_query[...] = dq
        else:
            grad_query[after, :] = grad_query[after, :] + dq

    for p in range(pairs):
        cols = slice(128 * p, 128 * p + 128)

        def inner(i):
            rows = rows_of(i, BLOCK)
            both = jnp.transpose(s["mixf"][rows, cols] * gm[rows, cols].astype(F32))
            delta[p, 0:1, rows] = jnp.sum(both[:HD], axis=0, keepdims=True)
            delta[p, 1:2, rows] = jnp.sum(both[HD:], axis=0, keepdims=True)

        loop(blocks, inner)
        for b in range(blocks):
            attend_back(p, b)
            if b in (1, 3):
                pump()

        def turn_query(i):
            rows = rows_of(i, BLOCK)
            low = (grad_query[rows, :] * HD**-0.5).astype(BF16).astype(F32)
            gqkv[rows, 384 * p : 384 * p + 128] = turn(low, rows, -1.0).astype(BF16)

        loop(blocks, turn_query)

        def grad_qkv(j):
            left = norm[:, pl.ds(pl.multiple_of(j * 384, 128), 384)]
            wide = mm_tn(left, gqkv[:, 384 * p : 384 * p + 384]).astype(BF16)
            gpair[p][pl.ds(2 * j, 2)] = wide.reshape(2, NY, NX, 2 * share, 384)

        loop(2, grad_qkv)
        reduce_qkv[p].first()
        if p:
            reduce_qkv[p - 1].second()
        if p > 1:
            reduce_qkv[p - 2].third()

    for made in arrive:
        wire.sent(made)

    def back_normed(rows, to, store):
        store[to, :] = mm_nt(gqkv[rows, :qkv_cols], s["wqkv"][...].reshape(width, qkv_cols))

    arrive = send_parts(back_normed, part_s, part_r)
    reduce_qkv[pairs - 1].second()
    pump(9)
    if pairs > 1:
        reduce_qkv[pairs - 2].third()
    own_s = out_s
    for i in range(2):
        back_normed(own(i, quarter), rows_of(i, quarter), own_s)
    reduce_qkv[pairs - 1].third()
    total = jnp.zeros((8, width), F32)
    for i in range(2):
        arrive[i].wait_recv()

        def norm_one_back(j, total):
            rows = pl.ds(pl.multiple_of(i * quarter + j * 32, 32), 32)
            grad = own_s[rows, :] + part_r[rows, :]
            xhat, root = normalize(in_ref[rows, :].astype(F32))
            gsec[rows, :] = gsec[rows, :] + norm_back(xhat, root, s["gain"][0:1, :], grad)
            return total + fold_rows(grad * xhat)

        total = lax.fori_loop(0, quarter // 32, norm_one_back, total)
    put_gin = pltpu.make_async_copy(gsec, gin_ref, s["osem"].at[1])
    put_gin.start()
    small[0:1, :] = jnp.sum(total, axis=0, keepdims=True)

    sr, sz = s["small_r"], s["small_z"]
    step_c = wire.copy(small, sr.at[0], at.core)

    fin, fin_r = s["fin"], s["fin_r"]
    mine_rows = pl.ds(pl.multiple_of(k * share, 8), share)
    other_rows = pl.ds(pl.multiple_of(o * share, 8), share)

    def settle(reduce, c, size):
        fin[:, c : c + size] = reduce.result()
        return wire.copy(
            fin.at[other_rows, pl.ds(c, size)], fin_r.at[:, pl.ds(c, size)], at.core
        )

    for i in range(2):
        gdown_ref[:, i * half : (i + 1) * half] = reduce_down[i].result()
    up0 = qkv_cols + half
    settled = [settle(reduce_up[i], up0 + i * width, width) for i in range(2)]
    settled.append(settle(reduce_o, qkv_cols, half))
    step_c.wait_recv()
    s["small1"][...] = small[...] + sr[0]
    step_y = wire.copy(s["small1"], sr.at[1], at.yn)
    for p in range(pairs - 1):
        settled.append(settle(reduce_qkv[p], 384 * p, 384))
    step_y.wait_recv()
    s["small2"][...] = s["small1"][...] + sr[1]
    step_x = wire.copy(s["small2"], sr.at[2], at.xn)
    settled.append(settle(reduce_qkv[pairs - 1], 384 * (pairs - 1), 384))
    step_x.wait_recv()
    sz[at.z] = s["small2"][...] + sr[2]
    step_z = [wire.copy(sz.at[at.z], sz.at[at.z], at.zn(step)) for step in range(1, NZ)]
    for made in settled:
        made.wait_recv()
    for p in range(pairs):
        for j, ref in enumerate((gq_ref, gk_ref, gv_ref)):
            c = 384 * p + 128 * j
            ref[:, lane_cut(k * half + 128 * p, 128)] = fin[mine_rows, c : c + 128]
            ref[:, lane_cut(o * half + 128 * p, 128)] = fin_r[:, c : c + 128]
    go_ref[:, my_cols] = fin[mine_rows, qkv_cols:up0]
    go_ref[:, other_cols] = fin_r[:, qkv_cols:up0]
    gup_ref[k] = fin[mine_rows, up0:]
    gup_ref[o] = fin_r[:, up0:]
    for made in step_z:
        made.wait_recv()
    small_ref[...] = ((sz[0] + sz[1]) + sz[2]) + sz[3]
    put_out.wait()
    put_gin.wait()
    wire.close()


def local(
    unit,
    devices,
    inputs,
    history,
    segment_ids,
    cotangent,
    mix_weights,
    attn_gain,
    query_weight,
    key_weight,
    value_weight,
    output_weight,
    mlp_gain,
    up_weight,
    down_weight,
):
    rows, tokens, width = inputs.shape
    hist = history.shape[0]
    length = segment_ids.shape[1]
    half = width // 2
    ff_half = up_weight.shape[1] // 2
    share = width // (2 * GROUPS)
    both = 2 * share
    down_share = 2 * ff_half // (2 * GROUPS)
    pairs = half // 128
    seq = lax.axis_index("seq")
    batch = lax.axis_index("batch")
    group_device = (batch // unit) * 2 + seq
    weights = [query_weight, key_weight, value_weight, output_weight, up_weight, down_weight]
    gains = [attn_gain, mlp_gain]
    if unit > 1:
        def widen(value):
            whole = lax.all_gather(value, ("batch", "seq"), axis=0, tiled=True)
            size = value.shape[0] * unit
            return lax.dynamic_slice_in_dim(whole, group_device * size, size)

        weights = [widen(value) for value in weights]
        gains = [widen(value) for value in gains]
    gain_tile = jnp.pad(jnp.stack(gains).astype(F32), ((0, 6), (0, 128 - share)))
    freq = (10000.0 ** (-(2.0 / HD) * (np.arange(128) % (HD // 2)))).astype(np.float32)
    freq = jnp.asarray(np.broadcast_to(freq, (8, 128)))

    sizes = []

    def scratch(name, shape, dtype=BF16):
        sizes.append((name, pltpu.VMEM(shape, dtype)))

    dims = (NZ, NY, NX)

    def reduction(rows_in, columns, cut):
        return [
            pltpu.VMEM((NZ, NX, rows_in, cut), BF16),
            pltpu.VMEM((NZ, NY, rows_in, columns - cut), BF16),
            pltpu.VMEM((NZ, rows_in, columns), BF16),
            pltpu.VMEM((NZ - 1, rows_in, columns), BF16),
        ]

    sizes.append(("send", pltpu.SemaphoreType.DMA((COPIES,))))
    sizes.append(("recv", pltpu.SemaphoreType.DMA((COPIES,))))
    sizes.append(("hsem", pltpu.SemaphoreType.DMA((2,))))
    sizes.append(("osem", pltpu.SemaphoreType.DMA((2,))))
    scratch("hbuf", (2, hist, 32, width))
    scratch("xs", (2, share, 2 * half + 2 * half + ff_half), F32)
    scratch("xr", (share, 2 * half + 2 * half + ff_half), F32)
    scratch("ga", (2,) + dims + (8, 128), F32)
    scratch("gain", (8, width), F32)
    scratch("wqkv", dims + (both, 3 * half))
    scratch("wo", dims + (both, half))
    scratch("wox", (2, NY, NX, both, half))
    scratch("wup", dims + (both, ff_half))
    scratch("wdown", dims + (down_share, width))
    for name in ("gbl", "norm", "sec", "gfl"):
        scratch(name, (length, width))
    scratch("start_row", (8, length), F32)
    scratch("start_col", (length, 128), F32)
    scratch("cos", (length, 128), F32)
    scratch("sin", (length, 128), F32)
    scratch("acc", (tokens, width), F32)
    scratch("mixacc", (hist, 8, 128), F32)
    for name in ("q", "kk", "v", "mix", "gm"):
        scratch(name, (length, half))
    scratch("mixf", (length, half), F32)
    scratch("lse", (pairs, 8, length), F32)
    scratch("delta", (pairs, 8, length), F32)
    scratch("dq", (length, 128), F32)
    for name in ("part_s", "part_r", "out_s", "out_r", "first", "gfirst"):
        scratch(name, (tokens, width), F32)
    scratch("outb", (tokens, width))
    scratch("hid", (length, ff_half))
    scratch("dgelu", (length, ff_half))
    scratch("gox", (2, NY, NX, both, half))
    for name in ("small", "small1", "small2"):
        scratch(name, (8, width), F32)
    scratch("small_r", (3, 8, width), F32)
    scratch("small_z", (NZ, 8, width), F32)
    scratch("fin", (both, 4 * half + ff_half), F32)
    scratch("fin_r", (share, 4 * half + ff_half), F32)
    sizes.append(("gdown", [pltpu.VMEM(dims + (down_share, half), BF16) for _ in range(2)]))
    sizes.append(("gup", [pltpu.VMEM(dims + (both, width), BF16) for _ in range(2)]))
    scratch("go", dims + (both, half))
    sizes.append(("gqkv", [pltpu.VMEM(dims + (both, 384), BF16) for _ in range(pairs)]))
    sizes.append(("rdown", [reduction(down_share, half, cut) for cut in (256, 128)]))
    sizes.append(("rup", [reduction(both, width, width // 2) for _ in range(2)]))
    sizes.append(("ro", reduction(both, half, 128)))
    sizes.append(("rqkv", [reduction(both, 384, (256, 128, 256)[p % 3]) for p in range(pairs)]))
    names = [name for name, _ in sizes]

    vmem = pl.BlockSpec(memory_space=pltpu.VMEM)
    anywhere = pl.BlockSpec(memory_space=pl.ANY)
    smem = pl.BlockSpec(memory_space=pltpu.SMEM)
    shape = jax.ShapeDtypeStruct
    outs = pl.pallas_call(
        functools.partial(layer, unit, names),
        out_shape=(
            shape((tokens, width), BF16),
            shape((tokens, width), F32),
            shape((share, width), F32),
            shape((share, width), F32),
            shape((share, width), F32),
            shape((share, width), F32),
            shape((2, share, ff_half), F32),
            shape((down_share, width), F32),
            shape((8, width), F32),
        ),
        in_specs=[vmem, vmem, smem] + [vmem] * 9 + [anywhere],
        out_specs=[anywhere, anywhere] + [vmem] * 7,
        scratch_shapes=[size for _, size in sizes],
        compiler_params=pltpu.CompilerParams(
            collective_id=0, has_side_effects=True, vmem_limit_bytes=64 * 1024 * 1024 - 64 * 1024
        ),
    )(
        segment_ids,
        freq,
        mix_weights,
        gain_tile,
        inputs.reshape(tokens, width),
        cotangent.reshape(tokens, width),
        *weights,
        history.reshape(hist, tokens, width),
    )
    output, grad_inputs, gq, gk, gv, go, gup, gdown, small = outs
    gup = (
        gup.reshape(2, share, GROUPS, down_share)
        .transpose(1, 2, 0, 3)
        .reshape(share, 2 * ff_half)
    )
    grads = [gq, gk, gv, go, gup, gdown]
    mix_grad = small[2, : hist + 1]
    device = batch * 2 + seq
    size = width // devices
    if unit > 1:
        def narrow(value):
            whole = jnp.zeros((value.shape[0] * 2 * GROUPS,) + value.shape[1:], F32)
            whole = lax.dynamic_update_slice_in_dim(whole, value, group_device * value.shape[0], 0)
            return lax.psum_scatter(whole, ("batch", "seq"), scatter_dimension=0, tiled=True)

        grads = [narrow(value) for value in grads]
        small = lax.psum(small, ("batch", "seq")) / (2 * GROUPS)
        mix_grad = small[2, : hist + 1]
    gain_one = lax.dynamic_slice(small, (0, device * size), (1, size))[0]
    gain_two = lax.dynamic_slice(small, (1, device * size), (1, size))[0]
    grad_history = (
        mix_weights[:-1, None, None, None] * cotangent.astype(F32)[None]
    ).astype(BF16)
    return (
        output.reshape(rows, tokens, width),
        grad_inputs.reshape(rows, tokens, width),
        grad_history,
        mix_grad,
        gain_one,
        grads[0],
        grads[1],
        grads[2],
        grads[3],
        gain_two,
        grads[4],
        grads[5],
    )


def solution(mesh):
    batch = mesh.shape["batch"]
    split = P(("batch", "seq"), None)
    gain = P(("batch", "seq"))
    placed = (
        P("batch", "seq", None),
        P(None, "batch", "seq", None),
        P("batch", None),
        P("batch", "seq", None),
        P(),
        gain,
        split,
        split,
        split,
        split,
        gain,
        split,
        split,
    )
    return jax.shard_map(
        functools.partial(local, batch // GROUPS, 2 * batch),
        mesh=mesh,
        in_specs=placed,
        out_specs=(
            P("batch", "seq", None),
            P("batch", "seq", None),
            P(None, "batch", "seq", None),
            P(),
            gain,
            split,
            split,
            split,
            split,
            gain,
            split,
            split,
        ),
        check_vma=False,
    )
```

```python
import functools

import jax
import jax.numpy as jnp
import numpy as np
from jax import lax
from jax.experimental import pallas as pl
from jax.experimental.pallas import tpu as pltpu
from jax.sharding import PartitionSpec as P

HD = 64
EPSILON = 1e-05
MASKED = -1000000000.0
MESH = pl.DeviceIdType.MESH
F32 = jnp.float32
BF16 = jnp.bfloat16
NZ, NY, NX = 4, 2, 2
GROUPS = NZ * NY * NX
COPIES = 183
SENDS = 48
CUTS = (256, 128, 256)
HBUF = 3
BLOCK = 256


def mm(a, b):
    return lax.dot_general(a, b, (((1,), (0,)), ((), ())), preferred_element_type=F32)


def mm_nt(a, b):
    return lax.dot_general(a, b, (((1,), (1,)), ((), ())), preferred_element_type=F32)


def mm_tn(a, b):
    return lax.dot_general(a, b, (((0,), (0,)), ((), ())), preferred_element_type=F32)


def loop(count, body):
    def step(i, carry):
        body(i)
        return carry

    lax.fori_loop(0, count, step, 0)


def rows_of(i, size):
    return pl.ds(pl.multiple_of(i * size, size), size)


def lane_cut(start, size):
    return pl.ds(pl.multiple_of(start, 128), size)


def normalize(value):
    mean = jnp.mean(value, axis=-1, keepdims=True)
    centred = value - mean
    variance = jnp.mean(centred * centred, axis=-1, keepdims=True)
    root = lax.rsqrt(variance + EPSILON)
    return centred * root, root


def norm_back(xhat, root, gain, grad):
    g = grad * gain
    return root * (
        g - jnp.mean(g, axis=-1, keepdims=True) - xhat * jnp.mean(g * xhat, axis=-1, keepdims=True)
    )


def fold_rows(value):
    total = value[0:8]
    for r in range(8, value.shape[0], 8):
        total = total + value[r : r + 8]
    return total


class Place:
    def __init__(self, unit):
        batch = lax.axis_index("batch")
        self.k = lax.axis_index("seq")
        self.o = 1 - self.k
        group = batch // unit
        self.unit = unit
        self.u = batch % unit
        self.z = group // (NY * NX)
        self.y = (group // NX) % NY
        self.x = group % NX
        self.core = (batch, self.o)
        self.xn = self.device(self.z, self.y, 1 - self.x)
        self.yn = self.device(self.z, 1 - self.y, self.x)
        self.diagonal = self.device(self.z, 1 - self.y, 1 - self.x)

    def device(self, z, y, x):
        return (((z * NY + y) * NX + x) * self.unit + self.u, self.k)

    def across(self, step):
        if step == 0:
            return self.z
        if step == 2:
            return (self.z + 2) % NZ
        flip = self.z + 1 - 2 * (self.z % 2)
        return flip if step == 1 else (flip + 2) % NZ

    def zn(self, step):
        return self.device(self.across(step), self.y, self.x)


class Wire:
    def __init__(self, send, recv):
        self.send = send
        self.recv = recv
        self.open = []
        self.count = 0

    def copy(self, src, dst, device):
        i = self.count
        self.count += 1
        while self.open and self.open[0][0] <= i - SENDS:
            self.open.pop(0)[1].wait_send()
        made = pltpu.make_async_remote_copy(
            src_ref=src,
            dst_ref=dst,
            send_sem=self.send.at[i % SENDS],
            recv_sem=self.recv.at[i],
            device_id=device,
            device_id_type=MESH,
        )
        made.start()
        self.open.append((i, made))
        return made

    def sent(self, *copies):
        for made in copies:
            if any(one is made for _, one in self.open):
                made.wait_send()
                self.open = [(i, one) for i, one in self.open if one is not made]

    def close(self):
        for _, made in self.open:
            made.wait_send()


class Gather:
    def __init__(self, wire, at, ref, a, b=None):
        self.wire, self.at, self.ref, self.a = wire, at, ref, a
        self.b = ref.shape[-1] if b is None else b
        self.third = self.b < ref.shape[-1]
        self.z, self.mid, self.last = {}, {}, {}
        self.cz = []

    def send_z(self, *steps):
        at = self.at
        own = self.ref.at[at.z, at.y, at.x]
        if self.third:
            own = self.ref.at[at.z, at.y, at.x, :, : self.b]
        for step in steps:
            self.z[step] = self.wire.copy(own, own, at.zn(step))

    def pass_mid(self, step):
        at, ref = self.at, self.ref
        if step:
            self.z[step].wait_recv()
        zz = at.across(step)
        left = ref.at[zz, at.y, at.x, :, : self.a]
        right = ref.at[zz, at.y, at.x, :, self.a : self.b]
        self.mid[step] = (
            self.wire.copy(left, left, at.xn),
            self.wire.copy(right, right, at.yn),
        )

    def pass_last(self, step):
        at, ref = self.at, self.ref
        zz = at.across(step)
        self.mid[step][0].wait_recv()
        left = ref.at[zz, at.y, :, :, : self.a]
        one = self.wire.copy(left, left, at.yn)
        self.mid[step][1].wait_recv()
        right = ref.at[zz, :, at.x, :, self.a : self.b]
        self.last[step] = (one, self.wire.copy(right, right, at.xn))

    def third_x(self):
        at = self.at
        part = self.ref.at[at.z, at.y, at.x, :, self.b :]
        self.cx = self.wire.copy(part, part, at.xn)

    def third_y(self):
        at = self.at
        self.cx.wait_recv()
        part = self.ref.at[at.z, at.y, :, :, self.b :]
        self.cy = self.wire.copy(part, part, at.yn)

    def third_z(self):
        at = self.at
        self.cy.wait_recv()
        part = self.ref.at[at.z, :, :, :, self.b :]
        self.cz = [self.wire.copy(part, part, at.zn(step)) for step in range(1, NZ)]

    def arrived(self, step):
        for made in self.last[step]:
            made.wait_recv()
        if self.third and step:
            self.cz[step - 1].wait_recv()

    def finish(self):
        for step in range(NZ):
            self.arrived(step)


class Reduce:
    def __init__(self, wire, at, grad, cuts, one_a, one_b, two, three, *third):
        self.wire, self.at, self.grad = wire, at, grad
        self.a, self.b = cuts
        self.one_a, self.one_b, self.two, self.three = one_a, one_b, two, three
        self.third_refs = third

    def add(self, index, more):
        self.grad[index] = (self.grad[index].astype(F32) + more.astype(F32)).astype(BF16)

    def first(self):
        at, grad, a, b = self.at, self.grad, self.a, self.b
        self.sa = self.wire.copy(grad.at[:, 1 - at.y, :, :, :a], self.one_a, at.yn)
        self.sb = self.wire.copy(grad.at[:, :, 1 - at.x, :, a:b], self.one_b, at.xn)
        if self.third_refs:
            self.cz = [
                self.wire.copy(
                    grad.at[at.across(step), :, :, :, b:], self.third_refs[0].at[step - 1], at.zn(step)
                )
                for step in range(1, NZ)
            ]

    def second(self):
        at, grad, a, b = self.at, self.grad, self.a, self.b
        left, right = slice(0, a), slice(a, b)

        def add_a(xx):
            loop(NZ, lambda zz: self.add((zz, at.y, xx, slice(None), left), self.one_a[zz, xx]))

        def add_b(yy):
            loop(NZ, lambda zz: self.add((zz, yy, at.x, slice(None), right), self.one_b[zz, yy]))

        self.sa.wait_recv()
        add_a(1 - at.x)
        self.saa = self.wire.copy(grad.at[:, at.y, 1 - at.x, :, :a], self.two.at[:, :, :a], at.xn)
        self.sb.wait_recv()
        add_b(1 - at.y)
        self.sbb = self.wire.copy(grad.at[:, 1 - at.y, at.x, :, a:b], self.two.at[:, :, a:], at.yn)
        add_a(at.x)
        add_b(at.y)

    def third(self):
        at, grad, b = self.at, self.grad, self.b
        self.saa.wait_recv()
        self.sbb.wait_recv()
        loop(NZ, lambda zz: self.add((zz, at.y, at.x, slice(None), slice(0, b)), self.two[zz]))
        self.sz = []
        for step in range(1, NZ):
            part = grad.at[at.across(step), at.y, at.x, :, :b]
            self.sz.append(self.wire.copy(part, self.three.at[step - 1], at.zn(step)))

    def third_y(self):
        at, grad, b = self.at, self.grad, self.b
        for made in self.cz:
            made.wait_recv()
        ref = self.third_refs[0]

        def body(yx):
            y, x = yx // NX, yx % NX
            more = ref[0, y, x].astype(F32) + ref[1, y, x].astype(F32) + ref[2, y, x].astype(F32)
            self.add((at.z, y, x, slice(None), slice(b, None)), more)

        loop(NY * NX, body)
        self.cy = self.wire.copy(grad.at[at.z, 1 - at.y, :, :, b:], self.third_refs[1], at.yn)

    def third_x(self):
        at, grad, b = self.at, self.grad, self.b
        self.cy.wait_recv()
        ref = self.third_refs[1]
        loop(NX, lambda x: self.add((at.z, at.y, x, slice(None), slice(b, None)), ref[x]))
        self.cx = self.wire.copy(grad.at[at.z, at.y, 1 - at.x, :, b:], self.third_refs[2], at.xn)

    def result(self):
        at, b = self.at, self.b
        total = self.grad[at.z, at.y, at.x, :, :b].astype(F32)
        for step in range(1, NZ):
            self.sz[step - 1].wait_recv()
            total = total + self.three[step - 1].astype(F32)
        return total

    def third_result(self):
        at = self.at
        self.cx.wait_recv()
        return self.grad[at.z, at.y, at.x, :, self.b :].astype(F32) + self.third_refs[2][
            ...
        ].astype(F32)


def layer(unit, names, *refs):
    (
        seg_ref, mix_ref, gain1_ref, gain2_ref, in_ref, cot_ref,
        q_ref, k_ref, v_ref, o_ref, up_ref, down_ref, hist_ref,
        out_ref, gin_ref, pack_ref, gdown_ref, small_ref,
    ) = refs[:18]
    s = dict(zip(names, refs[18:]))
    tokens, width = in_ref.shape
    length = 2 * tokens
    half = width // 2
    ff_half = up_ref.shape[1] // 2
    pairs = half // 128
    share = q_ref.shape[0]
    down_rows = down_ref.shape[0]
    blocks = length // BLOCK
    hist = hist_ref.shape[0]
    at = Place(unit)
    k, o = at.k, at.o
    wire = Wire(s["send"], s["recv"])

    hist_rows = s["hbuf"].shape[2]
    hist_chunks = tokens // hist_rows

    def fetch(i):
        return pltpu.make_async_copy(
            hist_ref.at[:, pl.ds(i * hist_rows, hist_rows)],
            s["hbuf"].at[i % HBUF],
            s["hsem"].at[i % HBUF],
        )

    for i in range(HBUF - 1):
        fetch(i).start()

    xs, xr = s["xs"], s["xr"]
    qkv_cols = 3 * half
    blk = down_rows
    for h in range(2):
        c = h * half
        for i in range(pairs):
            for j, ref in enumerate((q_ref, k_ref, v_ref)):
                xs[h, :, 384 * i + 128 * j : 384 * i + 128 * j + 128] = ref[
                    :, c + 128 * i : c + 128 * i + 128
                ].astype(F32)
        xs[h, :, qkv_cols : qkv_cols + half] = o_ref[:, c : c + half].astype(F32)
        wide = up_ref[...].astype(F32)
        xs[h, :, qkv_cols + half :] = jnp.concatenate(
            [
                wide[:, 2 * blk * i + blk * h : 2 * blk * i + blk * h + blk]
                for i in range(GROUPS)
            ],
            axis=1,
        )
    ga = s["ga"]
    ga[k, at.z, at.y, at.x] = jnp.zeros((8, 128), F32)
    ga[k, at.z, at.y, at.x, 0:1, :share] = gain1_ref[...].astype(F32)
    ga[k, at.z, at.y, at.x, 1:2, :share] = gain2_ref[...].astype(F32)

    barrier = pltpu.get_barrier_semaphore()
    for device in (at.core, at.xn, at.yn, at.diagonal, at.zn(1), at.zn(2), at.zn(3)):
        pl.semaphore_signal(barrier, inc=1, device_id=device, device_id_type=MESH)
    pl.semaphore_wait(barrier, 7)

    swap = wire.copy(xs.at[o], xr, at.core)
    gain_z = [
        wire.copy(ga.at[k, at.z, at.y, at.x], ga.at[k, at.z, at.y, at.x], at.zn(step))
        for step in range(1, NZ)
    ]
    s["wdown"][at.z, at.y, at.x] = down_ref[...]

    own0 = pl.multiple_of(k * tokens, tokens)
    other0 = pl.multiple_of(o * tokens, tokens)

    def own(i, size):
        return pl.ds(pl.multiple_of(own0 + i * size, size), size)

    def other(i, size):
        return pl.ds(pl.multiple_of(other0 + i * size, size), size)

    mix_last = mix_ref[hist]
    gbl, norm, sec, gfl = s["gbl"], s["norm"], s["sec"], s["gfl"]

    swap.wait_recv()
    mine = xs[k]
    theirs = xr[...]
    upper = jnp.where(k == 0, mine, theirs)
    lower = jnp.where(k == 0, theirs, mine)
    block = jnp.concatenate([upper, lower], axis=0).astype(BF16)
    s["wqkv"][at.z, at.y, at.x] = block[:, :qkv_cols]
    s["wo"][at.z, at.y, at.x] = block[:, qkv_cols : qkv_cols + half]
    s["wup"][at.z, at.y, at.x] = block[:, qkv_cols + half :]

    gather_qkv = Gather(wire, at, s["wqkv"], 640)
    gather_o = Gather(wire, at, s["wo"], 128)
    gather_up = Gather(wire, at, s["wup"], ff_half // 2)
    gather_down = Gather(wire, at, s["wdown"], width // 3, 2 * width // 3)
    gather_qkv.send_z(1, 2, 3)
    gather_qkv.pass_mid(0)
    gather_down.third_x()
    gather_up.pass_mid(0)
    todo = [
        lambda: (gather_qkv.pass_last(0), gather_o.send_z(1, 2, 3)),
        lambda: (
            gather_qkv.pass_mid(1),
            gather_o.pass_mid(0),
            gather_up.pass_last(0),
            gather_up.send_z(1),
        ),
        lambda: (gather_qkv.pass_last(1), gather_down.third_y(), gather_up.send_z(2, 3)),
        lambda: (gather_qkv.pass_mid(2), gather_down.pass_mid(0), gather_o.pass_last(0)),
        lambda: (gather_qkv.pass_mid(3), gather_qkv.pass_last(2)),
        lambda: (gather_qkv.pass_last(3), gather_down.send_z(1, 2, 3)),
        lambda: (
            gather_o.pass_mid(1),
            gather_o.pass_mid(2),
            gather_o.pass_mid(3),
            gather_up.pass_mid(1),
        ),
    ]
    later = [
        lambda: (gather_up.pass_mid(2), gather_up.pass_mid(3)),
        lambda: (gather_o.pass_last(1), gather_o.pass_last(2)),
        lambda: (gather_o.pass_last(3), gather_up.pass_last(1)),
        lambda: gather_down.third_z(),
        lambda: gather_up.pass_last(2),
        lambda: gather_up.pass_last(3),
        lambda: (gather_down.pass_mid(1), gather_down.pass_mid(2)),
        lambda: (gather_down.pass_last(0), gather_down.pass_mid(3)),
        lambda: gather_down.pass_last(1),
        lambda: gather_down.pass_last(2),
        lambda: gather_down.pass_last(3),
    ]

    def pump(count=1):
        for _ in range(count):
            if todo:
                todo.pop(0)()

    seg = seg_ref[...].astype(F32)
    seg_col = jnp.transpose(jnp.broadcast_to(seg, (128, length)))
    start_row = jnp.zeros((1, length), F32)
    start_col = jnp.zeros((length, 128), F32)
    for d in range(7):
        count = jnp.sum(jnp.where(seg == d, 1.0, 0.0), axis=1, keepdims=True)
        start_row = start_row + jnp.where(seg > d, count, 0.0)
        start_col = start_col + jnp.where(seg_col > d, count, 0.0)
    s["start_row"][...] = jnp.broadcast_to(start_row, (8, length))
    s["start_col"][...] = start_col
    lane = lax.broadcasted_iota(jnp.int32, (1, 128), 1)
    first_half = (lane % HD) < (HD // 2)

    def rope_tables(i):
        rows = rows_of(i, 64)
        order = (lax.broadcasted_iota(jnp.int32, (64, 128), 0) + i * 64).astype(F32)
        angles = (order - s["start_col"][rows, :]) * freq
        s["cos"][rows, :] = jnp.cos(angles)
        sine = jnp.sin(angles)
        s["sin"][rows, :] = jnp.where(first_half, -sine, sine)

    freq = jnp.zeros((1, 128), F32)
    for i in range(HD // 2):
        rate = float(np.float32(10000.0 ** (-2.0 * i / HD)))
        freq = jnp.where(lane % (HD // 2) == i, rate, freq)
    loop(length // 64, rope_tables)
    pump()
    for step in range(1, NZ):
        gain_z[step - 1].wait_recv()
    gain_x = wire.copy(ga.at[k, :, at.y, at.x], ga.at[k, :, at.y, at.x], at.xn)

    def low_block(i):
        gbl[own(i, 32), :] = (mix_last * cot_ref[rows_of(i, 32), :].astype(F32)).astype(BF16)

    loop(tokens // 32, low_block)
    send_gbl = wire.copy(
        gbl.at[pl.ds(own0, tokens)], gbl.at[pl.ds(own0, tokens)], at.core
    )
    pump()

    def history_chunk(i):
        if i + HBUF - 1 < hist_chunks:
            fetch(i + HBUF - 1).start()
        fetch(i).wait()

        def group(r, sums):
            rows = rows_of(r, 16)
            whole = pl.ds(pl.multiple_of(i * hist_rows + r * 16, 16), 16)
            cot = cot_ref[whole, :].astype(F32)
            total = jnp.zeros((16, width), F32)
            out = []
            for j in range(hist):
                earlier = s["hbuf"][i % HBUF, j, rows, :].astype(F32)
                total = total + mix_ref[j] * earlier
                term = fold_rows(earlier * cot)
                part = sums[j]
                for c in range(0, width, 128):
                    part = part + term[:, c : c + 128]
                out.append(part)
            s["acc"][whole, :] = total
            return tuple(out)

        sums = lax.fori_loop(
            0, hist_rows // 16, group, tuple(s["mixacc"][j] for j in range(hist))
        )
        for j in range(hist):
            s["mixacc"][j] = sums[j]

    s["mixacc"][...] = jnp.zeros_like(s["mixacc"])
    history_chunk(0)
    history_chunk(1)
    pump()
    history_chunk(2)
    history_chunk(3)
    pump()
    gain_x.wait_recv()
    gain_y = wire.copy(ga.at[k, :, at.y], ga.at[k, :, at.y], at.yn)
    history_chunk(4)
    history_chunk(5)
    pump()
    gain_y.wait_recv()
    gain_c = wire.copy(ga.at[k], ga.at[k], at.core)
    history_chunk(6)
    history_chunk(7)
    pump()
    gain_c.wait_recv()

    lanes = lax.broadcasted_iota(jnp.int32, (128, width), 1).astype(F32)
    rows_i = lax.broadcasted_iota(jnp.int32, (128, width), 0)
    owner = jnp.floor((lanes + 0.5) * (1.0 / share))
    spread = jnp.where(lanes - share * owner == rows_i.astype(F32), 1.0, 0.0).astype(BF16)
    gain_rows = [jnp.zeros((1, width), F32), jnp.zeros((1, width), F32)]
    for kk in range(2):
        tiles = ga[kk].reshape(GROUPS * 8, 128).astype(BF16)
        wide = mm(tiles, spread)
        for r in range(2):
            hit = ((rows_i % 8) == r) & (owner == (2 * (rows_i // 8) + kk).astype(F32))
            gain_rows[r] = gain_rows[r] + jnp.sum(
                jnp.where(hit, wide, 0.0), axis=0, keepdims=True
            )
    s["gain"][...] = jnp.concatenate([gain_rows[0], gain_rows[1], jnp.zeros((6, width), F32)], axis=0)

    def norm_one(i):
        xhat, _ = normalize(in_ref[rows_of(i, 128), :].astype(F32))
        norm[own(i, 128), :] = (xhat * s["gain"][0:1, :]).astype(BF16)

    loop(tokens // 128, norm_one)
    send_norm = wire.copy(norm.at[pl.ds(own0, tokens)], norm.at[pl.ds(own0, tokens)], at.core)
    pump()
    for i in range(8, hist_chunks):
        history_chunk(i)
    while len(todo) > 0:
        pump()
    todo.extend(later)
    send_norm.wait_recv()
    send_gbl.wait_recv()
    gather_qkv.finish()

    qs, ks, vs = s["q"], s["kk"], s["v"]

    def turn(value, rows, sign):
        partner = jnp.where(first_half, pltpu.roll(value, 96, 1), pltpu.roll(value, 32, 1))
        return value * s["cos"][rows, :] + (sign * partner) * s["sin"][rows, :]

    def project(i):
        rows = rows_of(i, BLOCK)
        left = norm[rows, :]
        for p in range(pairs):
            wide = mm(left, s["wqkv"][:, :, :, :, 384 * p : 384 * p + 384].reshape(width, 384))
            cols = slice(128 * p, 128 * p + 128)
            qs[rows, cols] = (turn(wide[:, :128], rows, 1.0).astype(BF16) * HD**-0.5).astype(BF16)
            ks[rows, cols] = turn(wide[:, 128:256], rows, 1.0).astype(BF16)
            vs[rows, cols] = wide[:, 256:].astype(BF16)

    for i in range(blocks):
        project(i)
        pump()

    lane_low = lane < HD
    ones = [
        jnp.where(lane_low, 1.0, 0.0).astype(BF16),
        jnp.where(lane_low, 0.0, 1.0).astype(BF16),
    ]

    def attend(p, b):
        cols = slice(128 * p, 128 * p + 128)
        r0 = b * tokens
        rows = slice(r0, r0 + tokens)
        here_q = lax.broadcasted_iota(jnp.int32, (tokens, tokens), 0)
        here_k = lax.broadcasted_iota(jnp.int32, (tokens, tokens), 1)
        start = s["start_col"][rows, 0:1]
        outs, tops = [], []
        for h in range(2):
            query = qs[rows, cols] * ones[h]
            near = mm_nt(query, ks[rows, cols])
            near = jnp.where(
                (here_k <= here_q) & ((here_k + r0).astype(F32) >= start), near, MASKED
            )
            top = jnp.max(near, axis=1, keepdims=True)
            if b:
                far = mm_nt(query, ks[0:r0, cols])
                far_k = lax.broadcasted_iota(jnp.int32, (1, r0), 1).astype(F32)
                far = jnp.where(far_k >= start, far, MASKED)
                top = jnp.maximum(top, jnp.max(far, axis=1, keepdims=True))
            raw = jnp.exp(near - top).astype(BF16)
            out = mm(raw, vs[rows, cols] * ones[h] + ones[1 - h])
            if b:
                raw = jnp.exp(far - top).astype(BF16)
                out = out + mm(raw, vs[0:r0, cols] * ones[h] + ones[1 - h])
            outs.append(out)
            tops.append(top)
        total = jnp.where(lane_low, pltpu.roll(outs[0], HD, 1), pltpu.roll(outs[1], HD, 1))
        mixed = jnp.where(lane_low, outs[0], outs[1]) / total
        s["mix"][rows, cols] = mixed.astype(BF16)
        s["mixf"][rows, cols] = mixed
        log_total = jnp.transpose(jnp.where(lane_low, tops[0], tops[1]) + jnp.log(total))
        s["lse"][p, 0:1, rows] = log_total[0:1]
        s["lse"][p, 1:2, rows] = log_total[HD : HD + 1]

    for p in range(pairs):
        for b in range(2):
            attend(p, b)
        pump()

    gather_o.finish()
    wo, wox = s["wo"], s["wox"]
    swap_o = wire.copy(wo.at[pl.ds(2 * o, 2)], wox, at.core)
    swap_o.wait_recv()
    my_cols = lane_cut(k * half, half)
    other_cols = lane_cut(o * half, half)

    def output_weight():
        return (
            wo[pl.ds(2 * k, 2)].reshape(half, half),
            wox[...].reshape(half, half),
        )

    part_s, part_r = s["part_s"], s["part_r"]
    quarter = tokens // 2

    def send_parts(make, store, recv):
        made = []
        for i in range(2):
            make(other(i, quarter), rows_of(i, quarter), store)
            made.append(
                wire.copy(
                    store.at[pl.ds(i * quarter, quarter)], recv.at[pl.ds(i * quarter, quarter)], at.core
                )
            )
        return made

    def attended(rows, to, store):
        left = s["mix"][rows, :]
        one, two = output_weight()
        store[to, my_cols] = mm(left, one)
        store[to, other_cols] = mm(left, two)

    arrive = send_parts(attended, part_s, part_r)
    first = s["first"]
    for i in range(2):
        attended(own(i, quarter), rows_of(i, quarter), first)
    send_sec = []
    for i in range(2):
        arrive[i].wait_recv()

        def norm_two(j):
            rows = pl.ds(pl.multiple_of(i * quarter + j * 128, 128), 128)
            value = in_ref[rows, :].astype(F32) + (first[rows, :] + part_r[rows, :])
            first[rows, :] = value
            xhat, _ = normalize(value)
            to = pl.ds(pl.multiple_of(own0 + i * quarter + j * 128, 128), 128)
            sec[to, :] = (xhat * s["gain"][1:2, :]).astype(BF16)

        loop(quarter // 128, norm_two)
        send_sec.append(wire.copy(sec.at[own(i, quarter)], sec.at[own(i, quarter)], at.core))
    pump()
    gather_up.finish()
    hid, dgelu = s["hid"], s["dgelu"]
    wup, wdown = s["wup"], s["wdown"]
    sqrt_2_over_pi = float(np.sqrt(2.0 / np.pi).astype(np.float32))

    def expand(start):
        rows = pl.ds(start, tokens)

        def body(j):
            cols = lane_cut(j * 256, 256)
            v = mm(sec[rows, :], wup[:, :, :, :, cols].reshape(width, 256))
            vv = v * v
            t = jnp.tanh(sqrt_2_over_pi * (v + 0.044715 * (vv * v)))
            hid[rows, cols] = (0.5 * v * (1.0 + t)).astype(BF16)
            dgelu[rows, cols] = (
                0.5 * (1.0 + t)
                + (0.5 * sqrt_2_over_pi) * v * (1.0 - t * t) * (1.0 + 3 * 0.044715 * vv)
            ).astype(BF16)

        loop(ff_half // 256, body)
        pump()

    expand(own0)
    for made in send_sec:
        made.wait_recv()
    expand(other0)

    gdown = s["gdown"]

    def grad_down(zz):
        left = hid[:, 384 * zz : 384 * zz + 384]
        wide = mm_tn(left, gbl[...]).astype(BF16)
        for i in range(2):
            gdown[i][zz] = wide[:, i * half : (i + 1) * half].reshape(NY, NX, down_rows, half)

    for zz in range(NZ):
        grad_down(zz)
        if zz % 2:
            pump()
    reduce_down = [
        Reduce(wire, at, gdown[i], (half // 3, 2 * half // 3), *s["rdown"][i]) for i in range(2)
    ]
    for r in reduce_down:
        r.first()

    def back_hidden(step):
        gather_down.arrived(step)
        zz = at.across(step)
        weight = wdown[zz].reshape(NY * NX * down_rows, width)
        cols = lane_cut(zz * 384, 384)
        for start in (0, tokens):
            rows = slice(start, start + tokens)
            grad = mm_nt(gbl[rows, :], weight)
            dgelu[rows, cols] = (grad * dgelu[rows, cols].astype(F32)).astype(BF16)

    back_hidden(0)
    pump()
    back_hidden(1)
    pump()
    back_hidden(2)
    assert not todo
    back_hidden(3)

    def back_second(rows, to, store):
        store[to, :] = mm_nt(dgelu[rows, :], wup[...].reshape(width, ff_half))

    wire.sent(*arrive)
    arrive = send_parts(back_second, part_s, part_r)
    reduce_down[0].second()
    gsec = s["gfirst"]
    back_second(own(0, tokens), slice(0, tokens), gsec)
    gup = s["gup"]
    small = s["small"]
    small[...] = jnp.zeros_like(small)

    def grad_up(j, i):
        left = sec[:, 384 * j : 384 * j + 384]
        wide = mm_tn(left, dgelu[:, i * width : (i + 1) * width]).astype(BF16)
        gup[i][2 * j : 2 * j + 2] = wide.reshape(2, NY, NX, 2 * share, width)

    def norm_two_back(i):
        arrive[i].wait_recv()

        def body(j, total):
            rows = pl.ds(pl.multiple_of(i * quarter + j * 64, 64), 64)
            grad = gsec[rows, :] + part_r[rows, :]
            xhat, root = normalize(first[rows, :])
            part = norm_back(xhat, root, s["gain"][1:2, :], grad)
            full = mix_last * cot_ref[rows, :].astype(F32) + part
            gsec[rows, :] = full
            to = pl.ds(pl.multiple_of(own0 + i * quarter + j * 64, 64), 64)
            gfl[to, :] = full.astype(BF16)
            return total + fold_rows(grad * xhat)

        total = lax.fori_loop(0, quarter // 64, body, jnp.zeros((8, width), F32))
        small[1:2, :] = small[1:2, :] + jnp.sum(total, axis=0, keepdims=True)
        return wire.copy(gfl.at[own(i, quarter)], gfl.at[own(i, quarter)], at.core)

    reduce_up = [
        Reduce(wire, at, gup[i], (width // 2, width), *s["rup"][i]) for i in range(2)
    ]

    def start_up(i):
        for j in range(2):
            grad_up(j, i)
        reduce_up[i].first()

    start_up(0)
    reduce_down[1].second()
    send_gfl = [norm_two_back(0), norm_two_back(1)]
    start_up(1)
    reduce_down[0].third()

    gm = s["gm"]

    def back_mixed(rows):
        one, two = output_weight()
        left = gfl[rows, my_cols]
        right = gfl[rows, other_cols]
        gm[rows, :] = (mm_nt(left, one) + mm_nt(right, two)).astype(BF16)

    back_mixed(own(0, tokens))
    for made in send_gfl:
        made.wait_recv()
    back_mixed(other(0, tokens))
    go = s["go"]
    left = s["mix"][...]
    s["gox"][...] = mm_tn(left, gfl[:, other_cols]).astype(BF16).reshape(
        2, NY, NX, 2 * share, half
    )
    swap_go = wire.copy(s["gox"], go.at[pl.ds(2 * k, 2)], at.core)
    go[pl.ds(2 * k, 2)] = mm_tn(left, gfl[:, my_cols]).astype(BF16).reshape(
        2, NY, NX, 2 * share, half
    )
    reduce_o = Reduce(wire, at, go, (128, half), *s["ro"])

    lse, delta = s["lse"], s["delta"]
    wire.sent(send_gbl, *send_sec)
    heads_in = [(gbl, 0), (gbl, 384), (sec, 0)]
    gpair = s["gqkv"]
    grad_query = s["dq"]
    reduce_qkv = [
        Reduce(wire, at, gpair[p], (CUTS[p % 3], 384), *s["rqkv"][p]) for p in range(pairs)
    ]

    nothing = lambda: None
    todo.extend(
        [
            nothing,
            lambda: (swap_go.wait_recv(), reduce_o.first()),
            reduce_down[1].third,
            lambda: (reduce_up[0].second(), reduce_down[0].third_y()),
            nothing,
            reduce_down[1].third_y,
            reduce_up[1].second,
            reduce_down[0].third_x,
            reduce_up[0].third,
            reduce_o.second,
            reduce_down[1].third_x,
            nothing,
            reduce_up[1].third,
            reduce_qkv[0].second,
            reduce_o.third,
            reduce_qkv[1].second,
            reduce_qkv[0].third,
            reduce_qkv[2].second,
            reduce_qkv[1].third,
            reduce_qkv[2].third,
        ]
    )

    def attend_back(p, b):
        cols = slice(128 * p, 128 * p + 128)
        r0 = b * BLOCK
        rows = slice(r0, r0 + BLOCK)
        after = slice(r0, length)
        count = length - r0
        here_k = lax.broadcasted_iota(jnp.int32, (BLOCK, count), 0)
        here_q = lax.broadcasted_iota(jnp.int32, (BLOCK, count), 1)
        allowed = (here_k <= here_q) & (
            (here_k + r0).astype(F32) >= s["start_row"][0:1, after]
        )
        key, value = ks[rows, cols], vs[rows, cols]
        query, grad = qs[after, cols], gm[after, cols]
        dk = jnp.zeros((BLOCK, 128), F32)
        dv = jnp.zeros((BLOCK, 128), F32)
        dq = jnp.zeros((count, 128), F32)
        for h in range(2):
            key_h = key * ones[h]
            scores = mm_nt(key_h, query)
            weights = jnp.exp(jnp.where(allowed, scores - lse[p, h : h + 1, after], MASKED))
            grad_w = mm_nt(value * ones[h], grad)
            grad_s = (weights * (grad_w - delta[p, h : h + 1, after])).astype(BF16)
            dv = dv + mm(weights.astype(BF16), grad * ones[h])
            dk = dk + mm(grad_s, query * ones[h])
            dq = dq + mm_tn(grad_s, key_h)
        gqkv, base = heads_in[p]
        gqkv[rows, base + 256 : base + 384] = dv.astype(BF16)
        gqkv[rows, base + 128 : base + 256] = turn(
            dk.astype(BF16).astype(F32), rows, -1.0
        ).astype(BF16)
        if b == 0:
            grad_query[...] = dq
        else:
            grad_query[after, :] = grad_query[after, :] + dq

    for p in range(pairs):
        cols = slice(128 * p, 128 * p + 128)

        def inner(i):
            rows = rows_of(i, BLOCK)
            both = jnp.transpose(s["mixf"][rows, cols] * gm[rows, cols].astype(F32))
            delta[p, 0:1, rows] = jnp.sum(both[:HD], axis=0, keepdims=True)
            delta[p, 1:2, rows] = jnp.sum(both[HD:], axis=0, keepdims=True)

        loop(blocks, inner)
        for b in range(blocks):
            attend_back(p, b)
            pump()

        gqkv, base = heads_in[p]

        def turn_query(i):
            rows = rows_of(i, BLOCK)
            low = (grad_query[rows, :] * HD**-0.5).astype(BF16).astype(F32)
            gqkv[rows, base : base + 128] = turn(low, rows, -1.0).astype(BF16)

        loop(blocks, turn_query)

        def grad_qkv(j):
            left = norm[:, pl.ds(pl.multiple_of(j * 384, 128), 384)]
            wide = mm_tn(left, gqkv[:, base : base + 384]).astype(BF16)
            gpair[p][pl.ds(2 * j, 2)] = wide.reshape(2, NY, NX, 2 * share, 384)

        loop(2, grad_qkv)
        reduce_qkv[p].first()
        pump()

    wire.sent(*arrive)

    def back_normed(rows, to, store):
        weight = s["wqkv"][...].reshape(width, qkv_cols)
        store[to, :] = mm_nt(gbl[rows, :], weight[:, :768]) + mm_nt(
            sec[rows, :384], weight[:, 768:]
        )

    arrive = send_parts(back_normed, part_s, part_r)
    own_s = first

    out_s, out_r = s["out_s"], s["out_r"]

    def contract(rows, to, store):
        store[to, :] = mm(hid[rows, :], wdown[...].reshape(ff_half, width))

    arrive_out = send_parts(contract, out_s, out_r)
    pump(2)
    wire.sent(*send_gfl)
    outb = gfl.at[pl.ds(0, tokens)]
    block_sum = jnp.zeros((8, width), F32)
    for i in range(2):
        rows = pl.ds(i * quarter, quarter)
        mine_out = out_s
        wire.sent(arrive_out[i])
        contract(own(i, quarter), rows, mine_out)
        arrive_out[i].wait_recv()

        def finish_out(j, total):
            part = pl.ds(pl.multiple_of(i * quarter + j * 32, 32), 32)
            block = first[part, :] + (mine_out[part, :] + out_r[part, :])
            outb[part, :] = (s["acc"][part, :] + mix_last * block).astype(BF16)
            return total + fold_rows(block * cot_ref[part, :].astype(F32))

        pump()
        block_sum = lax.fori_loop(0, quarter // 32, finish_out, block_sum)
    put_out = pltpu.make_async_copy(outb, out_ref, s["osem"].at[0])
    put_out.start()
    terms = jnp.zeros((1, width), F32)
    wide_lane = lax.broadcasted_iota(jnp.int32, (1, width), 1)
    for j in range(hist):
        terms = jnp.where(wide_lane == j, jnp.sum(s["mixacc"][j]), terms)
    terms = jnp.where(wide_lane == hist, jnp.sum(block_sum), terms)
    small[2:3, :] = terms
    back_normed(own(0, tokens), slice(0, tokens), own_s)
    pump()
    total = jnp.zeros((8, width), F32)

    def norm_one_back(i, total):
        arrive[i].wait_recv()

        def body(j, total):
            rows = pl.ds(pl.multiple_of(i * quarter + j * 64, 64), 64)
            grad = own_s[rows, :] + part_r[rows, :]
            xhat, root = normalize(in_ref[rows, :].astype(F32))
            gsec[rows, :] = gsec[rows, :] + norm_back(xhat, root, s["gain"][0:1, :], grad)
            return total + fold_rows(grad * xhat)

        return lax.fori_loop(0, quarter // 64, body, total)

    for i in range(2):
        total = norm_one_back(i, total)
    put_gin = pltpu.make_async_copy(gsec, gin_ref, s["osem"].at[1])
    put_gin.start()
    small[0:1, :] = jnp.sum(total, axis=0, keepdims=True)

    sr, sp, sz = s["small_r"], s["small_p"], s["small_z"]
    step_c = wire.copy(small, sr, at.core)

    wire.sent(swap)
    fin, fin_r = xs, xr
    def settle(reduce, c, size):
        total = reduce.result()
        fin[0, :, c : c + size] = total[:share]
        fin[1, :, c : c + size] = total[share:]
        return wire.copy(fin.at[o, :, pl.ds(c, size)], fin_r.at[:, pl.ds(c, size)], at.core)

    up0 = qkv_cols + half
    settled = [settle(reduce_up[i], up0 + i * width, width) for i in range(2)]
    settled.append(settle(reduce_o, qkv_cols, half))
    for i in range(2):
        c = i * half + 2 * half // 3
        s["fin_d"][:, i * half : c] = reduce_down[i].result()
        s["fin_d"][:, c : (i + 1) * half] = reduce_down[i].third_result()
    put_down = pltpu.make_async_copy(s["fin_d"], gdown_ref, s["osem"].at[2])
    put_down.start()
    step_c.wait_recv()
    sp[at.y, at.x] = small[...] + sr[...]
    plane = sp.at[at.y, at.x]
    step_p = [wire.copy(plane, plane, device) for device in (at.xn, at.yn, at.diagonal)]
    settled.append(settle(reduce_qkv[0], 0, 384))
    for made in step_p:
        made.wait_recv()
    sz[at.z] = (sp[0, 0] + sp[0, 1]) + (sp[1, 0] + sp[1, 1])
    step_z = [wire.copy(sz.at[at.z], sz.at[at.z], at.zn(step)) for step in range(1, NZ)]
    for p in range(1, pairs):
        settled.append(settle(reduce_qkv[p], 384 * p, 384))
    assert not todo
    put_mine = pltpu.make_async_copy(fin.at[k], pack_ref.at[k], s["osem"].at[3])
    put_mine.start()
    for made in settled:
        made.wait_recv()
    put_other = pltpu.make_async_copy(fin_r, pack_ref.at[o], s["osem"].at[4])
    put_other.start()
    for made in step_z:
        made.wait_recv()
    wire.sent(step_c)
    small[...] = ((sz[0] + sz[1]) + sz[2]) + sz[3]
    put_small = pltpu.make_async_copy(small, small_ref, s["osem"].at[5])
    put_small.start()
    for made in (put_down, put_mine, put_other, put_small):
        made.wait()
    put_out.wait()
    put_gin.wait()
    wire.close()


def finish(unit, *refs):
    mix_ref, cot_ref, small_ref, pack_ref, gdown_ref, out_ref, gin_ref = refs[:7]
    out_o, gin_o, ghist_o, gdown_o = refs[7:11]
    rest_o = refs[11:19]
    cot, small, pack, buffer, out, gin, gdown = refs[19:26]
    rest = refs[26:34]
    sems, hsems = refs[34:]
    hist = ghist_o.shape[0]
    tokens, width = cot.shape
    share = pack.shape[1]
    half = width // 2
    gets = [
        pltpu.make_async_copy(src, dst, sems.at[i])
        for i, (src, dst) in enumerate(
            (
                (cot_ref, cot),
                (pack_ref, pack),
                (small_ref, small),
                (out_ref, out),
                (gin_ref, gin),
                (gdown_ref, gdown),
            )
        )
    ]
    for made in gets:
        made.start()
    gets[0].wait()
    puts = []
    rows = 128
    for j in range(hist):

        def scale(i):
            part = rows_of(i, rows)
            buffer[j, part, :] = (mix_ref[j] * cot[part, :].astype(F32)).astype(BF16)

        loop(tokens // rows, scale)
        puts.append(pltpu.make_async_copy(buffer.at[j], ghist_o.at[j], hsems.at[j]))
        puts[j].start()
    for made in gets[1:]:
        made.wait()
    moves = [
        pltpu.make_async_copy(src, dst, sems.at[i])
        for i, (src, dst) in enumerate(((out, out_o), (gin, gin_o), (gdown, gdown_o)))
    ]
    for made in moves:
        made.start()
    gain1, gain2, mix, gq, gk, gv, go, gup = rest
    device = (lax.axis_index("batch") // unit) * 2 + lax.axis_index("seq")
    own = pltpu.roll(small[...], width - device * share, 1)
    gain1[...] = own[0:1, :share]
    gain2[...] = own[1:2, :share]
    mix[...] = small[2:3, : hist + 1]
    for h in range(2):
        for p in range(half // 128):
            for j, ref in enumerate((gq, gk, gv)):
                c = 384 * p + 128 * j
                ref[:, h * half + 128 * p : h * half + 128 * p + 128] = pack[h, :, c : c + 128]
        go[:, h * half : h * half + half] = pack[h, :, 3 * half : 4 * half]
    blk = gdown_o.shape[0]
    gup[...] = jnp.concatenate(
        [
            pack[h, :, 4 * half + blk * i : 4 * half + blk * i + blk]
            for i in range(GROUPS)
            for h in range(2)
        ],
        axis=1,
    )
    for i, (src, dst) in enumerate(zip(rest, rest_o)):
        puts.append(pltpu.make_async_copy(src, dst, sems.at[6 + i]))
        puts[-1].start()
    for made in puts + moves:
        made.wait()


def local(
    unit,
    inputs,
    history,
    segment_ids,
    cotangent,
    mix_weights,
    attn_gain,
    query_weight,
    key_weight,
    value_weight,
    output_weight,
    mlp_gain,
    up_weight,
    down_weight,
):
    rows, tokens, width = inputs.shape
    hist = history.shape[0]
    length = segment_ids.shape[1]
    half = width // 2
    ff_half = up_weight.shape[1] // 2
    share = width // (2 * GROUPS)
    both = 2 * share
    down_share = 2 * ff_half // (2 * GROUPS)
    pairs = half // 128
    seq = lax.axis_index("seq")
    batch = lax.axis_index("batch")
    group_device = (batch // unit) * 2 + seq
    weights = [query_weight, key_weight, value_weight, output_weight, up_weight, down_weight]
    gains = [attn_gain, mlp_gain]
    if unit > 1:
        def widen(value):
            whole = lax.all_gather(value, ("batch", "seq"), axis=0, tiled=True)
            size = value.shape[0] * unit
            return lax.dynamic_slice_in_dim(whole, group_device * size, size)

        weights = [widen(value) for value in weights]
        gains = [widen(value) for value in gains]
    sizes = []

    def scratch(name, shape, dtype=BF16):
        sizes.append((name, pltpu.VMEM(shape, dtype)))

    dims = (NZ, NY, NX)

    def reduction(rows_in, columns, a, b):
        rest = columns - b
        third = [
            pltpu.VMEM((NZ - 1, NY, NX, rows_in, rest), BF16),
            pltpu.VMEM((NX, rows_in, rest), BF16),
            pltpu.VMEM((rows_in, rest), BF16),
        ]
        return [
            pltpu.VMEM((NZ, NX, rows_in, a), BF16),
            pltpu.VMEM((NZ, NY, rows_in, b - a), BF16),
            pltpu.VMEM((NZ, rows_in, b), BF16),
            pltpu.VMEM((NZ - 1, rows_in, b), BF16),
        ] + (third if rest else [])

    sizes.append(("send", pltpu.SemaphoreType.DMA((SENDS,))))
    sizes.append(("recv", pltpu.SemaphoreType.DMA((COPIES,))))
    sizes.append(("hsem", pltpu.SemaphoreType.DMA((HBUF,))))
    sizes.append(("osem", pltpu.SemaphoreType.DMA((6,))))
    scratch("fin_d", (down_share, width), F32)
    scratch("hbuf", (HBUF, hist, 32, width))
    scratch("xs", (2, share, 2 * half + 2 * half + ff_half), F32)
    scratch("xr", (share, 2 * half + 2 * half + ff_half), F32)
    scratch("ga", (2,) + dims + (8, 128), F32)
    scratch("gain", (8, width), F32)
    scratch("wqkv", dims + (both, 3 * half))
    scratch("wo", dims + (both, half))
    scratch("wox", (2, NY, NX, both, half))
    scratch("wup", dims + (both, ff_half))
    scratch("wdown", dims + (down_share, width))
    for name in ("gbl", "norm", "sec", "gfl"):
        scratch(name, (length, width))
    scratch("start_row", (8, length), F32)
    scratch("start_col", (length, 128), F32)
    scratch("cos", (length, 128), F32)
    scratch("sin", (length, 128), F32)
    scratch("acc", (tokens, width), F32)
    scratch("mixacc", (hist, 8, 128), F32)
    for name in ("q", "kk", "v", "mix", "gm"):
        scratch(name, (length, half))
    scratch("mixf", (length, half), F32)
    scratch("lse", (pairs, 8, length), F32)
    scratch("delta", (pairs, 8, length), F32)
    scratch("dq", (length, 128), F32)
    for name in ("part_s", "part_r", "out_s", "out_r", "first", "gfirst"):
        scratch(name, (tokens, width), F32)
    scratch("hid", (length, ff_half))
    scratch("dgelu", (length, ff_half))
    scratch("gox", (2, NY, NX, both, half))
    for name in ("small", "small_r"):
        scratch(name, (8, width), F32)
    scratch("small_p", (NY, NX, 8, width), F32)
    scratch("small_z", (NZ, 8, width), F32)
    sizes.append(("gdown", [pltpu.VMEM(dims + (down_share, half), BF16) for _ in range(2)]))
    sizes.append(("gup", [pltpu.VMEM(dims + (both, width), BF16) for _ in range(2)]))
    scratch("go", dims + (both, half))
    sizes.append(("gqkv", [pltpu.VMEM(dims + (both, 384), BF16) for _ in range(pairs)]))
    sizes.append(("rdown", [reduction(down_share, half, half // 3, 2 * half // 3) for _ in range(2)]))
    sizes.append(("rup", [reduction(both, width, width // 2, width) for _ in range(2)]))
    sizes.append(("ro", reduction(both, half, 128, half)))
    sizes.append(("rqkv", [reduction(both, 384, CUTS[p % 3], 384) for p in range(pairs)]))
    names = [name for name, _ in sizes]

    vmem = pl.BlockSpec(memory_space=pltpu.VMEM)
    anywhere = pl.BlockSpec(memory_space=pl.ANY)
    smem = pl.BlockSpec(memory_space=pltpu.SMEM)
    shape = jax.ShapeDtypeStruct
    outs = pl.pallas_call(
        functools.partial(layer, unit, names),
        out_shape=(
            shape((tokens, width), BF16),
            shape((tokens, width), F32),
            shape((2, share, 4 * half + ff_half), F32),
            shape((down_share, width), F32),
            shape((8, width), F32),
        ),
        in_specs=[vmem, smem] + [vmem] * 10 + [anywhere],
        out_specs=[anywhere] * 5,
        scratch_shapes=[size for _, size in sizes],
        compiler_params=pltpu.CompilerParams(
            collective_id=0, has_side_effects=True, vmem_limit_bytes=64 * 1024 * 1024 - 64 * 1024
        ),
    )(
        segment_ids,
        mix_weights,
        gains[0].reshape(1, share),
        gains[1].reshape(1, share),
        inputs.reshape(tokens, width),
        cotangent.reshape(tokens, width),
        *weights,
        history.reshape(hist, tokens, width),
    )
    partial_out, partial_gin, pack, gdown, small = outs
    rest = [
        shape((1, share), F32),
        shape((1, share), F32),
        shape((1, hist + 1), F32),
        shape((share, width), F32),
        shape((share, width), F32),
        shape((share, width), F32),
        shape((share, width), F32),
        shape((share, 2 * ff_half), F32),
    ]
    ends = pl.pallas_call(
        functools.partial(finish, unit),
        out_shape=[
            shape((tokens, width), BF16),
            shape((tokens, width), F32),
            shape((hist, tokens, width), BF16),
            shape((down_share, width), F32),
        ]
        + rest,
        in_specs=[smem] + [anywhere] * 6,
        out_specs=[anywhere] * 12,
        scratch_shapes=[
            pltpu.VMEM((tokens, width), BF16),
            pltpu.VMEM((8, width), F32),
            pltpu.VMEM((2, share, 4 * half + ff_half), F32),
            pltpu.VMEM((hist, tokens, width), BF16),
            pltpu.VMEM((tokens, width), BF16),
            pltpu.VMEM((tokens, width), F32),
            pltpu.VMEM((down_share, width), F32),
        ]
        + [pltpu.VMEM(one.shape, F32) for one in rest]
        + [pltpu.SemaphoreType.DMA((14,)), pltpu.SemaphoreType.DMA((hist,))],
        compiler_params=pltpu.CompilerParams(vmem_limit_bytes=64 * 1024 * 1024 - 64 * 1024),
    )(
        mix_weights,
        cotangent.reshape(tokens, width),
        small,
        pack,
        gdown,
        partial_out,
        partial_gin,
    )
    output, grad_inputs, grad_history, gdown, gain_one, gain_two, mix_grad = ends[:7]
    grads = list(ends[7:]) + [gdown, gain_one.reshape(share), gain_two.reshape(share)]
    mix_grad = mix_grad.reshape(hist + 1)
    if unit > 1:
        def narrow(value):
            whole = jnp.zeros((value.shape[0] * 2 * GROUPS,) + value.shape[1:], F32)
            whole = lax.dynamic_update_slice_in_dim(whole, value, group_device * value.shape[0], 0)
            return lax.psum_scatter(whole, ("batch", "seq"), scatter_dimension=0, tiled=True)

        grads = [narrow(value) for value in grads]
        mix_grad = lax.psum(mix_grad, ("batch", "seq")) / (2 * GROUPS)
    gq, gk, gv, go, gup, gdown, gain_one, gain_two = grads
    return (
        output.reshape(rows, tokens, width),
        grad_inputs.reshape(rows, tokens, width),
        grad_history.reshape(hist, rows, tokens, width),
        mix_grad,
        gain_one,
        gq,
        gk,
        gv,
        go,
        gain_two,
        gup,
        gdown,
    )


def solution(mesh):
    batch = mesh.shape["batch"]
    split = P(("batch", "seq"), None)
    gain = P(("batch", "seq"))
    placed = (
        P("batch", "seq", None),
        P(None, "batch", "seq", None),
        P("batch", None),
        P("batch", "seq", None),
        P(),
        gain,
        split,
        split,
        split,
        split,
        gain,
        split,
        split,
    )
    return jax.shard_map(
        functools.partial(local, batch // GROUPS),
        mesh=mesh,
        in_specs=placed,
        out_specs=(
            P("batch", "seq", None),
            P("batch", "seq", None),
            P(None, "batch", "seq", None),
            P(),
            gain,
            split,
            split,
            split,
            split,
            gain,
            split,
            split,
        ),
        check_vma=False,
    )
```

```python
import functools

import jax
import jax.numpy as jnp
import numpy as np
from jax import lax
from jax.experimental import pallas as pl
from jax.experimental.pallas import tpu as pltpu
from jax.sharding import PartitionSpec as P

HD = 64
EPSILON = 1e-05
MASKED = -1000000000.0
MESH = pl.DeviceIdType.MESH
F32 = jnp.float32
BF16 = jnp.bfloat16
NZ, NY, NX = 4, 2, 2
GROUPS = NZ * NY * NX
COPIES = 187
SENDS = 32
CUTS = (256, 128, 256)
HBUF = 3
BLOCK = 256


def mm(a, b):
    return lax.dot_general(a, b, (((1,), (0,)), ((), ())), preferred_element_type=F32)


def mm_nt(a, b):
    return lax.dot_general(a, b, (((1,), (1,)), ((), ())), preferred_element_type=F32)


def mm_tn(a, b):
    return lax.dot_general(a, b, (((0,), (0,)), ((), ())), preferred_element_type=F32)


def loop(count, body):
    def step(i, carry):
        body(i)
        return carry

    lax.fori_loop(0, count, step, 0)


def rows_of(i, size):
    return pl.ds(pl.multiple_of(i * size, size), size)


def lane_cut(start, size):
    return pl.ds(pl.multiple_of(start, 128), size)


def normalize(value):
    mean = jnp.mean(value, axis=-1, keepdims=True)
    centred = value - mean
    variance = jnp.mean(centred * centred, axis=-1, keepdims=True)
    root = lax.rsqrt(variance + EPSILON)
    return centred * root, jnp.where(lax.broadcasted_iota(jnp.int32, (1, 128), 1) == 0, mean, root)


def normalize_again(value, kept):
    root = kept[:, 1:2]
    return (value - kept[:, 0:1]) * root, root


def norm_back(xhat, root, gain, grad):
    g = grad * gain
    return root * (
        g - jnp.mean(g, axis=-1, keepdims=True) - xhat * jnp.mean(g * xhat, axis=-1, keepdims=True)
    )


def fold_rows(value):
    total = value[0:8]
    for r in range(8, value.shape[0], 8):
        total = total + value[r : r + 8]
    return total


class Place:
    def __init__(self, unit):
        batch = lax.axis_index("batch")
        self.k = lax.axis_index("seq")
        self.o = 1 - self.k
        group = batch // unit
        self.unit = unit
        self.u = batch % unit
        self.z = group // (NY * NX)
        self.y = (group // NX) % NY
        self.x = group % NX
        self.core = (batch, self.o)
        self.xn = self.device(self.z, self.y, 1 - self.x)
        self.yn = self.device(self.z, 1 - self.y, self.x)
        self.diagonal = self.device(self.z, 1 - self.y, 1 - self.x)
        self.block = [self.xn, self.yn, self.diagonal, self.core] + [
            (batch_of, self.o) for batch_of, _ in (self.xn, self.yn, self.diagonal)
        ]

    def device(self, z, y, x):
        return (((z * NY + y) * NX + x) * self.unit + self.u, self.k)

    def across(self, step):
        if step == 0:
            return self.z
        if step == 2:
            return (self.z + 2) % NZ
        flip = self.z + 1 - 2 * (self.z % 2)
        return flip if step == 1 else (flip + 2) % NZ

    def zn(self, step):
        return self.device(self.across(step), self.y, self.x)


class Wire:
    def __init__(self, send, recv):
        self.send = send
        self.recv = recv
        self.open = []
        self.count = 0

    def copy(self, src, dst, device):
        i = self.count
        self.count += 1
        while self.open and self.open[0][0] <= i - SENDS:
            self.open.pop(0)[1].wait_send()
        made = pltpu.make_async_remote_copy(
            src_ref=src,
            dst_ref=dst,
            send_sem=self.send.at[i % SENDS],
            recv_sem=self.recv.at[i],
            device_id=device,
            device_id_type=MESH,
        )
        made.start()
        self.open.append((i, made))
        return made

    def sent(self, *copies):
        for made in copies:
            if any(one is made for _, one in self.open):
                made.wait_send()
                self.open = [(i, one) for i, one in self.open if one is not made]

    def close(self):
        for _, made in self.open:
            made.wait_send()


class Gather:
    def __init__(self, wire, at, ref, a, b=None):
        self.wire, self.at, self.ref, self.a = wire, at, ref, a
        self.b = ref.shape[-1] if b is None else b
        self.third = self.b < ref.shape[-1]
        self.z, self.mid, self.last = {}, {}, {}
        self.cz = []

    def send_z(self, *steps):
        at = self.at
        own = self.ref.at[at.z, at.y, at.x]
        if self.third:
            own = self.ref.at[at.z, at.y, at.x, :, : self.b]
        for step in steps:
            self.z[step] = self.wire.copy(own, own, at.zn(step))

    def pass_mid(self, step):
        at, ref = self.at, self.ref
        if step:
            self.z[step].wait_recv()
        zz = at.across(step)
        left = ref.at[zz, at.y, at.x, :, : self.a]
        right = ref.at[zz, at.y, at.x, :, self.a : self.b]
        self.mid[step] = (
            self.wire.copy(left, left, at.xn),
            self.wire.copy(right, right, at.yn),
        )

    def pass_last(self, step):
        at, ref = self.at, self.ref
        zz = at.across(step)
        self.mid[step][0].wait_recv()
        left = ref.at[zz, at.y, :, :, : self.a]
        one = self.wire.copy(left, left, at.yn)
        self.mid[step][1].wait_recv()
        right = ref.at[zz, :, at.x, :, self.a : self.b]
        self.last[step] = (one, self.wire.copy(right, right, at.xn))

    def third_x(self):
        at = self.at
        part = self.ref.at[at.z, at.y, at.x, :, self.b :]
        self.cx = self.wire.copy(part, part, at.xn)

    def third_y(self):
        at = self.at
        self.cx.wait_recv()
        part = self.ref.at[at.z, at.y, :, :, self.b :]
        self.cy = self.wire.copy(part, part, at.yn)

    def third_z(self):
        at = self.at
        self.cy.wait_recv()
        part = self.ref.at[at.z, :, :, :, self.b :]
        self.cz = [self.wire.copy(part, part, at.zn(step)) for step in range(1, NZ)]

    def arrived(self, step):
        for made in self.last[step]:
            made.wait_recv()
        if self.third and step:
            self.cz[step - 1].wait_recv()

    def finish(self):
        for step in range(NZ):
            self.arrived(step)


class Reduce:
    def __init__(self, wire, at, grad, cuts, one_a, one_b, two, three, *third):
        self.wire, self.at, self.grad = wire, at, grad
        self.a, self.b = cuts
        self.one_a, self.one_b, self.two, self.three = one_a, one_b, two, three
        self.third_refs = third

    def add(self, index, more):
        self.grad[index] = (self.grad[index].astype(F32) + more.astype(F32)).astype(BF16)

    def first(self):
        at, grad, a, b = self.at, self.grad, self.a, self.b
        self.sa = self.wire.copy(grad.at[:, 1 - at.y, :, :, :a], self.one_a, at.yn)
        self.sb = self.wire.copy(grad.at[:, :, 1 - at.x, :, a:b], self.one_b, at.xn)
        if self.third_refs:
            self.cz = [
                self.wire.copy(
                    grad.at[at.across(step), :, :, :, b:], self.third_refs[0].at[step - 1], at.zn(step)
                )
                for step in range(1, NZ)
            ]

    def second(self):
        at, grad, a, b = self.at, self.grad, self.a, self.b
        left, right = slice(0, a), slice(a, b)

        def add_a(xx):
            loop(NZ, lambda zz: self.add((zz, at.y, xx, slice(None), left), self.one_a[zz, xx]))

        def add_b(yy):
            loop(NZ, lambda zz: self.add((zz, yy, at.x, slice(None), right), self.one_b[zz, yy]))

        self.sa.wait_recv()
        add_a(1 - at.x)
        self.saa = self.wire.copy(grad.at[:, at.y, 1 - at.x, :, :a], self.two.at[:, :, :a], at.xn)
        self.sb.wait_recv()
        add_b(1 - at.y)
        self.sbb = self.wire.copy(grad.at[:, 1 - at.y, at.x, :, a:b], self.two.at[:, :, a:], at.yn)
        add_a(at.x)
        add_b(at.y)

    def third(self):
        at, grad, b = self.at, self.grad, self.b
        self.saa.wait_recv()
        self.sbb.wait_recv()
        loop(NZ, lambda zz: self.add((zz, at.y, at.x, slice(None), slice(0, b)), self.two[zz]))
        self.sz = []
        for step in range(1, NZ):
            part = grad.at[at.across(step), at.y, at.x, :, :b]
            self.sz.append(self.wire.copy(part, self.three.at[step - 1], at.zn(step)))

    def third_y(self):
        at, grad, b = self.at, self.grad, self.b
        for made in self.cz:
            made.wait_recv()
        ref = self.third_refs[0]

        def body(yx):
            y, x = yx // NX, yx % NX
            more = ref[0, y, x].astype(F32) + ref[1, y, x].astype(F32) + ref[2, y, x].astype(F32)
            self.add((at.z, y, x, slice(None), slice(b, None)), more)

        loop(NY * NX, body)
        self.cy = self.wire.copy(grad.at[at.z, 1 - at.y, :, :, b:], self.third_refs[1], at.yn)

    def third_x(self):
        at, grad, b = self.at, self.grad, self.b
        self.cy.wait_recv()
        ref = self.third_refs[1]
        loop(NX, lambda x: self.add((at.z, at.y, x, slice(None), slice(b, None)), ref[x]))
        self.cx = self.wire.copy(grad.at[at.z, at.y, 1 - at.x, :, b:], self.third_refs[2], at.xn)

    def result(self):
        at, b = self.at, self.b
        total = self.grad[at.z, at.y, at.x, :, :b].astype(F32)
        for step in range(1, NZ):
            self.sz[step - 1].wait_recv()
            total = total + self.three[step - 1].astype(F32)
        return total

    def third_result(self):
        at = self.at
        self.cx.wait_recv()
        return self.grad[at.z, at.y, at.x, :, self.b :].astype(F32) + self.third_refs[2][
            ...
        ].astype(F32)


def layer(unit, names, *refs):
    (
        mix_ref, gain1_ref, gain2_ref, seg_any, in_any, cot_any,
        q_any, k_any, v_any, o_any, up_any, down_any, hist_ref,
        out_ref, gin_ref, pack_ref, gdown_ref, small_ref,
    ) = refs[:18]
    s = dict(zip(names, refs[18:]))
    seg_ref, in_ref, cot_ref = s["seg"], s["in"], s["cot"]
    q_ref, k_ref, v_ref, o_ref, up_ref, down_ref = (s[n] for n in ("w0", "w1", "w2", "w3", "w4", "w5"))
    tokens, width = in_ref.shape
    length = 2 * tokens
    half = width // 2
    ff_half = up_ref.shape[1] // 2
    pairs = half // 128
    share = q_ref.shape[0]
    down_rows = down_ref.shape[0]
    blocks = length // BLOCK
    hist = hist_ref.shape[0]
    at = Place(unit)
    k, o = at.k, at.o
    wire = Wire(s["send"], s["recv"])

    barrier = pltpu.get_barrier_semaphore()
    for device in (*at.block, at.zn(1), at.zn(2), at.zn(3)):
        pl.semaphore_signal(barrier, inc=1, device_id=device, device_id_type=MESH)
    gets = []
    for src, dst in (
        (q_any, q_ref), (k_any, k_ref), (v_any, v_ref), (o_any, o_ref), (up_any, up_ref),
        (down_any, down_ref), (seg_any, seg_ref), (in_any, in_ref), (cot_any, cot_ref),
    ):
        gets.append(pltpu.make_async_copy(src, dst, s["isem"].at[len(gets)]))
        gets[-1].start()
    hist_rows = s["hbuf"].shape[2]
    hist_chunks = tokens // hist_rows

    def fetch(i):
        return pltpu.make_async_copy(
            hist_ref.at[:, pl.ds(i * hist_rows, hist_rows)],
            s["hbuf"].at[i % HBUF],
            s["hsem"].at[i % HBUF],
        )

    for i in range(HBUF - 1):
        fetch(i).start()

    for made in gets[:3]:
        made.wait()

    xs, xr = s["xs"], s["xr"]
    qkv_cols = 3 * half
    blk = down_rows
    for h in range(2):
        c = h * half
        for i in range(pairs):
            for j, ref in enumerate((q_ref, k_ref, v_ref)):
                xs[h, :, 384 * i + 128 * j : 384 * i + 128 * j + 128] = ref[
                    :, c + 128 * i : c + 128 * i + 128
                ].astype(F32)
    ga = s["ga"]
    ga[k, at.z, at.y, at.x] = jnp.zeros((8, 128), F32)
    ga[k, at.z, at.y, at.x, 0:1, :share] = gain1_ref[...].astype(F32)
    ga[k, at.z, at.y, at.x, 1:2, :share] = gain2_ref[...].astype(F32)

    pl.semaphore_wait(barrier, 10)

    swap = [wire.copy(xs.at[o, :, :qkv_cols], xr.at[:, :qkv_cols], at.core)]
    gain_z = [
        wire.copy(ga.at[k, at.z, at.y, at.x], ga.at[k, at.z, at.y, at.x], at.zn(step))
        for step in range(1, NZ)
    ]
    for made in gets[3:6]:
        made.wait()
    s["wdown"][at.z, at.y, at.x] = down_ref[...]
    gather_down = Gather(wire, at, s["wdown"], width // 3, 2 * width // 3)
    gather_down.third_x()
    gather_down.pass_mid(0)
    wide = up_ref[...].astype(F32)
    for h in range(2):
        c = h * half
        xs[h, :, qkv_cols : qkv_cols + half] = o_ref[:, c : c + half].astype(F32)
        xs[h, :, qkv_cols + half :] = jnp.concatenate(
            [
                wide[:, 2 * blk * i + blk * h : 2 * blk * i + blk * h + blk]
                for i in range(GROUPS)
            ],
            axis=1,
        )
    swap.append(wire.copy(xs.at[o, :, qkv_cols:], xr.at[:, qkv_cols:], at.core))

    own0 = pl.multiple_of(k * tokens, tokens)
    other0 = pl.multiple_of(o * tokens, tokens)

    def own(i, size):
        return pl.ds(pl.multiple_of(own0 + i * size, size), size)

    def other(i, size):
        return pl.ds(pl.multiple_of(other0 + i * size, size), size)

    mix_last = mix_ref[hist]
    gbl, norm, sec, gfl = s["gbl"], s["norm"], s["sec"], s["gfl"]

    def own_block(cols):
        mine = xs[k, :, cols]
        theirs = xr[:, cols]
        upper = jnp.where(k == 0, mine, theirs)
        lower = jnp.where(k == 0, theirs, mine)
        return jnp.concatenate([upper, lower], axis=0).astype(BF16)

    gather_qkv = Gather(wire, at, s["wqkv"], 640)
    gather_o = Gather(wire, at, s["wo"], 128)
    gather_up = Gather(wire, at, s["wup"], ff_half // 2)
    swap[0].wait_recv()
    s["wqkv"][at.z, at.y, at.x] = own_block(slice(0, qkv_cols))
    gather_qkv.send_z(1, 2, 3)
    gather_qkv.pass_mid(0)
    swap[1].wait_recv()
    s["wo"][at.z, at.y, at.x] = own_block(slice(qkv_cols, qkv_cols + half))
    s["wup"][at.z, at.y, at.x] = own_block(slice(qkv_cols + half, qkv_cols + half + ff_half))
    gather_up.pass_mid(0)
    todo = [
        lambda: (gather_qkv.pass_last(0), gather_o.send_z(1, 2, 3)),
        lambda: (
            gather_qkv.pass_mid(1),
            gather_o.pass_mid(0),
            gather_up.pass_last(0),
            gather_up.send_z(1),
        ),
        lambda: (gather_qkv.pass_last(1), gather_down.third_y(), gather_up.send_z(2, 3)),
        lambda: (gather_qkv.pass_mid(2), gather_o.pass_last(0)),
        lambda: (gather_qkv.pass_mid(3), gather_qkv.pass_last(2)),
        lambda: (gather_qkv.pass_last(3), gather_down.send_z(1, 2, 3)),
        lambda: (
            gather_o.pass_mid(1),
            gather_o.pass_mid(2),
            gather_o.pass_mid(3),
            gather_up.pass_mid(1),
        ),
    ]
    later = [
        lambda: (gather_up.pass_mid(2), gather_up.pass_mid(3)),
        lambda: (gather_o.pass_last(1), gather_o.pass_last(2)),
        lambda: (gather_o.pass_last(3), gather_up.pass_last(1)),
        lambda: gather_down.third_z(),
        lambda: gather_up.pass_last(2),
        lambda: gather_up.pass_last(3),
        lambda: (gather_down.pass_mid(1), gather_down.pass_mid(2)),
        lambda: (gather_down.pass_last(0), gather_down.pass_mid(3)),
        lambda: gather_down.pass_last(1),
        lambda: gather_down.pass_last(2),
        lambda: gather_down.pass_last(3),
    ]

    def pump(count=1):
        for _ in range(count):
            if todo:
                todo.pop(0)()

    for made in gets[6:]:
        made.wait()
    seg = seg_ref[...].astype(F32)
    seg_col = jnp.transpose(jnp.broadcast_to(seg, (128, length)))
    start_row = jnp.zeros((1, length), F32)
    start_col = jnp.zeros((length, 128), F32)
    for d in range(7):
        count = jnp.sum(jnp.where(seg == d, 1.0, 0.0), axis=1, keepdims=True)
        start_row = start_row + jnp.where(seg > d, count, 0.0)
        start_col = start_col + jnp.where(seg_col > d, count, 0.0)
    s["start_row"][...] = jnp.broadcast_to(start_row, (8, length))
    s["start_col"][...] = start_col
    lane = lax.broadcasted_iota(jnp.int32, (1, 128), 1)
    first_half = (lane % HD) < (HD // 2)

    def rope_tables(i):
        rows = rows_of(i, 64)
        order = (lax.broadcasted_iota(jnp.int32, (64, 128), 0) + i * 64).astype(F32)
        angles = (order - s["start_col"][rows, :]) * freq
        s["cos"][rows, :] = jnp.cos(angles)
        sine = jnp.sin(angles)
        s["sin"][rows, :] = jnp.where(first_half, -sine, sine)

    freq = jnp.zeros((1, 128), F32)
    for i in range(HD // 2):
        rate = float(np.float32(10000.0 ** (-2.0 * i / HD)))
        freq = jnp.where(lane % (HD // 2) == i, rate, freq)
    loop(length // 64, rope_tables)
    pump()
    for step in range(1, NZ):
        gain_z[step - 1].wait_recv()
    gain_x = wire.copy(ga.at[k, :, at.y, at.x], ga.at[k, :, at.y, at.x], at.xn)

    def low_block(i):
        gbl[own(i, 32), :] = (mix_last * cot_ref[rows_of(i, 32), :].astype(F32)).astype(BF16)

    loop(tokens // 32, low_block)
    send_gbl = wire.copy(
        gbl.at[pl.ds(own0, tokens)], gbl.at[pl.ds(own0, tokens)], at.core
    )
    pump()

    def history_chunk(i):
        if i + HBUF - 1 < hist_chunks:
            fetch(i + HBUF - 1).start()
        fetch(i).wait()

        def group(r, sums):
            rows = rows_of(r, 16)
            whole = pl.ds(pl.multiple_of(i * hist_rows + r * 16, 16), 16)
            cot = cot_ref[whole, :].astype(F32)
            total = jnp.zeros((16, width), F32)
            out = []
            for j in range(hist):
                earlier = s["hbuf"][i % HBUF, j, rows, :].astype(F32)
                total = total + mix_ref[j] * earlier
                term = fold_rows(earlier * cot)
                part = sums[j]
                for c in range(0, width, 128):
                    part = part + term[:, c : c + 128]
                out.append(part)
            s["acc"][whole, :] = total
            return tuple(out)

        sums = lax.fori_loop(
            0, hist_rows // 16, group, tuple(s["mixacc"][j] for j in range(hist))
        )
        for j in range(hist):
            s["mixacc"][j] = sums[j]

    s["mixacc"][...] = jnp.zeros_like(s["mixacc"])
    history_chunk(0)
    history_chunk(1)
    pump()
    history_chunk(2)
    history_chunk(3)
    pump()
    gain_x.wait_recv()
    gain_y = wire.copy(ga.at[k, :, at.y], ga.at[k, :, at.y], at.yn)
    history_chunk(4)
    history_chunk(5)
    pump()
    gain_y.wait_recv()
    gain_c = wire.copy(ga.at[k], ga.at[k], at.core)
    history_chunk(6)
    history_chunk(7)
    pump()
    gain_c.wait_recv()

    lanes = lax.broadcasted_iota(jnp.int32, (128, width), 1).astype(F32)
    rows_i = lax.broadcasted_iota(jnp.int32, (128, width), 0)
    owner = jnp.floor((lanes + 0.5) * (1.0 / share))
    spread = jnp.where(lanes - share * owner == rows_i.astype(F32), 1.0, 0.0).astype(BF16)
    gain_rows = [jnp.zeros((1, width), F32), jnp.zeros((1, width), F32)]
    for kk in range(2):
        tiles = ga[kk].reshape(GROUPS * 8, 128).astype(BF16)
        wide = mm(tiles, spread)
        for r in range(2):
            hit = ((rows_i % 8) == r) & (owner == (2 * (rows_i // 8) + kk).astype(F32))
            gain_rows[r] = gain_rows[r] + jnp.sum(
                jnp.where(hit, wide, 0.0), axis=0, keepdims=True
            )
    s["gain"][...] = jnp.concatenate([gain_rows[0], gain_rows[1], jnp.zeros((6, width), F32)], axis=0)

    def norm_one(i):
        xhat, s["kept_one"][rows_of(i, 128), :] = normalize(in_ref[rows_of(i, 128), :].astype(F32))
        norm[own(i, 128), :] = (xhat * s["gain"][0:1, :]).astype(BF16)

    loop(tokens // 128, norm_one)
    send_norm = wire.copy(norm.at[pl.ds(own0, tokens)], norm.at[pl.ds(own0, tokens)], at.core)
    pump()
    for i in range(8, hist_chunks):
        history_chunk(i)
    while len(todo) > 0:
        pump()
    todo.extend(later)
    send_norm.wait_recv()
    send_gbl.wait_recv()
    gather_qkv.finish()

    qs, ks, vs = s["q"], s["kk"], s["v"]

    def turn(value, rows, sign):
        partner = jnp.where(first_half, pltpu.roll(value, 96, 1), pltpu.roll(value, 32, 1))
        return value * s["cos"][rows, :] + (sign * partner) * s["sin"][rows, :]

    def project(i):
        rows = rows_of(i, BLOCK)
        left = norm[rows, :]
        both_pairs = mm(left, s["wqkv"][:, :, :, :, :768].reshape(width, 768))
        for p in range(pairs):
            if p < 2:
                wide = both_pairs[:, 384 * p : 384 * p + 384]
            else:
                wide = mm(left, s["wqkv"][:, :, :, :, 768:].reshape(width, qkv_cols - 768))
            cols = slice(128 * p, 128 * p + 128)
            qs[rows, cols] = (turn(wide[:, :128], rows, 1.0).astype(BF16) * HD**-0.5).astype(BF16)
            ks[rows, cols] = turn(wide[:, 128:256], rows, 1.0).astype(BF16)
            vs[rows, cols] = wide[:, 256:].astype(BF16)

    for i in range(blocks):
        project(i)
        pump()

    lane_low = lane < HD
    ones = [
        jnp.where(lane_low, 1.0, 0.0).astype(BF16),
        jnp.where(lane_low, 0.0, 1.0).astype(BF16),
    ]

    def attend(p, b):
        cols = slice(128 * p, 128 * p + 128)
        r0 = b * tokens
        rows = slice(r0, r0 + tokens)
        here_q = lax.broadcasted_iota(jnp.int32, (tokens, tokens), 0)
        here_k = lax.broadcasted_iota(jnp.int32, (tokens, tokens), 1)
        start = s["start_col"][rows, 0:1]
        outs, tops = [], []
        for h in range(2):
            query = qs[rows, cols] * ones[h]
            near = mm_nt(query, ks[rows, cols])
            near = jnp.where(
                (here_k <= here_q) & ((here_k + r0).astype(F32) >= start), near, MASKED
            )
            top = jnp.max(near, axis=1, keepdims=True)
            if b:
                far = mm_nt(query, ks[0:r0, cols])
                far_k = lax.broadcasted_iota(jnp.int32, (1, r0), 1).astype(F32)
                far = jnp.where(far_k >= start, far, MASKED)
                top = jnp.maximum(top, jnp.max(far, axis=1, keepdims=True))
            raw = jnp.exp(near - top).astype(BF16)
            out = mm(raw, vs[rows, cols] * ones[h] + ones[1 - h])
            if b:
                raw = jnp.exp(far - top).astype(BF16)
                out = out + mm(raw, vs[0:r0, cols] * ones[h] + ones[1 - h])
            outs.append(out)
            tops.append(top)
        total = jnp.where(lane_low, pltpu.roll(outs[0], HD, 1), pltpu.roll(outs[1], HD, 1))
        mixed = jnp.where(lane_low, outs[0], outs[1]) / total
        s["mix"][rows, cols] = mixed.astype(BF16)
        s["mixf"][rows, cols] = mixed
        log_total = jnp.transpose(jnp.where(lane_low, tops[0], tops[1]) + jnp.log(total))
        s["lse"][p, 0:1, rows] = log_total[0:1]
        s["lse"][p, 1:2, rows] = log_total[HD : HD + 1]

    wo, wof = s["wo"], s["wof"]
    my_cols = lane_cut(k * half, half)
    for p in range(pairs):
        for b in range(2):
            attend(p, b)
        pump()
        if p == 1:
            gather_o.finish()
            swap_o = wire.copy(wo.at[pl.ds(2 * o, 2)], wof.at[:, :, :, :, my_cols], at.core)
            wof[:, :, :, :, my_cols] = wo[pl.ds(2 * k, 2)]

    swap_o.wait_recv()

    def output_weight():
        return wof[...].reshape(half, width)

    part_s, part_r = s["part_s"], s["part_r"]
    quarter = tokens // 2

    def send_parts(make, store, recv, pieces=1):
        made = []
        size = tokens // pieces
        for i in range(pieces):
            make(other(i, size), rows_of(i, size), store)
            for j in range(2 // pieces):
                to = pl.ds((i * (2 // pieces) + j) * quarter, quarter)
                made.append(wire.copy(store.at[to], recv.at[to], at.core))
        return made

    def attended(rows, to, store):
        store[to, :] = mm(s["mix"][rows, :], output_weight())

    arrive = send_parts(attended, part_s, part_r, 2)
    first = s["first"]
    for i in range(2):
        attended(own(i, quarter), rows_of(i, quarter), first)
    send_sec = []
    for i in range(2):
        arrive[i].wait_recv()

        def norm_two(j):
            rows = pl.ds(pl.multiple_of(i * quarter + j * 128, 128), 128)
            value = in_ref[rows, :].astype(F32) + (first[rows, :] + part_r[rows, :])
            first[rows, :] = value
            xhat, s["kept_two"][rows, :] = normalize(value)
            to = pl.ds(pl.multiple_of(own0 + i * quarter + j * 128, 128), 128)
            sec[to, :] = (xhat * s["gain"][1:2, :]).astype(BF16)

        loop(quarter // 128, norm_two)
        send_sec.append(wire.copy(sec.at[own(i, quarter)], sec.at[own(i, quarter)], at.core))
    pump()
    gather_up.finish()
    hid, dgelu = s["hid"], s["dgelu"]
    wup, wdown = s["wup"], s["wdown"]
    root_2_pi = float(np.sqrt(2.0 / np.pi).astype(np.float32))

    def expand(start):
        rows = pl.ds(start, tokens)

        def part(cols):
            v = mm(sec[rows, :], wup[:, :, :, :, cols].reshape(width, 256))
            vv = v * v
            t = jnp.tanh(v * (root_2_pi + (0.044715 * root_2_pi) * vv))
            a = 0.5 * t + 0.5
            out = v * a
            hid[rows, cols] = out.astype(BF16)
            slope = 2.0 * root_2_pi + (6.0 * 0.044715 * root_2_pi) * vv
            dgelu[rows, cols] = (a + out * (1.0 - a) * slope).astype(BF16)

        def body(j):
            for c in range(2):
                part(lane_cut(j * 512 + c * 256, 256))

        loop(ff_half // 512, body)
        pump()

    expand(own0)
    for made in send_sec:
        made.wait_recv()
    expand(other0)

    gdown = s["gdown"]

    def grad_down(zz):
        left = hid[:, 384 * zz : 384 * zz + 384]
        wide = mm_tn(left, gbl[...]).astype(BF16)
        for i in range(2):
            gdown[i][zz] = wide[:, i * half : (i + 1) * half].reshape(NY, NX, down_rows, half)

    for zz in range(NZ):
        grad_down(zz)
        if zz % 2:
            pump()
    reduce_down = [
        Reduce(wire, at, gdown[i], (half // 3, 2 * half // 3), *s["rdown"][i]) for i in range(2)
    ]
    for r in reduce_down:
        r.first()

    def back_hidden(step):
        gather_down.arrived(step)
        zz = at.across(step)
        weight = wdown[zz].reshape(NY * NX * down_rows, width)
        cols = lane_cut(zz * 384, 384)
        for start in (0, tokens):
            rows = slice(start, start + tokens)
            grad = mm_nt(gbl[rows, :], weight)
            dgelu[rows, cols] = (grad * dgelu[rows, cols].astype(F32)).astype(BF16)

    back_hidden(0)
    pump()
    back_hidden(1)
    pump()
    back_hidden(2)
    assert not todo
    back_hidden(3)

    def back_second(rows, to, store):
        store[to, :] = mm_nt(dgelu[rows, :], wup[...].reshape(width, ff_half))

    wire.sent(*arrive)
    arrive = send_parts(back_second, part_s, part_r)
    reduce_down[0].second()
    gsec = s["gfirst"]
    back_second(own(0, tokens), slice(0, tokens), gsec)
    gup = s["gup"]
    small = s["small"]
    small[...] = jnp.zeros_like(small)

    def grad_up(j, i):
        left = sec[:, 384 * j : 384 * j + 384]
        wide = mm_tn(left, dgelu[:, i * width : (i + 1) * width]).astype(BF16)
        gup[i][2 * j : 2 * j + 2] = wide.reshape(2, NY, NX, 2 * share, width)

    def norm_two_back(i):
        arrive[i].wait_recv()

        def body(j, total):
            rows = pl.ds(pl.multiple_of(i * quarter + j * 64, 64), 64)
            grad = gsec[rows, :] + part_r[rows, :]
            xhat, root = normalize_again(first[rows, :], s["kept_two"][rows, :])
            part = norm_back(xhat, root, s["gain"][1:2, :], grad)
            full = mix_last * cot_ref[rows, :].astype(F32) + part
            gsec[rows, :] = full
            to = pl.ds(pl.multiple_of(own0 + i * quarter + j * 64, 64), 64)
            gfl[to, :] = full.astype(BF16)
            return total + fold_rows(grad * xhat)

        total = lax.fori_loop(0, quarter // 64, body, jnp.zeros((8, width), F32))
        small[1:2, :] = small[1:2, :] + jnp.sum(total, axis=0, keepdims=True)
        return wire.copy(gfl.at[own(i, quarter)], gfl.at[own(i, quarter)], at.core)

    reduce_up = [
        Reduce(wire, at, gup[i], (width // 2, width), *s["rup"][i]) for i in range(2)
    ]

    def start_up(i):
        for j in range(2):
            grad_up(j, i)
        reduce_up[i].first()

    start_up(0)
    reduce_down[1].second()
    send_gfl = [norm_two_back(0), norm_two_back(1)]
    start_up(1)
    reduce_down[0].third()

    gm = s["gm"]

    def back_mixed(rows):
        gm[rows, :] = mm_nt(gfl[rows, :], output_weight()).astype(BF16)

    back_mixed(own(0, tokens))
    for made in send_gfl:
        made.wait_recv()
    back_mixed(other(0, tokens))
    go = s["go"]
    wide = mm_tn(s["mix"][...], gfl[...])
    left, right = wide[:, :half], wide[:, half:]
    blocks_o = (2, NY, NX, 2 * share, half)
    s["gox"][...] = jnp.where(k == 0, right, left).astype(BF16).reshape(blocks_o)
    swap_go = wire.copy(s["gox"], go.at[pl.ds(2 * k, 2)], at.core)
    go[pl.ds(2 * k, 2)] = jnp.where(k == 0, left, right).astype(BF16).reshape(blocks_o)
    reduce_o = Reduce(wire, at, go, (128, half), *s["ro"])

    lse, delta = s["lse"], s["delta"]
    wire.sent(send_gbl, *send_sec)
    heads_in = [(gbl, 0), (gbl, 384), (sec, 0)]
    gpair = s["gqkv"]
    grad_query = s["dq"]
    reduce_qkv = [
        Reduce(wire, at, gpair[p], (CUTS[p % 3], 384), *s["rqkv"][p]) for p in range(pairs)
    ]

    nothing = lambda: None
    todo.extend(
        [
            reduce_up[0].second,
            reduce_down[1].third,
            reduce_down[0].third_y,
            nothing,
            nothing,
            reduce_up[1].second,
            lambda: (swap_go.wait_recv(), reduce_o.first()),
            reduce_up[0].third,
            reduce_down[1].third_y,
            nothing,
            reduce_down[0].third_x,
            reduce_qkv[0].second,
            reduce_o.second,
            reduce_up[1].third,
            nothing,
            lambda: (reduce_qkv[0].third(), reduce_o.third()),
            lambda: (reduce_qkv[1].second(), reduce_down[1].third_x()),
            reduce_qkv[2].second,
            reduce_qkv[1].third,
            reduce_qkv[2].third,
        ]
    )

    def attend_back(p, b):
        cols = slice(128 * p, 128 * p + 128)
        r0 = b * BLOCK
        rows = slice(r0, r0 + BLOCK)
        after = slice(r0, length)
        count = length - r0
        here_k = lax.broadcasted_iota(jnp.int32, (BLOCK, count), 0)
        here_q = lax.broadcasted_iota(jnp.int32, (BLOCK, count), 1)
        allowed = (here_k <= here_q) & (
            (here_k + r0).astype(F32) >= s["start_row"][0:1, after]
        )
        key, value = ks[rows, cols], vs[rows, cols]
        query, grad = qs[after, cols], gm[after, cols]
        dk = jnp.zeros((BLOCK, 128), F32)
        dv = jnp.zeros((BLOCK, 128), F32)
        dq = jnp.zeros((count, 128), F32)
        for h in range(2):
            key_h = key * ones[h]
            scores = mm_nt(key_h, query)
            weights = jnp.exp(jnp.where(allowed, scores - lse[p, h : h + 1, after], MASKED))
            grad_w = mm_nt(value * ones[h], grad)
            grad_s = (weights * (grad_w - delta[p, h : h + 1, after])).astype(BF16)
            dv = dv + mm(weights.astype(BF16), grad * ones[h])
            dk = dk + mm(grad_s, query * ones[h])
            dq = dq + mm_tn(grad_s, key_h)
        gqkv, base = heads_in[p]
        gqkv[rows, base + 256 : base + 384] = dv.astype(BF16)
        gqkv[rows, base + 128 : base + 256] = turn(
            dk.astype(BF16).astype(F32), rows, -1.0
        ).astype(BF16)
        if b == 0:
            grad_query[...] = dq
        else:
            grad_query[after, :] = grad_query[after, :] + dq

    out_s, out_r = s["out_s"], s["out_r"]

    def contract(rows, to, store):
        store[to, :] = mm(hid[rows, :], wdown[...].reshape(ff_half, width))

    outb = gfl.at[pl.ds(0, tokens)]
    put_out = pltpu.make_async_copy(outb, out_ref, s["osem"].at[0])

    def write_output(arrive_out):
        wire.sent(*send_gfl)
        block_sum = jnp.zeros((8, width), F32)
        for i in range(2):
            rows = pl.ds(i * quarter, quarter)
            mine = mm(hid[own(i, quarter), :], wdown[...].reshape(ff_half, width))
            arrive_out[i].wait_recv()
            block = first[rows, :] + (mine + out_r[rows, :])
            outb[rows, :] = (s["acc"][rows, :] + mix_last * block).astype(BF16)
            block_sum = block_sum + fold_rows(block * cot_ref[rows, :].astype(F32))
        put_out.start()
        terms = jnp.zeros((1, width), F32)
        wide_lane = lax.broadcasted_iota(jnp.int32, (1, width), 1)
        for j in range(hist):
            terms = jnp.where(wide_lane == j, jnp.sum(s["mixacc"][j]), terms)
        small[2:3, :] = jnp.where(wide_lane == hist, jnp.sum(block_sum), terms)

    for p in range(pairs):
        cols = slice(128 * p, 128 * p + 128)

        def inner(i):
            rows = rows_of(i, BLOCK)
            both = jnp.transpose(s["mixf"][rows, cols] * gm[rows, cols].astype(F32))
            delta[p, 0:1, rows] = jnp.sum(both[:HD], axis=0, keepdims=True)
            delta[p, 1:2, rows] = jnp.sum(both[HD:], axis=0, keepdims=True)

        loop(blocks, inner)
        for b in range(blocks):
            attend_back(p, b)
            pump()

        gqkv, base = heads_in[p]

        def turn_query(i):
            rows = rows_of(i, BLOCK)
            low = (grad_query[rows, :] * HD**-0.5).astype(BF16).astype(F32)
            gqkv[rows, base : base + 128] = turn(low, rows, -1.0).astype(BF16)

        loop(blocks, turn_query)

        def grad_qkv(j):
            left = norm[:, pl.ds(pl.multiple_of(j * 384, 128), 384)]
            wide = mm_tn(left, gqkv[:, base : base + 384]).astype(BF16)
            gpair[p][pl.ds(2 * j, 2)] = wide.reshape(2, NY, NX, 2 * share, 384)

        loop(2, grad_qkv)
        reduce_qkv[p].first()
        pump()

    wire.sent(*arrive)

    def normed_grad(rows):
        weight = s["wqkv"][...].reshape(width, qkv_cols)
        return mm_nt(gbl[rows, :], weight[:, :768]) + mm_nt(sec[rows, :384], weight[:, 768:])

    def back_normed(rows, to, store):
        store[to, :] = normed_grad(rows)

    arrive = send_parts(back_normed, part_s, part_r)
    arrive_out = send_parts(contract, out_s, out_r)
    pump(2)
    write_output(arrive_out)
    own_s = first
    back_normed(own(0, tokens), slice(0, tokens), own_s)
    pump()
    total = jnp.zeros((8, width), F32)
    for i in range(2):
        arrive[i].wait_recv()

        def norm_one_back(j, total):
            rows = pl.ds(pl.multiple_of(i * quarter + j * 64, 64), 64)
            grad = own_s[rows, :] + part_r[rows, :]
            xhat, root = normalize_again(in_ref[rows, :].astype(F32), s["kept_one"][rows, :])
            gsec[rows, :] = gsec[rows, :] + norm_back(xhat, root, s["gain"][0:1, :], grad)
            return total + fold_rows(grad * xhat)

        total = lax.fori_loop(0, quarter // 64, norm_one_back, total)
        if i == 0:
            pump()
    put_gin = pltpu.make_async_copy(gsec, gin_ref, s["osem"].at[1])
    put_gin.start()
    small[0:1, :] = jnp.sum(total, axis=0, keepdims=True)

    sp, sz = s["small_p"], s["small_z"]
    sp[k, at.y, at.x] = small[...]
    mine = sp.at[k, at.y, at.x]
    step_p = [wire.copy(mine, mine, device) for device in at.block]
    pump()

    wire.sent(*swap)
    fin, fin_r = xs, xr
    def settle(reduce, c, size):
        total = reduce.result()
        fin[0, :, c : c + size] = total[:share]
        fin[1, :, c : c + size] = total[share:]
        return wire.copy(fin.at[o, :, pl.ds(c, size)], fin_r.at[:, pl.ds(c, size)], at.core)

    up0 = qkv_cols + half
    settled = [settle(reduce_up[i], up0 + i * width, width) for i in range(2)]
    settled.append(settle(reduce_o, qkv_cols, half))
    for i in range(2):
        c = i * half + 2 * half // 3
        s["fin_d"][:, i * half : c] = reduce_down[i].result()
        s["fin_d"][:, c : (i + 1) * half] = reduce_down[i].third_result()
    put_down = pltpu.make_async_copy(s["fin_d"], gdown_ref, s["osem"].at[2])
    put_down.start()
    settled.append(settle(reduce_qkv[0], 0, 384))
    for made in step_p:
        made.wait_recv()
    both = sp[0] + sp[1]
    sz[at.z] = (both[0, 0] + both[0, 1]) + (both[1, 0] + both[1, 1])
    step_z = [wire.copy(sz.at[at.z], sz.at[at.z], at.zn(step)) for step in range(1, NZ)]
    for p in range(1, pairs):
        settled.append(settle(reduce_qkv[p], 384 * p, 384))
    assert not todo
    put_mine = pltpu.make_async_copy(fin.at[k], pack_ref.at[k], s["osem"].at[3])
    put_mine.start()
    for made in settled:
        made.wait_recv()
    put_other = pltpu.make_async_copy(fin_r, pack_ref.at[o], s["osem"].at[4])
    put_other.start()
    for made in step_z:
        made.wait_recv()
    small[...] = ((sz[0] + sz[1]) + sz[2]) + sz[3]
    put_small = pltpu.make_async_copy(small, small_ref, s["osem"].at[5])
    put_small.start()
    for made in (put_down, put_mine, put_other, put_small):
        made.wait()
    put_out.wait()
    put_gin.wait()
    wire.close()


def finish(unit, *refs):
    mix_ref, cot_ref, small_ref, pack_ref, gdown_ref, out_ref, gin_ref = refs[:7]
    out_o, gin_o, ghist_o, gdown_o = refs[7:11]
    rest_o = refs[11:19]
    cot, small, pack, buffer, out, gin, gdown = refs[19:26]
    rest = refs[26:34]
    sems, hsems = refs[34:]
    hist = ghist_o.shape[0]
    tokens, width = cot.shape
    share = pack.shape[1]
    half = width // 2
    gets = [
        pltpu.make_async_copy(src, dst, sems.at[i])
        for i, (src, dst) in enumerate(
            (
                (cot_ref, cot),
                (pack_ref, pack),
                (small_ref, small),
                (out_ref, out),
                (gin_ref, gin),
                (gdown_ref, gdown),
            )
        )
    ]
    for made in gets:
        made.start()
    gets[0].wait()
    puts = []
    rows = 128
    for j in range(hist):

        def scale(i):
            part = rows_of(i, rows)
            buffer[j, part, :] = (mix_ref[j] * cot[part, :].astype(F32)).astype(BF16)

        loop(tokens // rows, scale)
        puts.append(pltpu.make_async_copy(buffer.at[j], ghist_o.at[j], hsems.at[j]))
        puts[j].start()
    for made in gets[1:]:
        made.wait()
    moves = [
        pltpu.make_async_copy(src, dst, sems.at[i])
        for i, (src, dst) in enumerate(((out, out_o), (gin, gin_o), (gdown, gdown_o)))
    ]
    for made in moves:
        made.start()
    gain1, gain2, mix, gq, gk, gv, go, gup = rest
    device = (lax.axis_index("batch") // unit) * 2 + lax.axis_index("seq")
    own = pltpu.roll(small[...], width - device * share, 1)
    gain1[...] = own[0:1, :share]
    gain2[...] = own[1:2, :share]
    mix[...] = small[2:3, : hist + 1]
    for h in range(2):
        for p in range(half // 128):
            for j, ref in enumerate((gq, gk, gv)):
                c = 384 * p + 128 * j
                ref[:, h * half + 128 * p : h * half + 128 * p + 128] = pack[h, :, c : c + 128]
        go[:, h * half : h * half + half] = pack[h, :, 3 * half : 4 * half]
    blk = gdown_o.shape[0]
    gup[...] = jnp.concatenate(
        [
            pack[h, :, 4 * half + blk * i : 4 * half + blk * i + blk]
            for i in range(GROUPS)
            for h in range(2)
        ],
        axis=1,
    )
    for i, (src, dst) in enumerate(zip(rest, rest_o)):
        puts.append(pltpu.make_async_copy(src, dst, sems.at[6 + i]))
        puts[-1].start()
    for made in puts + moves:
        made.wait()


def local(
    unit,
    inputs,
    history,
    segment_ids,
    cotangent,
    mix_weights,
    attn_gain,
    query_weight,
    key_weight,
    value_weight,
    output_weight,
    mlp_gain,
    up_weight,
    down_weight,
):
    rows, tokens, width = inputs.shape
    hist = history.shape[0]
    length = segment_ids.shape[1]
    half = width // 2
    ff_half = up_weight.shape[1] // 2
    share = width // (2 * GROUPS)
    both = 2 * share
    down_share = 2 * ff_half // (2 * GROUPS)
    pairs = half // 128
    seq = lax.axis_index("seq")
    batch = lax.axis_index("batch")
    group_device = (batch // unit) * 2 + seq
    weights = [query_weight, key_weight, value_weight, output_weight, up_weight, down_weight]
    gains = [attn_gain, mlp_gain]
    if unit > 1:
        def widen(value):
            whole = lax.all_gather(value, ("batch", "seq"), axis=0, tiled=True)
            size = value.shape[0] * unit
            return lax.dynamic_slice_in_dim(whole, group_device * size, size)

        weights = [widen(value) for value in weights]
        gains = [widen(value) for value in gains]
    sizes = []

    def scratch(name, shape, dtype=BF16):
        sizes.append((name, pltpu.VMEM(shape, dtype)))

    dims = (NZ, NY, NX)

    def reduction(rows_in, columns, a, b):
        rest = columns - b
        third = [
            pltpu.VMEM((NZ - 1, NY, NX, rows_in, rest), BF16),
            pltpu.VMEM((NX, rows_in, rest), BF16),
            pltpu.VMEM((rows_in, rest), BF16),
        ]
        return [
            pltpu.VMEM((NZ, NX, rows_in, a), BF16),
            pltpu.VMEM((NZ, NY, rows_in, b - a), BF16),
            pltpu.VMEM((NZ, rows_in, b), BF16),
            pltpu.VMEM((NZ - 1, rows_in, b), BF16),
        ] + (third if rest else [])

    sizes.append(("send", pltpu.SemaphoreType.DMA((SENDS,))))
    sizes.append(("recv", pltpu.SemaphoreType.DMA((COPIES,))))
    sizes.append(("hsem", pltpu.SemaphoreType.DMA((HBUF,))))
    sizes.append(("osem", pltpu.SemaphoreType.DMA((6,))))
    scratch("fin_d", (down_share, width), F32)
    sizes.append(("isem", pltpu.SemaphoreType.DMA((9,))))
    scratch("seg", (1, length), jnp.int32)
    scratch("in", (tokens, width))
    scratch("cot", (tokens, width))
    for i, value in enumerate(weights):
        scratch("w%d" % i, value.shape)
    scratch("hbuf", (HBUF, hist, 32, width))
    scratch("xs", (2, share, 2 * half + 2 * half + ff_half), F32)
    scratch("xr", (share, 2 * half + 2 * half + ff_half), F32)
    scratch("ga", (2,) + dims + (8, 128), F32)
    scratch("gain", (8, width), F32)
    scratch("wqkv", dims + (both, 3 * half))
    scratch("wo", dims + (both, half))
    scratch("wof", (2, NY, NX, both, width))
    scratch("wup", dims + (both, ff_half))
    scratch("wdown", dims + (down_share, width))
    for name in ("gbl", "norm", "sec", "gfl"):
        scratch(name, (length, width))
    scratch("kept_one", (tokens, 128), F32)
    scratch("kept_two", (tokens, 128), F32)
    scratch("start_row", (8, length), F32)
    scratch("start_col", (length, 128), F32)
    scratch("cos", (length, 128), F32)
    scratch("sin", (length, 128), F32)
    scratch("acc", (tokens, width), F32)
    scratch("mixacc", (hist, 8, 128), F32)
    for name in ("q", "kk", "v", "mix", "gm"):
        scratch(name, (length, half))
    scratch("mixf", (length, half), F32)
    scratch("lse", (pairs, 8, length), F32)
    scratch("delta", (pairs, 8, length), F32)
    scratch("dq", (length, 128), F32)
    for name in ("part_s", "part_r", "out_s", "out_r", "first", "gfirst"):
        scratch(name, (tokens, width), F32)
    scratch("hid", (length, ff_half))
    scratch("dgelu", (length, ff_half))
    scratch("gox", (2, NY, NX, both, half))
    scratch("small", (8, width), F32)
    scratch("small_p", (2, NY, NX, 8, width), F32)
    scratch("small_z", (NZ, 8, width), F32)
    sizes.append(("gdown", [pltpu.VMEM(dims + (down_share, half), BF16) for _ in range(2)]))
    sizes.append(("gup", [pltpu.VMEM(dims + (both, width), BF16) for _ in range(2)]))
    scratch("go", dims + (both, half))
    sizes.append(("gqkv", [pltpu.VMEM(dims + (both, 384), BF16) for _ in range(pairs)]))
    sizes.append(("rdown", [reduction(down_share, half, half // 3, 2 * half // 3) for _ in range(2)]))
    sizes.append(("rup", [reduction(both, width, width // 2, width) for _ in range(2)]))
    sizes.append(("ro", reduction(both, half, 128, half)))
    sizes.append(("rqkv", [reduction(both, 384, CUTS[p % 3], 384) for p in range(pairs)]))
    names = [name for name, _ in sizes]

    vmem = pl.BlockSpec(memory_space=pltpu.VMEM)
    anywhere = pl.BlockSpec(memory_space=pl.ANY)
    smem = pl.BlockSpec(memory_space=pltpu.SMEM)
    shape = jax.ShapeDtypeStruct
    outs = pl.pallas_call(
        functools.partial(layer, unit, names),
        out_shape=(
            shape((tokens, width), BF16),
            shape((tokens, width), F32),
            shape((2, share, 4 * half + ff_half), F32),
            shape((down_share, width), F32),
            shape((8, width), F32),
        ),
        in_specs=[smem, vmem, vmem] + [anywhere] * 10,
        out_specs=[anywhere] * 5,
        scratch_shapes=[size for _, size in sizes],
        compiler_params=pltpu.CompilerParams(
            collective_id=0, has_side_effects=True, vmem_limit_bytes=64 * 1024 * 1024 - 64 * 1024
        ),
    )(
        mix_weights,
        gains[0].reshape(1, share),
        gains[1].reshape(1, share),
        segment_ids,
        inputs.reshape(tokens, width),
        cotangent.reshape(tokens, width),
        *weights,
        history.reshape(hist, tokens, width),
    )
    partial_out, partial_gin, pack, gdown, small = outs
    rest = [
        shape((1, share), F32),
        shape((1, share), F32),
        shape((1, hist + 1), F32),
        shape((share, width), F32),
        shape((share, width), F32),
        shape((share, width), F32),
        shape((share, width), F32),
        shape((share, 2 * ff_half), F32),
    ]
    ends = pl.pallas_call(
        functools.partial(finish, unit),
        out_shape=[
            shape((tokens, width), BF16),
            shape((tokens, width), F32),
            shape((hist, tokens, width), BF16),
            shape((down_share, width), F32),
        ]
        + rest,
        in_specs=[smem] + [anywhere] * 6,
        out_specs=[anywhere] * 12,
        scratch_shapes=[
            pltpu.VMEM((tokens, width), BF16),
            pltpu.VMEM((8, width), F32),
            pltpu.VMEM((2, share, 4 * half + ff_half), F32),
            pltpu.VMEM((hist, tokens, width), BF16),
            pltpu.VMEM((tokens, width), BF16),
            pltpu.VMEM((tokens, width), F32),
            pltpu.VMEM((down_share, width), F32),
        ]
        + [pltpu.VMEM(one.shape, F32) for one in rest]
        + [pltpu.SemaphoreType.DMA((14,)), pltpu.SemaphoreType.DMA((hist,))],
        compiler_params=pltpu.CompilerParams(vmem_limit_bytes=64 * 1024 * 1024 - 64 * 1024),
    )(
        mix_weights,
        cotangent.reshape(tokens, width),
        small,
        pack,
        gdown,
        partial_out,
        partial_gin,
    )
    output, grad_inputs, grad_history, gdown, gain_one, gain_two, mix_grad = ends[:7]
    grads = list(ends[7:]) + [gdown, gain_one.reshape(share), gain_two.reshape(share)]
    mix_grad = mix_grad.reshape(hist + 1)
    if unit > 1:
        def narrow(value):
            whole = jnp.zeros((value.shape[0] * 2 * GROUPS,) + value.shape[1:], F32)
            whole = lax.dynamic_update_slice_in_dim(whole, value, group_device * value.shape[0], 0)
            return lax.psum_scatter(whole, ("batch", "seq"), scatter_dimension=0, tiled=True)

        grads = [narrow(value) for value in grads]
        mix_grad = lax.psum(mix_grad, ("batch", "seq")) / (2 * GROUPS)
    gq, gk, gv, go, gup, gdown, gain_one, gain_two = grads
    return (
        output.reshape(rows, tokens, width),
        grad_inputs.reshape(rows, tokens, width),
        grad_history.reshape(hist, rows, tokens, width),
        mix_grad,
        gain_one,
        gq,
        gk,
        gv,
        go,
        gain_two,
        gup,
        gdown,
    )


def solution(mesh):
    batch = mesh.shape["batch"]
    split = P(("batch", "seq"), None)
    gain = P(("batch", "seq"))
    placed = (
        P("batch", "seq", None),
        P(None, "batch", "seq", None),
        P("batch", None),
        P("batch", "seq", None),
        P(),
        gain,
        split,
        split,
        split,
        split,
        gain,
        split,
        split,
    )
    return jax.shard_map(
        functools.partial(local, batch // GROUPS),
        mesh=mesh,
        in_specs=placed,
        out_specs=(
            P("batch", "seq", None),
            P("batch", "seq", None),
            P(None, "batch", "seq", None),
            P(),
            gain,
            split,
            split,
            split,
            split,
            gain,
            split,
            split,
        ),
        check_vma=False,
    )
```

```python
import functools

import jax
import jax.numpy as jnp
import numpy as np
from jax import lax
from jax.experimental import pallas as pl
from jax.experimental.pallas import tpu as pltpu
from jax.sharding import PartitionSpec as P

HD = 64
EPSILON = 1e-05
MASKED = -1000000000.0
MESH = pl.DeviceIdType.MESH
F32 = jnp.float32
BF16 = jnp.bfloat16
NZ, NY, NX = 4, 2, 2
GROUPS = NZ * NY * NX
COPIES = 192
SENDS = 32
UP_CUTS = (5, 10)
CUTS = (256, 128, 256)
HBUF = 3
BLOCK = 256


def mm(a, b):
    return lax.dot_general(a, b, (((1,), (0,)), ((), ())), preferred_element_type=F32)


def mm_nt(a, b):
    return lax.dot_general(a, b, (((1,), (1,)), ((), ())), preferred_element_type=F32)


def mm_tn(a, b):
    return lax.dot_general(a, b, (((0,), (0,)), ((), ())), preferred_element_type=F32)


def loop(count, body):
    def step(i, carry):
        body(i)
        return carry

    lax.fori_loop(0, count, step, 0)


def rows_of(i, size):
    return pl.ds(pl.multiple_of(i * size, size), size)


def lane_cut(start, size):
    return pl.ds(pl.multiple_of(start, 128), size)


def normalize(value):
    mean = jnp.mean(value, axis=-1, keepdims=True)
    centred = value - mean
    variance = jnp.mean(centred * centred, axis=-1, keepdims=True)
    root = lax.rsqrt(variance + EPSILON)
    return centred * root, jnp.where(lax.broadcasted_iota(jnp.int32, (1, 128), 1) == 0, mean, root)


def normalize_again(value, kept):
    root = kept[:, 1:2]
    return (value - kept[:, 0:1]) * root, root


def norm_back(xhat, root, gain, grad):
    g = grad * gain
    return root * (
        g - jnp.mean(g, axis=-1, keepdims=True) - xhat * jnp.mean(g * xhat, axis=-1, keepdims=True)
    )


def fold_rows(value):
    total = value[0:8]
    for r in range(8, value.shape[0], 8):
        total = total + value[r : r + 8]
    return total


class Place:
    def __init__(self, unit):
        batch = lax.axis_index("batch")
        self.k = lax.axis_index("seq")
        self.o = 1 - self.k
        group = batch // unit
        self.unit = unit
        self.u = batch % unit
        self.z = group // (NY * NX)
        self.y = (group // NX) % NY
        self.x = group % NX
        self.core = (batch, self.o)
        self.xn = self.device(self.z, self.y, 1 - self.x)
        self.yn = self.device(self.z, 1 - self.y, self.x)
        self.diagonal = self.device(self.z, 1 - self.y, 1 - self.x)
        self.block = [self.xn, self.yn, self.diagonal, self.core] + [
            (batch_of, self.o) for batch_of, _ in (self.xn, self.yn, self.diagonal)
        ]

    def device(self, z, y, x):
        return (((z * NY + y) * NX + x) * self.unit + self.u, self.k)

    def across(self, step):
        if step == 0:
            return self.z
        if step == 2:
            return (self.z + 2) % NZ
        flip = self.z + 1 - 2 * (self.z % 2)
        return flip if step == 1 else (flip + 2) % NZ

    def zn(self, step):
        return self.device(self.across(step), self.y, self.x)


def guarded(condition, action):
    if condition is None:
        action()
    else:
        pl.when(condition)(action)


class Wire:
    def __init__(self, send, recv):
        self.send = send
        self.recv = recv
        self.open = []
        self.count = 0
        self.slots = 0

    def slot(self):
        self.slots += 1
        return self.slots - 1

    def copy(self, src, dst, device, condition=None, slot=None):
        i = self.count
        self.count += 1
        while self.open and self.open[0][0] <= i - SENDS:
            _, made, held = self.open.pop(0)
            guarded(held, made.wait_send)
        made = pltpu.make_async_remote_copy(
            src_ref=src,
            dst_ref=dst,
            send_sem=self.send.at[i % SENDS],
            recv_sem=self.recv.at[self.slot() if slot is None else slot],
            device_id=device,
            device_id_type=MESH,
        )
        guarded(condition, made.start)
        self.open.append((i, made, condition))
        return made

    def sent(self, *copies):
        for made in copies:
            if any(one is made for _, one, _ in self.open):
                made.wait_send()
                self.open = [entry for entry in self.open if entry[1] is not made]

    def close(self):
        for _, made, held in self.open:
            guarded(held, made.wait_send)


class Column:
    def __init__(self, wire, at, block, layer):
        self.wire, self.at, self.block, self.layer = wire, at, block, layer
        self.middle = (at.z == 1) | (at.z == 2)
        self.outer = (at.z == 0) | (at.z == 3)

    def start(self):
        at = self.at
        own = self.block(at.z)
        self.slots = {2: self.wire.slot(), 3: self.wire.slot()}
        self.made = {
            1: self.wire.copy(own, own, at.zn(1)),
            2: self.wire.copy(own, own, at.zn(3), self.middle, self.slots[2]),
            3: self.wire.copy(own, own, at.zn(2), self.outer, self.slots[3]),
        }

    def take(self, step):
        guarded(self.middle, self.made[step].wait_recv)
        part = self.block(self.layer(step))
        self.wire.copy(part, part, self.at.zn(1), self.middle, self.slots[step])

    def wait(self, step):
        guarded(self.outer if step > 1 else None, self.made[step].wait_recv)


class Gather:
    def __init__(self, wire, at, ref, a, b=None):
        self.wire, self.at, self.ref, self.a = wire, at, ref, a
        self.b = ref.shape[-1] if b is None else b
        self.third = self.b < ref.shape[-1]
        self.mid, self.last = {}, {}
        if self.third:
            self.z = Column(wire, at, lambda zz: ref.at[zz, at.y, at.x, :, : self.b], self.layer)
            self.cz = Column(wire, at, lambda zz: ref.at[zz, :, :, :, self.b :], self.layer)
        else:
            self.z = Column(wire, at, lambda zz: ref.at[zz, at.y, at.x], self.layer)

    def layer(self, step):
        z = self.at.z
        if step < 2:
            return self.at.across(step)
        return 2 - z // 2 if step == 2 else (NZ - 1) * (1 - z // 2)

    def pass_mid(self, *steps):
        at, ref = self.at, self.ref
        for step in steps:
            if step:
                self.z.wait(step)
            zz = self.layer(step)
            left = ref.at[zz, at.y, at.x, :, : self.a]
            right = ref.at[zz, at.y, at.x, :, self.a : self.b]
            self.mid[step] = (
                self.wire.copy(left, left, at.xn),
                self.wire.copy(right, right, at.yn),
            )

    def pass_last(self, step):
        at, ref = self.at, self.ref
        zz = self.layer(step)
        self.mid[step][0].wait_recv()
        left = ref.at[zz, at.y, :, :, : self.a]
        one = self.wire.copy(left, left, at.yn)
        self.mid[step][1].wait_recv()
        right = ref.at[zz, :, at.x, :, self.a : self.b]
        self.last[step] = (one, self.wire.copy(right, right, at.xn))

    def third_x(self):
        at = self.at
        part = self.ref.at[at.z, at.y, at.x, :, self.b :]
        self.cx = self.wire.copy(part, part, at.xn)

    def third_y(self):
        at = self.at
        self.cx.wait_recv()
        part = self.ref.at[at.z, at.y, :, :, self.b :]
        self.cy = self.wire.copy(part, part, at.yn)

    def third_z(self):
        self.cy.wait_recv()
        self.cz.start()

    def arrived(self, step):
        for made in self.last[step]:
            made.wait_recv()
        if self.third and step:
            self.cz.wait(step)

    def finish(self):
        for step in range(NZ):
            self.arrived(step)


class Reduce:
    def __init__(self, wire, at, grad, cuts, one_a, one_b, two, three, *third):
        self.wire, self.at, self.grad = wire, at, grad
        self.a, self.b = cuts
        self.one_a, self.one_b, self.two, self.three = one_a, one_b, two, three
        self.third_refs = third

    def add(self, index, more):
        self.grad[index] = (self.grad[index].astype(F32) + more.astype(F32)).astype(BF16)

    def first(self):
        at, grad, a, b = self.at, self.grad, self.a, self.b
        self.sa = self.wire.copy(grad.at[:, 1 - at.y, :, :, :a], self.one_a, at.yn)
        self.sb = self.wire.copy(grad.at[:, :, 1 - at.x, :, a:b], self.one_b, at.xn)
        if self.third_refs:
            self.cz = [
                self.wire.copy(
                    grad.at[at.across(step), :, :, :, b:], self.third_refs[0].at[step - 1], at.zn(step)
                )
                for step in range(1, NZ)
            ]

    def second(self):
        at, grad, a, b = self.at, self.grad, self.a, self.b
        left, right = slice(0, a), slice(a, b)

        def add_a(xx):
            loop(NZ, lambda zz: self.add((zz, at.y, xx, slice(None), left), self.one_a[zz, xx]))

        def add_b(yy):
            loop(NZ, lambda zz: self.add((zz, yy, at.x, slice(None), right), self.one_b[zz, yy]))

        self.sa.wait_recv()
        add_a(1 - at.x)
        self.saa = self.wire.copy(grad.at[:, at.y, 1 - at.x, :, :a], self.two.at[:, :, :a], at.xn)
        self.sb.wait_recv()
        add_b(1 - at.y)
        self.sbb = self.wire.copy(grad.at[:, 1 - at.y, at.x, :, a:b], self.two.at[:, :, a:], at.yn)
        add_a(at.x)
        add_b(at.y)

    def third(self):
        at, grad, b = self.at, self.grad, self.b
        self.saa.wait_recv()
        self.sbb.wait_recv()
        loop(NZ, lambda zz: self.add((zz, at.y, at.x, slice(None), slice(0, b)), self.two[zz]))
        self.sz = []
        for step in range(1, NZ):
            part = grad.at[at.across(step), at.y, at.x, :, :b]
            self.sz.append(self.wire.copy(part, self.three.at[step - 1], at.zn(step)))

    def third_y(self):
        at, grad, b = self.at, self.grad, self.b
        for made in self.cz:
            made.wait_recv()
        ref = self.third_refs[0]

        def body(yx):
            y, x = yx // NX, yx % NX
            more = ref[0, y, x].astype(F32) + ref[1, y, x].astype(F32) + ref[2, y, x].astype(F32)
            self.add((at.z, y, x, slice(None), slice(b, None)), more)

        loop(NY * NX, body)
        self.cy = self.wire.copy(grad.at[at.z, 1 - at.y, :, :, b:], self.third_refs[1], at.yn)

    def third_x(self):
        at, grad, b = self.at, self.grad, self.b
        self.cy.wait_recv()
        ref = self.third_refs[1]
        loop(NX, lambda x: self.add((at.z, at.y, x, slice(None), slice(b, None)), ref[x]))
        self.cx = self.wire.copy(grad.at[at.z, at.y, 1 - at.x, :, b:], self.third_refs[2], at.xn)

    def result(self):
        at, b = self.at, self.b
        total = self.grad[at.z, at.y, at.x, :, :b].astype(F32)
        for step in range(1, NZ):
            self.sz[step - 1].wait_recv()
            total = total + self.three[step - 1].astype(F32)
        return total

    def third_result(self):
        at = self.at
        self.cx.wait_recv()
        return self.grad[at.z, at.y, at.x, :, self.b :].astype(F32) + self.third_refs[2][
            ...
        ].astype(F32)


def layer(unit, names, *refs):
    (
        mix_ref, gain1_ref, gain2_ref, seg_any, in_any, cot_any,
        q_any, k_any, v_any, o_any, up_any, down_any, hist_ref,
        out_ref, gin_ref, pack_ref, gdown_ref, small_ref,
    ) = refs[:18]
    s = dict(zip(names, refs[18:]))
    seg_ref, in_ref, cot_ref = s["seg"], s["in"], s["cot"]
    q_ref, k_ref, v_ref, o_ref, up_ref, down_ref = (s[n] for n in ("w0", "w1", "w2", "w3", "w4", "w5"))
    tokens, width = in_ref.shape
    length = 2 * tokens
    half = width // 2
    ff_half = up_ref.shape[1] // 2
    pairs = half // 128
    share = q_ref.shape[0]
    down_rows = down_ref.shape[0]
    blocks = length // BLOCK
    hist = hist_ref.shape[0]
    at = Place(unit)
    k, o = at.k, at.o
    wire = Wire(s["send"], s["recv"])

    barrier = pltpu.get_barrier_semaphore()
    for device in (*at.block, at.zn(1), at.zn(2), at.zn(3)):
        pl.semaphore_signal(barrier, inc=1, device_id=device, device_id_type=MESH)
    gets = []
    for src, dst in (
        (q_any, q_ref), (k_any, k_ref), (v_any, v_ref), (o_any, o_ref), (up_any, up_ref),
        (down_any, down_ref), (seg_any, seg_ref), (in_any, in_ref), (cot_any, cot_ref),
    ):
        gets.append(pltpu.make_async_copy(src, dst, s["isem"].at[len(gets)]))
        gets[-1].start()
    hist_rows = s["hbuf"].shape[2]
    hist_chunks = tokens // hist_rows

    def fetch(i):
        return pltpu.make_async_copy(
            hist_ref.at[:, pl.ds(i * hist_rows, hist_rows)],
            s["hbuf"].at[i % HBUF],
            s["hsem"].at[i % HBUF],
        )

    for i in range(HBUF - 1):
        fetch(i).start()

    for made in gets[:3]:
        made.wait()

    xs, xr = s["xs"], s["xr"]
    qkv_cols = 3 * half
    blk = down_rows
    for h in range(2):
        c = h * half
        for i in range(pairs):
            for j, ref in enumerate((q_ref, k_ref, v_ref)):
                xs[h, :, 384 * i + 128 * j : 384 * i + 128 * j + 128] = ref[
                    :, c + 128 * i : c + 128 * i + 128
                ].astype(F32)
    ga = s["ga"]
    ga[k, at.z, at.y, at.x] = jnp.zeros((8, 128), F32)
    ga[k, at.z, at.y, at.x, 0:1, :share] = gain1_ref[...].astype(F32)
    ga[k, at.z, at.y, at.x, 1:2, :share] = gain2_ref[...].astype(F32)

    pl.semaphore_wait(barrier, 10)

    swap = [wire.copy(xs.at[o, :, :qkv_cols], xr.at[:, :qkv_cols], at.core)]
    gain_z = [
        wire.copy(ga.at[k, at.z, at.y, at.x], ga.at[k, at.z, at.y, at.x], at.zn(step))
        for step in range(1, NZ)
    ]
    for made in gets[3:6]:
        made.wait()
    s["wdown"][at.z, at.y, at.x] = down_ref[...]
    gather_down = Gather(wire, at, s["wdown"], width // 3, 2 * width // 3)
    gather_down.third_x()
    gather_down.pass_mid(0)
    wide = up_ref[...].astype(F32)
    for h in range(2):
        c = h * half
        xs[h, :, qkv_cols : qkv_cols + half] = o_ref[:, c : c + half].astype(F32)
        xs[h, :, qkv_cols + half :] = jnp.concatenate(
            [
                wide[:, 2 * blk * i + blk * h : 2 * blk * i + blk * h + blk]
                for i in range(GROUPS)
            ],
            axis=1,
        )
    swap.append(wire.copy(xs.at[o, :, qkv_cols:], xr.at[:, qkv_cols:], at.core))

    own0 = pl.multiple_of(k * tokens, tokens)
    other0 = pl.multiple_of(o * tokens, tokens)

    def own(i, size):
        return pl.ds(pl.multiple_of(own0 + i * size, size), size)

    def other(i, size):
        return pl.ds(pl.multiple_of(other0 + i * size, size), size)

    mix_last = mix_ref[hist]
    gbl, norm, sec, gfl = s["gbl"], s["norm"], s["sec"], s["gfl"]

    def own_block(cols):
        mine = xs[k, :, cols]
        theirs = xr[:, cols]
        upper = jnp.where(k == 0, mine, theirs)
        lower = jnp.where(k == 0, theirs, mine)
        return jnp.concatenate([upper, lower], axis=0).astype(BF16)

    gather_qkv = Gather(wire, at, s["wqkv"], 640)
    gather_o = Gather(wire, at, s["wo"], 128)
    gather_up = Gather(wire, at, s["wup"], UP_CUTS[0] * ff_half // 12, UP_CUTS[1] * ff_half // 12)
    swap[0].wait_recv()
    s["wqkv"][at.z, at.y, at.x] = own_block(slice(0, qkv_cols))
    gather_qkv.z.start()
    gather_qkv.pass_mid(0)
    swap[1].wait_recv()
    s["wo"][at.z, at.y, at.x] = own_block(slice(qkv_cols, qkv_cols + half))
    s["wup"][at.z, at.y, at.x] = own_block(slice(qkv_cols + half, qkv_cols + half + ff_half))
    gather_up.third_x()
    gather_up.pass_mid(0)
    todo = [
        lambda: (gather_qkv.pass_last(0), gather_o.z.start()),
        lambda: (
            gather_qkv.z.take(2),
            gather_qkv.pass_mid(1),
            gather_o.pass_mid(0),
            gather_up.pass_last(0),
            gather_up.z.start(),
        ),
        lambda: (
            gather_qkv.z.take(3),
            gather_qkv.pass_mid(2),
            gather_up.third_y(),
            gather_down.third_y(),
        ),
        lambda: (
            gather_qkv.pass_mid(3),
            gather_o.z.take(2),
            gather_o.z.take(3),
        ),
        lambda: (
            gather_qkv.pass_last(1),
            gather_qkv.pass_last(2),
            gather_up.z.take(2),
        ),
        lambda: (
            gather_qkv.pass_last(3),
            gather_up.z.take(3),
            gather_up.third_z(),
            gather_down.z.start(),
            gather_o.pass_last(0),
        ),
        lambda: (gather_up.pass_mid(1), gather_o.pass_mid(1, 2, 3)),
    ]
    later = [
        lambda: (gather_up.pass_mid(2, 3), gather_up.cz.take(2), gather_up.cz.take(3)),
        lambda: (gather_o.pass_last(1), gather_o.pass_last(2), gather_down.z.take(2)),
        lambda: (gather_o.pass_last(3), gather_up.pass_last(1), gather_down.z.take(3)),
        lambda: gather_down.third_z(),
        lambda: gather_up.pass_last(2),
        lambda: (gather_up.pass_last(3), gather_down.cz.take(2)),
        lambda: (gather_down.pass_mid(1, 2), gather_down.cz.take(3)),
        lambda: (gather_down.pass_last(0), gather_down.pass_mid(3)),
        lambda: gather_down.pass_last(1),
        lambda: gather_down.pass_last(2),
        lambda: gather_down.pass_last(3),
    ]

    def pump(count=1):
        for _ in range(count):
            if todo:
                todo.pop(0)()

    for made in gets[6:]:
        made.wait()
    seg = seg_ref[...].astype(F32)
    seg_col = jnp.transpose(jnp.broadcast_to(seg, (128, length)))
    start_row = jnp.zeros((1, length), F32)
    start_col = jnp.zeros((length, 128), F32)
    for d in range(7):
        count = jnp.sum(jnp.where(seg == d, 1.0, 0.0), axis=1, keepdims=True)
        start_row = start_row + jnp.where(seg > d, count, 0.0)
        start_col = start_col + jnp.where(seg_col > d, count, 0.0)
    s["start_row"][...] = jnp.broadcast_to(start_row, (8, length))
    s["start_col"][...] = start_col
    lane = lax.broadcasted_iota(jnp.int32, (1, 128), 1)
    first_half = (lane % HD) < (HD // 2)

    def rope_tables(i):
        rows = rows_of(i, 64)
        order = (lax.broadcasted_iota(jnp.int32, (64, 128), 0) + i * 64).astype(F32)
        angles = (order - s["start_col"][rows, :]) * freq
        s["cos"][rows, :] = jnp.cos(angles)
        sine = jnp.sin(angles)
        s["sin"][rows, :] = jnp.where(first_half, -sine, sine)

    freq = jnp.zeros((1, 128), F32)
    for i in range(HD // 2):
        rate = float(np.float32(10000.0 ** (-2.0 * i / HD)))
        freq = jnp.where(lane % (HD // 2) == i, rate, freq)
    loop(length // 64, rope_tables)
    for step in range(1, NZ):
        gain_z[step - 1].wait_recv()
    gain_x = wire.copy(ga.at[k, :, at.y, at.x], ga.at[k, :, at.y, at.x], at.xn)
    pump()

    def low_block(i):
        gbl[own(i, 32), :] = (mix_last * cot_ref[rows_of(i, 32), :].astype(F32)).astype(BF16)

    loop(tokens // 32, low_block)
    send_gbl = wire.copy(
        gbl.at[pl.ds(own0, tokens)], gbl.at[pl.ds(own0, tokens)], at.core
    )
    pump()

    def history_chunk(i):
        if i + HBUF - 1 < hist_chunks:
            fetch(i + HBUF - 1).start()
        fetch(i).wait()

        def group(r, sums):
            rows = rows_of(r, 16)
            whole = pl.ds(pl.multiple_of(i * hist_rows + r * 16, 16), 16)
            cot = cot_ref[whole, :].astype(F32)
            total = jnp.zeros((16, width), F32)
            out = []
            for j in range(hist):
                earlier = s["hbuf"][i % HBUF, j, rows, :].astype(F32)
                total = total + mix_ref[j] * earlier
                term = fold_rows(earlier * cot)
                part = sums[j]
                for c in range(0, width, 128):
                    part = part + term[:, c : c + 128]
                out.append(part)
            s["acc"][whole, :] = total
            return tuple(out)

        sums = lax.fori_loop(
            0, hist_rows // 16, group, tuple(s["mixacc"][j] for j in range(hist))
        )
        for j in range(hist):
            s["mixacc"][j] = sums[j]

    s["mixacc"][...] = jnp.zeros_like(s["mixacc"])
    history_chunk(0)
    history_chunk(1)
    gain_x.wait_recv()
    gain_y = wire.copy(ga.at[k, :, at.y], ga.at[k, :, at.y], at.yn)
    pump()
    history_chunk(2)
    history_chunk(3)
    pump()
    history_chunk(4)
    gain_y.wait_recv()
    gain_c = wire.copy(ga.at[k], ga.at[k], at.core)
    pump()
    gain_c.wait_recv()

    lanes = lax.broadcasted_iota(jnp.int32, (128, width), 1).astype(F32)
    rows_i = lax.broadcasted_iota(jnp.int32, (128, width), 0)
    owner = jnp.floor((lanes + 0.5) * (1.0 / share))
    spread = jnp.where(lanes - share * owner == rows_i.astype(F32), 1.0, 0.0).astype(BF16)
    gain_rows = [jnp.zeros((1, width), F32), jnp.zeros((1, width), F32)]
    for kk in range(2):
        tiles = ga[kk].reshape(GROUPS * 8, 128).astype(BF16)
        wide = mm(tiles, spread)
        for r in range(2):
            hit = ((rows_i % 8) == r) & (owner == (2 * (rows_i // 8) + kk).astype(F32))
            gain_rows[r] = gain_rows[r] + jnp.sum(
                jnp.where(hit, wide, 0.0), axis=0, keepdims=True
            )
    s["gain"][...] = jnp.concatenate([gain_rows[0], gain_rows[1], jnp.zeros((6, width), F32)], axis=0)

    def norm_one(i):
        xhat, s["kept_one"][rows_of(i, 128), :] = normalize(in_ref[rows_of(i, 128), :].astype(F32))
        norm[own(i, 128), :] = (xhat * s["gain"][0:1, :]).astype(BF16)

    loop(tokens // 128, norm_one)
    send_norm = wire.copy(norm.at[pl.ds(own0, tokens)], norm.at[pl.ds(own0, tokens)], at.core)
    pump()
    for i in range(5, hist_chunks):
        history_chunk(i)
        if i % 3 == 1:
            pump()
    while len(todo) > 0:
        pump()
    todo.extend(later)
    send_norm.wait_recv()
    send_gbl.wait_recv()
    gather_qkv.finish()

    qs, ks, vs = s["q"], s["kk"], s["v"]

    def turn(value, rows, sign):
        partner = jnp.where(first_half, pltpu.roll(value, 96, 1), pltpu.roll(value, 32, 1))
        return value * s["cos"][rows, :] + (sign * partner) * s["sin"][rows, :]

    def project(i):
        rows = rows_of(i, BLOCK)
        left = norm[rows, :]
        both_pairs = mm(left, s["wqkv"][:, :, :, :, :768].reshape(width, 768))
        for p in range(pairs):
            if p < 2:
                wide = both_pairs[:, 384 * p : 384 * p + 384]
            else:
                wide = mm(left, s["wqkv"][:, :, :, :, 768:].reshape(width, qkv_cols - 768))
            cols = slice(128 * p, 128 * p + 128)
            qs[rows, cols] = (turn(wide[:, :128], rows, 1.0).astype(BF16) * HD**-0.5).astype(BF16)
            ks[rows, cols] = turn(wide[:, 128:256], rows, 1.0).astype(BF16)
            vs[rows, cols] = wide[:, 256:].astype(BF16)

    for i in range(blocks):
        project(i)
        pump()

    lane_low = lane < HD
    ones = [
        jnp.where(lane_low, 1.0, 0.0).astype(BF16),
        jnp.where(lane_low, 0.0, 1.0).astype(BF16),
    ]

    def attend(p, b):
        cols = slice(128 * p, 128 * p + 128)
        r0 = b * tokens
        rows = slice(r0, r0 + tokens)
        here_q = lax.broadcasted_iota(jnp.int32, (tokens, tokens), 0)
        here_k = lax.broadcasted_iota(jnp.int32, (tokens, tokens), 1)
        start = s["start_col"][rows, 0:1]
        outs, tops = [], []
        for h in range(2):
            query = qs[rows, cols] * ones[h]
            near = mm_nt(query, ks[rows, cols])
            near = jnp.where(
                (here_k <= here_q) & ((here_k + r0).astype(F32) >= start), near, MASKED
            )
            top = jnp.max(near, axis=1, keepdims=True)
            if b:
                far = mm_nt(query, ks[0:r0, cols])
                far_k = lax.broadcasted_iota(jnp.int32, (1, r0), 1).astype(F32)
                far = jnp.where(far_k >= start, far, MASKED)
                top = jnp.maximum(top, jnp.max(far, axis=1, keepdims=True))
            raw = jnp.exp(near - top).astype(BF16)
            out = mm(raw, vs[rows, cols] * ones[h] + ones[1 - h])
            if b:
                raw = jnp.exp(far - top).astype(BF16)
                out = out + mm(raw, vs[0:r0, cols] * ones[h] + ones[1 - h])
            outs.append(out)
            tops.append(top)
        total = jnp.where(lane_low, pltpu.roll(outs[0], HD, 1), pltpu.roll(outs[1], HD, 1))
        mixed = jnp.where(lane_low, outs[0], outs[1]) / total
        s["mix"][rows, cols] = mixed.astype(BF16)
        s["mixf"][rows, cols] = mixed
        log_total = jnp.transpose(jnp.where(lane_low, tops[0], tops[1]) + jnp.log(total))
        s["lse"][p, 0:1, rows] = log_total[0:1]
        s["lse"][p, 1:2, rows] = log_total[HD : HD + 1]

    wo, wof = s["wo"], s["wof"]
    my_cols = lane_cut(k * half, half)
    for p in range(pairs):
        for b in range(2):
            attend(p, b)
        pump()
        if p == 1:
            gather_o.finish()
            swap_o = wire.copy(wo.at[pl.ds(2 * o, 2)], wof.at[:, :, :, :, my_cols], at.core)
            wof[:, :, :, :, my_cols] = wo[pl.ds(2 * k, 2)]

    swap_o.wait_recv()

    def output_weight():
        return wof[...].reshape(half, width)

    part_s, part_r = s["part_s"], s["part_r"]
    quarter = tokens // 2

    def send_parts(make, store, recv, pieces=1):
        made = []
        size = tokens // pieces
        for i in range(pieces):
            make(other(i, size), rows_of(i, size), store)
            for j in range(2 // pieces):
                to = pl.ds((i * (2 // pieces) + j) * quarter, quarter)
                made.append(wire.copy(store.at[to], recv.at[to], at.core))
        return made

    def attended(rows, to, store):
        store[to, :] = mm(s["mix"][rows, :], output_weight())

    arrive = send_parts(attended, part_s, part_r, 2)
    first = s["first"]
    for i in range(2):
        attended(own(i, quarter), rows_of(i, quarter), first)
    send_sec = []
    for i in range(2):
        arrive[i].wait_recv()

        def norm_two(j):
            rows = pl.ds(pl.multiple_of(i * quarter + j * 128, 128), 128)
            value = in_ref[rows, :].astype(F32) + (first[rows, :] + part_r[rows, :])
            first[rows, :] = value
            xhat, s["kept_two"][rows, :] = normalize(value)
            to = pl.ds(pl.multiple_of(own0 + i * quarter + j * 128, 128), 128)
            sec[to, :] = (xhat * s["gain"][1:2, :]).astype(BF16)

        loop(quarter // 128, norm_two)
        send_sec.append(wire.copy(sec.at[own(i, quarter)], sec.at[own(i, quarter)], at.core))
    pump()
    gather_up.finish()
    hid, dgelu = s["hid"], s["dgelu"]
    wup, wdown = s["wup"], s["wdown"]
    root_2_pi = float(np.sqrt(2.0 / np.pi).astype(np.float32))

    def expand(start):
        rows = pl.ds(start, tokens)

        def part(cols):
            v = mm(sec[rows, :], wup[:, :, :, :, cols].reshape(width, 256))
            vv = v * v
            t = jnp.tanh(v * (root_2_pi + (0.044715 * root_2_pi) * vv))
            a = 0.5 * t + 0.5
            out = v * a
            hid[rows, cols] = out.astype(BF16)
            slope = 2.0 * root_2_pi + (6.0 * 0.044715 * root_2_pi) * vv
            dgelu[rows, cols] = (a + out * (1.0 - a) * slope).astype(BF16)

        def body(j):
            for c in range(2):
                part(lane_cut(j * 512 + c * 256, 256))

        loop(ff_half // 512, body)
        pump()

    expand(own0)
    for made in send_sec:
        made.wait_recv()
    expand(other0)

    gdown = s["gdown"]

    def grad_down(zz):
        left = hid[:, 384 * zz : 384 * zz + 384]
        wide = mm_tn(left, gbl[...]).astype(BF16)
        for i in range(2):
            gdown[i][zz] = wide[:, i * half : (i + 1) * half].reshape(NY, NX, down_rows, half)

    for zz in range(NZ):
        grad_down(zz)
        if zz % 2:
            pump()
    reduce_down = [
        Reduce(wire, at, gdown[i], (half // 3, 2 * half // 3), *s["rdown"][i]) for i in range(2)
    ]
    for r in reduce_down:
        r.first()

    def back_hidden(step):
        gather_down.arrived(step)
        zz = gather_down.layer(step)
        weight = wdown[zz].reshape(NY * NX * down_rows, width)
        cols = lane_cut(zz * 384, 384)
        for start in (0, tokens):
            rows = slice(start, start + tokens)
            grad = mm_nt(gbl[rows, :], weight)
            dgelu[rows, cols] = (grad * dgelu[rows, cols].astype(F32)).astype(BF16)

    back_hidden(0)
    pump()
    back_hidden(1)
    pump()
    back_hidden(2)
    assert not todo
    back_hidden(3)

    def back_second(rows, to, store):
        store[to, :] = mm_nt(dgelu[rows, :], wup[...].reshape(width, ff_half))

    wire.sent(*arrive)
    arrive = send_parts(back_second, part_s, part_r)
    reduce_down[0].second()
    gsec = s["gfirst"]
    back_second(own(0, tokens), slice(0, tokens), gsec)
    gup = s["gup"]
    small = s["small"]
    small[...] = jnp.zeros_like(small)

    def grad_up(j, i):
        left = sec[:, 384 * j : 384 * j + 384]
        wide = mm_tn(left, dgelu[:, i * width : (i + 1) * width]).astype(BF16)
        gup[i][2 * j : 2 * j + 2] = wide.reshape(2, NY, NX, 2 * share, width)

    def norm_two_back(i):
        arrive[i].wait_recv()

        def body(j, total):
            rows = pl.ds(pl.multiple_of(i * quarter + j * 64, 64), 64)
            grad = gsec[rows, :] + part_r[rows, :]
            xhat, root = normalize_again(first[rows, :], s["kept_two"][rows, :])
            part = norm_back(xhat, root, s["gain"][1:2, :], grad)
            full = mix_last * cot_ref[rows, :].astype(F32) + part
            gsec[rows, :] = full
            to = pl.ds(pl.multiple_of(own0 + i * quarter + j * 64, 64), 64)
            gfl[to, :] = full.astype(BF16)
            return total + fold_rows(grad * xhat)

        total = lax.fori_loop(0, quarter // 64, body, jnp.zeros((8, width), F32))
        small[1:2, :] = small[1:2, :] + jnp.sum(total, axis=0, keepdims=True)
        return wire.copy(gfl.at[own(i, quarter)], gfl.at[own(i, quarter)], at.core)

    reduce_up = [
        Reduce(wire, at, gup[i], (width // 2, width), *s["rup"][i]) for i in range(2)
    ]

    def start_up(i):
        for j in range(2):
            grad_up(j, i)
        reduce_up[i].first()

    start_up(0)
    reduce_down[1].second()
    send_gfl = [norm_two_back(0), norm_two_back(1)]
    start_up(1)
    reduce_down[0].third()

    gm = s["gm"]

    def back_mixed(rows):
        gm[rows, :] = mm_nt(gfl[rows, :], output_weight()).astype(BF16)

    back_mixed(own(0, tokens))
    for made in send_gfl:
        made.wait_recv()
    back_mixed(other(0, tokens))
    go = s["go"]
    wide = mm_tn(s["mix"][...], gfl[...])
    left, right = wide[:, :half], wide[:, half:]
    blocks_o = (2, NY, NX, 2 * share, half)
    s["gox"][...] = jnp.where(k == 0, right, left).astype(BF16).reshape(blocks_o)
    swap_go = wire.copy(s["gox"], go.at[pl.ds(2 * k, 2)], at.core)
    go[pl.ds(2 * k, 2)] = jnp.where(k == 0, left, right).astype(BF16).reshape(blocks_o)
    reduce_o = Reduce(wire, at, go, (128, half), *s["ro"])

    lse, delta = s["lse"], s["delta"]
    wire.sent(send_gbl, *send_sec)
    heads_in = [(gbl, 0), (gbl, 384), (sec, 0)]
    gpair = s["gqkv"]
    grad_query = s["dq"]
    reduce_qkv = [
        Reduce(wire, at, gpair[p], (CUTS[p % 3], 384), *s["rqkv"][p]) for p in range(pairs)
    ]

    nothing = lambda: None
    todo.extend(
        [
            reduce_up[0].second,
            reduce_down[1].third,
            reduce_down[0].third_y,
            nothing,
            nothing,
            reduce_up[1].second,
            lambda: (swap_go.wait_recv(), reduce_o.first()),
            reduce_up[0].third,
            reduce_down[1].third_y,
            nothing,
            reduce_down[0].third_x,
            reduce_qkv[0].second,
            reduce_o.second,
            reduce_up[1].third,
            nothing,
            lambda: (reduce_qkv[0].third(), reduce_o.third()),
            lambda: (reduce_qkv[1].second(), reduce_down[1].third_x()),
            reduce_qkv[2].second,
            reduce_qkv[1].third,
            reduce_qkv[2].third,
        ]
    )

    def attend_back(p, b):
        cols = slice(128 * p, 128 * p + 128)
        r0 = b * BLOCK
        rows = slice(r0, r0 + BLOCK)
        after = slice(r0, length)
        count = length - r0
        here_k = lax.broadcasted_iota(jnp.int32, (BLOCK, count), 0)
        here_q = lax.broadcasted_iota(jnp.int32, (BLOCK, count), 1)
        allowed = (here_k <= here_q) & (
            (here_k + r0).astype(F32) >= s["start_row"][0:1, after]
        )
        key, value = ks[rows, cols], vs[rows, cols]
        query, grad = qs[after, cols], gm[after, cols]
        dk = jnp.zeros((BLOCK, 128), F32)
        dv = jnp.zeros((BLOCK, 128), F32)
        dq = jnp.zeros((count, 128), F32)
        for h in range(2):
            key_h = key * ones[h]
            scores = mm_nt(key_h, query)
            weights = jnp.exp(jnp.where(allowed, scores - lse[p, h : h + 1, after], MASKED))
            grad_w = mm_nt(value * ones[h], grad)
            grad_s = (weights * (grad_w - delta[p, h : h + 1, after])).astype(BF16)
            dv = dv + mm(weights.astype(BF16), grad * ones[h])
            dk = dk + mm(grad_s, query * ones[h])
            dq = dq + mm_tn(grad_s, key_h)
        gqkv, base = heads_in[p]
        gqkv[rows, base + 256 : base + 384] = dv.astype(BF16)
        gqkv[rows, base + 128 : base + 256] = turn(
            dk.astype(BF16).astype(F32), rows, -1.0
        ).astype(BF16)
        if b == 0:
            grad_query[...] = dq
        else:
            grad_query[after, :] = grad_query[after, :] + dq

    out_s, out_r = s["out_s"], s["out_r"]

    def contract(rows, to, store):
        store[to, :] = mm(hid[rows, :], wdown[...].reshape(ff_half, width))

    outb = gfl.at[pl.ds(0, tokens)]
    put_out = pltpu.make_async_copy(outb, out_ref, s["osem"].at[0])

    def write_output(arrive_out):
        wire.sent(*send_gfl)
        block_sum = jnp.zeros((8, width), F32)
        for i in range(2):
            rows = pl.ds(i * quarter, quarter)
            mine = mm(hid[own(i, quarter), :], wdown[...].reshape(ff_half, width))
            arrive_out[i].wait_recv()
            block = first[rows, :] + (mine + out_r[rows, :])
            outb[rows, :] = (s["acc"][rows, :] + mix_last * block).astype(BF16)
            block_sum = block_sum + fold_rows(block * cot_ref[rows, :].astype(F32))
        put_out.start()
        terms = jnp.zeros((1, width), F32)
        wide_lane = lax.broadcasted_iota(jnp.int32, (1, width), 1)
        for j in range(hist):
            terms = jnp.where(wide_lane == j, jnp.sum(s["mixacc"][j]), terms)
        small[2:3, :] = jnp.where(wide_lane == hist, jnp.sum(block_sum), terms)

    for p in range(pairs):
        cols = slice(128 * p, 128 * p + 128)

        def inner(i):
            rows = rows_of(i, BLOCK)
            both = jnp.transpose(s["mixf"][rows, cols] * gm[rows, cols].astype(F32))
            delta[p, 0:1, rows] = jnp.sum(both[:HD], axis=0, keepdims=True)
            delta[p, 1:2, rows] = jnp.sum(both[HD:], axis=0, keepdims=True)

        loop(blocks, inner)
        for b in range(blocks):
            attend_back(p, b)
            pump()

        gqkv, base = heads_in[p]

        def turn_query(i):
            rows = rows_of(i, BLOCK)
            low = (grad_query[rows, :] * HD**-0.5).astype(BF16).astype(F32)
            gqkv[rows, base : base + 128] = turn(low, rows, -1.0).astype(BF16)

        loop(blocks, turn_query)

        def grad_qkv(j):
            left = norm[:, pl.ds(pl.multiple_of(j * 384, 128), 384)]
            wide = mm_tn(left, gqkv[:, base : base + 384]).astype(BF16)
            gpair[p][pl.ds(2 * j, 2)] = wide.reshape(2, NY, NX, 2 * share, 384)

        loop(2, grad_qkv)
        reduce_qkv[p].first()
        pump()

    wire.sent(*arrive)

    def normed_grad(rows):
        weight = s["wqkv"][...].reshape(width, qkv_cols)
        return mm_nt(gbl[rows, :], weight[:, :768]) + mm_nt(sec[rows, :384], weight[:, 768:])

    def back_normed(rows, to, store):
        store[to, :] = normed_grad(rows)

    arrive = send_parts(back_normed, part_s, part_r)
    arrive_out = send_parts(contract, out_s, out_r)
    pump(2)
    write_output(arrive_out)
    own_s = first
    back_normed(own(0, tokens), slice(0, tokens), own_s)
    pump()
    total = jnp.zeros((8, width), F32)
    for i in range(2):
        arrive[i].wait_recv()

        def norm_one_back(j, total):
            rows = pl.ds(pl.multiple_of(i * quarter + j * 64, 64), 64)
            grad = own_s[rows, :] + part_r[rows, :]
            xhat, root = normalize_again(in_ref[rows, :].astype(F32), s["kept_one"][rows, :])
            gsec[rows, :] = gsec[rows, :] + norm_back(xhat, root, s["gain"][0:1, :], grad)
            return total + fold_rows(grad * xhat)

        total = lax.fori_loop(0, quarter // 64, norm_one_back, total)
        if i == 0:
            pump()
    put_gin = pltpu.make_async_copy(gsec, gin_ref, s["osem"].at[1])
    put_gin.start()
    small[0:1, :] = jnp.sum(total, axis=0, keepdims=True)

    sp, sz = s["small_p"], s["small_z"]
    sp[k, at.y, at.x] = small[...]
    mine = sp.at[k, at.y, at.x]
    step_p = [wire.copy(mine, mine, device) for device in at.block]
    pump()

    wire.sent(*swap)
    fin, fin_r = xs, xr
    def settle(reduce, c, size):
        total = reduce.result()
        fin[0, :, c : c + size] = total[:share]
        fin[1, :, c : c + size] = total[share:]
        return wire.copy(fin.at[o, :, pl.ds(c, size)], fin_r.at[:, pl.ds(c, size)], at.core)

    up0 = qkv_cols + half
    settled = [settle(reduce_up[i], up0 + i * width, width) for i in range(2)]
    settled.append(settle(reduce_o, qkv_cols, half))
    for i in range(2):
        c = i * half + 2 * half // 3
        s["fin_d"][:, i * half : c] = reduce_down[i].result()
        s["fin_d"][:, c : (i + 1) * half] = reduce_down[i].third_result()
    put_down = pltpu.make_async_copy(s["fin_d"], gdown_ref, s["osem"].at[2])
    put_down.start()
    settled.append(settle(reduce_qkv[0], 0, 384))
    for made in step_p:
        made.wait_recv()
    both = sp[0] + sp[1]
    sz[at.z] = (both[0, 0] + both[0, 1]) + (both[1, 0] + both[1, 1])
    step_z = [wire.copy(sz.at[at.z], sz.at[at.z], at.zn(step)) for step in range(1, NZ)]
    for p in range(1, pairs):
        settled.append(settle(reduce_qkv[p], 384 * p, 384))
    assert not todo
    put_mine = pltpu.make_async_copy(fin.at[k], pack_ref.at[k], s["osem"].at[3])
    put_mine.start()
    for made in settled:
        made.wait_recv()
    put_other = pltpu.make_async_copy(fin_r, pack_ref.at[o], s["osem"].at[4])
    put_other.start()
    for made in step_z:
        made.wait_recv()
    small[...] = ((sz[0] + sz[1]) + sz[2]) + sz[3]
    put_small = pltpu.make_async_copy(small, small_ref, s["osem"].at[5])
    put_small.start()
    for made in (put_down, put_mine, put_other, put_small):
        made.wait()
    put_out.wait()
    put_gin.wait()
    wire.close()


def finish(unit, *refs):
    mix_ref, cot_ref, small_ref, pack_ref, gdown_ref, out_ref, gin_ref = refs[:7]
    out_o, gin_o, ghist_o, gdown_o = refs[7:11]
    rest_o = refs[11:19]
    cot, small, pack, buffer, out, gin, gdown = refs[19:26]
    rest = refs[26:34]
    sems, hsems = refs[34:]
    hist = ghist_o.shape[0]
    tokens, width = cot.shape
    share = pack.shape[1]
    half = width // 2
    gets = [
        pltpu.make_async_copy(src, dst, sems.at[i])
        for i, (src, dst) in enumerate(
            (
                (cot_ref, cot),
                (pack_ref, pack),
                (small_ref, small),
                (out_ref, out),
                (gin_ref, gin),
                (gdown_ref, gdown),
            )
        )
    ]
    for made in gets:
        made.start()
    gets[0].wait()
    puts = []
    rows = 128
    for j in range(hist):

        def scale(i):
            part = rows_of(i, rows)
            buffer[j, part, :] = (mix_ref[j] * cot[part, :].astype(F32)).astype(BF16)

        loop(tokens // rows, scale)
        puts.append(pltpu.make_async_copy(buffer.at[j], ghist_o.at[j], hsems.at[j]))
        puts[j].start()
    for made in gets[1:]:
        made.wait()
    moves = [
        pltpu.make_async_copy(src, dst, sems.at[i])
        for i, (src, dst) in enumerate(((out, out_o), (gin, gin_o), (gdown, gdown_o)))
    ]
    for made in moves:
        made.start()
    gain1, gain2, mix, gq, gk, gv, go, gup = rest
    device = (lax.axis_index("batch") // unit) * 2 + lax.axis_index("seq")
    own = pltpu.roll(small[...], width - device * share, 1)
    gain1[...] = own[0:1, :share]
    gain2[...] = own[1:2, :share]
    mix[...] = small[2:3, : hist + 1]
    for h in range(2):
        for p in range(half // 128):
            for j, ref in enumerate((gq, gk, gv)):
                c = 384 * p + 128 * j
                ref[:, h * half + 128 * p : h * half + 128 * p + 128] = pack[h, :, c : c + 128]
        go[:, h * half : h * half + half] = pack[h, :, 3 * half : 4 * half]
    blk = gdown_o.shape[0]
    gup[...] = jnp.concatenate(
        [
            pack[h, :, 4 * half + blk * i : 4 * half + blk * i + blk]
            for i in range(GROUPS)
            for h in range(2)
        ],
        axis=1,
    )
    for i, (src, dst) in enumerate(zip(rest, rest_o)):
        puts.append(pltpu.make_async_copy(src, dst, sems.at[6 + i]))
        puts[-1].start()
    for made in puts + moves:
        made.wait()


def local(
    unit,
    inputs,
    history,
    segment_ids,
    cotangent,
    mix_weights,
    attn_gain,
    query_weight,
    key_weight,
    value_weight,
    output_weight,
    mlp_gain,
    up_weight,
    down_weight,
):
    rows, tokens, width = inputs.shape
    hist = history.shape[0]
    length = segment_ids.shape[1]
    half = width // 2
    ff_half = up_weight.shape[1] // 2
    share = width // (2 * GROUPS)
    both = 2 * share
    down_share = 2 * ff_half // (2 * GROUPS)
    pairs = half // 128
    seq = lax.axis_index("seq")
    batch = lax.axis_index("batch")
    group_device = (batch // unit) * 2 + seq
    weights = [query_weight, key_weight, value_weight, output_weight, up_weight, down_weight]
    gains = [attn_gain, mlp_gain]
    if unit > 1:
        def widen(value):
            whole = lax.all_gather(value, ("batch", "seq"), axis=0, tiled=True)
            size = value.shape[0] * unit
            return lax.dynamic_slice_in_dim(whole, group_device * size, size)

        weights = [widen(value) for value in weights]
        gains = [widen(value) for value in gains]
    sizes = []

    def scratch(name, shape, dtype=BF16):
        sizes.append((name, pltpu.VMEM(shape, dtype)))

    dims = (NZ, NY, NX)

    def reduction(rows_in, columns, a, b):
        rest = columns - b
        third = [
            pltpu.VMEM((NZ - 1, NY, NX, rows_in, rest), BF16),
            pltpu.VMEM((NX, rows_in, rest), BF16),
            pltpu.VMEM((rows_in, rest), BF16),
        ]
        return [
            pltpu.VMEM((NZ, NX, rows_in, a), BF16),
            pltpu.VMEM((NZ, NY, rows_in, b - a), BF16),
            pltpu.VMEM((NZ, rows_in, b), BF16),
            pltpu.VMEM((NZ - 1, rows_in, b), BF16),
        ] + (third if rest else [])

    sizes.append(("send", pltpu.SemaphoreType.DMA((SENDS,))))
    sizes.append(("recv", pltpu.SemaphoreType.DMA((COPIES,))))
    sizes.append(("hsem", pltpu.SemaphoreType.DMA((HBUF,))))
    sizes.append(("osem", pltpu.SemaphoreType.DMA((6,))))
    scratch("fin_d", (down_share, width), F32)
    sizes.append(("isem", pltpu.SemaphoreType.DMA((9,))))
    scratch("seg", (1, length), jnp.int32)
    scratch("in", (tokens, width))
    scratch("cot", (tokens, width))
    for i, value in enumerate(weights):
        scratch("w%d" % i, value.shape)
    scratch("hbuf", (HBUF, hist, 32, width))
    scratch("xs", (2, share, 2 * half + 2 * half + ff_half), F32)
    scratch("xr", (share, 2 * half + 2 * half + ff_half), F32)
    scratch("ga", (2,) + dims + (8, 128), F32)
    scratch("gain", (8, width), F32)
    scratch("wqkv", dims + (both, 3 * half))
    scratch("wo", dims + (both, half))
    scratch("wof", (2, NY, NX, both, width))
    scratch("wup", dims + (both, ff_half))
    scratch("wdown", dims + (down_share, width))
    for name in ("gbl", "norm", "sec", "gfl"):
        scratch(name, (length, width))
    scratch("kept_one", (tokens, 128), F32)
    scratch("kept_two", (tokens, 128), F32)
    scratch("start_row", (8, length), F32)
    scratch("start_col", (length, 128), F32)
    scratch("cos", (length, 128), F32)
    scratch("sin", (length, 128), F32)
    scratch("acc", (tokens, width), F32)
    scratch("mixacc", (hist, 8, 128), F32)
    for name in ("q", "kk", "v", "mix", "gm"):
        scratch(name, (length, half))
    scratch("mixf", (length, half), F32)
    scratch("lse", (pairs, 8, length), F32)
    scratch("delta", (pairs, 8, length), F32)
    scratch("dq", (length, 128), F32)
    for name in ("part_s", "part_r", "out_s", "out_r", "first", "gfirst"):
        scratch(name, (tokens, width), F32)
    scratch("hid", (length, ff_half))
    scratch("dgelu", (length, ff_half))
    scratch("gox", (2, NY, NX, both, half))
    scratch("small", (8, width), F32)
    scratch("small_p", (2, NY, NX, 8, width), F32)
    scratch("small_z", (NZ, 8, width), F32)
    sizes.append(("gdown", [pltpu.VMEM(dims + (down_share, half), BF16) for _ in range(2)]))
    sizes.append(("gup", [pltpu.VMEM(dims + (both, width), BF16) for _ in range(2)]))
    scratch("go", dims + (both, half))
    sizes.append(("gqkv", [pltpu.VMEM(dims + (both, 384), BF16) for _ in range(pairs)]))
    sizes.append(("rdown", [reduction(down_share, half, half // 3, 2 * half // 3) for _ in range(2)]))
    sizes.append(("rup", [reduction(both, width, width // 2, width) for _ in range(2)]))
    sizes.append(("ro", reduction(both, half, 128, half)))
    sizes.append(("rqkv", [reduction(both, 384, CUTS[p % 3], 384) for p in range(pairs)]))
    names = [name for name, _ in sizes]

    vmem = pl.BlockSpec(memory_space=pltpu.VMEM)
    anywhere = pl.BlockSpec(memory_space=pl.ANY)
    smem = pl.BlockSpec(memory_space=pltpu.SMEM)
    shape = jax.ShapeDtypeStruct
    outs = pl.pallas_call(
        functools.partial(layer, unit, names),
        out_shape=(
            shape((tokens, width), BF16),
            shape((tokens, width), F32),
            shape((2, share, 4 * half + ff_half), F32),
            shape((down_share, width), F32),
            shape((8, width), F32),
        ),
        in_specs=[smem, vmem, vmem] + [anywhere] * 10,
        out_specs=[anywhere] * 5,
        scratch_shapes=[size for _, size in sizes],
        compiler_params=pltpu.CompilerParams(
            collective_id=0, has_side_effects=True, vmem_limit_bytes=64 * 1024 * 1024 - 64 * 1024
        ),
    )(
        mix_weights,
        gains[0].reshape(1, share),
        gains[1].reshape(1, share),
        segment_ids,
        inputs.reshape(tokens, width),
        cotangent.reshape(tokens, width),
        *weights,
        history.reshape(hist, tokens, width),
    )
    partial_out, partial_gin, pack, gdown, small = outs
    rest = [
        shape((1, share), F32),
        shape((1, share), F32),
        shape((1, hist + 1), F32),
        shape((share, width), F32),
        shape((share, width), F32),
        shape((share, width), F32),
        shape((share, width), F32),
        shape((share, 2 * ff_half), F32),
    ]
    ends = pl.pallas_call(
        functools.partial(finish, unit),
        out_shape=[
            shape((tokens, width), BF16),
            shape((tokens, width), F32),
            shape((hist, tokens, width), BF16),
            shape((down_share, width), F32),
        ]
        + rest,
        in_specs=[smem] + [anywhere] * 6,
        out_specs=[anywhere] * 12,
        scratch_shapes=[
            pltpu.VMEM((tokens, width), BF16),
            pltpu.VMEM((8, width), F32),
            pltpu.VMEM((2, share, 4 * half + ff_half), F32),
            pltpu.VMEM((hist, tokens, width), BF16),
            pltpu.VMEM((tokens, width), BF16),
            pltpu.VMEM((tokens, width), F32),
            pltpu.VMEM((down_share, width), F32),
        ]
        + [pltpu.VMEM(one.shape, F32) for one in rest]
        + [pltpu.SemaphoreType.DMA((14,)), pltpu.SemaphoreType.DMA((hist,))],
        compiler_params=pltpu.CompilerParams(vmem_limit_bytes=64 * 1024 * 1024 - 64 * 1024),
    )(
        mix_weights,
        cotangent.reshape(tokens, width),
        small,
        pack,
        gdown,
        partial_out,
        partial_gin,
    )
    output, grad_inputs, grad_history, gdown, gain_one, gain_two, mix_grad = ends[:7]
    grads = list(ends[7:]) + [gdown, gain_one.reshape(share), gain_two.reshape(share)]
    mix_grad = mix_grad.reshape(hist + 1)
    if unit > 1:
        def narrow(value):
            whole = jnp.zeros((value.shape[0] * 2 * GROUPS,) + value.shape[1:], F32)
            whole = lax.dynamic_update_slice_in_dim(whole, value, group_device * value.shape[0], 0)
            return lax.psum_scatter(whole, ("batch", "seq"), scatter_dimension=0, tiled=True)

        grads = [narrow(value) for value in grads]
        mix_grad = lax.psum(mix_grad, ("batch", "seq")) / (2 * GROUPS)
    gq, gk, gv, go, gup, gdown, gain_one, gain_two = grads
    return (
        output.reshape(rows, tokens, width),
        grad_inputs.reshape(rows, tokens, width),
        grad_history.reshape(hist, rows, tokens, width),
        mix_grad,
        gain_one,
        gq,
        gk,
        gv,
        go,
        gain_two,
        gup,
        gdown,
    )


def solution(mesh):
    batch = mesh.shape["batch"]
    split = P(("batch", "seq"), None)
    gain = P(("batch", "seq"))
    placed = (
        P("batch", "seq", None),
        P(None, "batch", "seq", None),
        P("batch", None),
        P("batch", "seq", None),
        P(),
        gain,
        split,
        split,
        split,
        split,
        gain,
        split,
        split,
    )
    return jax.shard_map(
        functools.partial(local, batch // GROUPS),
        mesh=mesh,
        in_specs=placed,
        out_specs=(
            P("batch", "seq", None),
            P("batch", "seq", None),
            P(None, "batch", "seq", None),
            P(),
            gain,
            split,
            split,
            split,
            split,
            gain,
            split,
            split,
        ),
        check_vma=False,
    )
```

```python
import functools

import jax
import jax.numpy as jnp
import numpy as np
from jax import lax
from jax.experimental import pallas as pl
from jax.experimental.pallas import tpu as pltpu
from jax.sharding import PartitionSpec as P

HD = 64
EPSILON = 1e-05
MASKED = -1000000000.0
MESH = pl.DeviceIdType.MESH
F32 = jnp.float32
BF16 = jnp.bfloat16
NZ, NY, NX = 4, 2, 2
GROUPS = NZ * NY * NX
COPIES = 192
SENDS = 32
UP_CUTS = (5, 10)
CUTS = (256, 128, 256)
HBUF = 3
BLOCK = 256


def mm(a, b):
    return lax.dot_general(a, b, (((1,), (0,)), ((), ())), preferred_element_type=F32)


def mm_nt(a, b):
    return lax.dot_general(a, b, (((1,), (1,)), ((), ())), preferred_element_type=F32)


def mm_tn(a, b):
    return lax.dot_general(a, b, (((0,), (0,)), ((), ())), preferred_element_type=F32)


def loop(count, body):
    def step(i, carry):
        body(i)
        return carry

    lax.fori_loop(0, count, step, 0)


def rows_of(i, size):
    return pl.ds(pl.multiple_of(i * size, size), size)


def lane_cut(start, size):
    return pl.ds(pl.multiple_of(start, 128), size)


def normalize(value):
    mean = jnp.mean(value, axis=-1, keepdims=True)
    centred = value - mean
    variance = jnp.mean(centred * centred, axis=-1, keepdims=True)
    root = lax.rsqrt(variance + EPSILON)
    return centred * root, jnp.where(lax.broadcasted_iota(jnp.int32, (1, 128), 1) == 0, mean, root)


def normalize_again(value, kept):
    root = kept[:, 1:2]
    return (value - kept[:, 0:1]) * root, root


def norm_back(xhat, root, gain, grad):
    g = grad * gain
    return root * (
        g - jnp.mean(g, axis=-1, keepdims=True) - xhat * jnp.mean(g * xhat, axis=-1, keepdims=True)
    )


def fold_rows(value):
    total = value[0:8]
    for r in range(8, value.shape[0], 8):
        total = total + value[r : r + 8]
    return total


class Place:
    def __init__(self, unit):
        batch = lax.axis_index("batch")
        self.k = lax.axis_index("seq")
        self.o = 1 - self.k
        group = batch // unit
        self.unit = unit
        self.u = batch % unit
        self.z = group // (NY * NX)
        self.y = (group // NX) % NY
        self.x = group % NX
        self.core = (batch, self.o)
        self.xn = self.device(self.z, self.y, 1 - self.x)
        self.yn = self.device(self.z, 1 - self.y, self.x)
        self.diagonal = self.device(self.z, 1 - self.y, 1 - self.x)
        self.block = [self.xn, self.yn, self.diagonal, self.core] + [
            (batch_of, self.o) for batch_of, _ in (self.xn, self.yn, self.diagonal)
        ]

    def device(self, z, y, x):
        return (((z * NY + y) * NX + x) * self.unit + self.u, self.k)

    def across(self, step):
        if step == 0:
            return self.z
        if step == 2:
            return (self.z + 2) % NZ
        flip = self.z + 1 - 2 * (self.z % 2)
        return flip if step == 1 else (flip + 2) % NZ

    def zn(self, step):
        return self.device(self.across(step), self.y, self.x)


def guarded(condition, action):
    if condition is None:
        action()
    else:
        pl.when(condition)(action)


class Wire:
    def __init__(self, send, recv):
        self.send = send
        self.recv = recv
        self.open = []
        self.count = 0
        self.slots = 0

    def slot(self):
        self.slots += 1
        return self.slots - 1

    def copy(self, src, dst, device, condition=None, slot=None):
        i = self.count
        self.count += 1
        while self.open and self.open[0][0] <= i - SENDS:
            _, made, held = self.open.pop(0)
            guarded(held, made.wait_send)
        made = pltpu.make_async_remote_copy(
            src_ref=src,
            dst_ref=dst,
            send_sem=self.send.at[i % SENDS],
            recv_sem=self.recv.at[self.slot() if slot is None else slot],
            device_id=device,
            device_id_type=MESH,
        )
        guarded(condition, made.start)
        self.open.append((i, made, condition))
        return made

    def sent(self, *copies):
        for made in copies:
            if any(one is made for _, one, _ in self.open):
                made.wait_send()
                self.open = [entry for entry in self.open if entry[1] is not made]

    def close(self):
        for _, made, held in self.open:
            guarded(held, made.wait_send)


class Column:
    def __init__(self, wire, at, block, layer):
        self.wire, self.at, self.block, self.layer = wire, at, block, layer
        self.middle = (at.z == 1) | (at.z == 2)
        self.outer = (at.z == 0) | (at.z == 3)

    def start(self):
        at = self.at
        own = self.block(at.z)
        self.slots = {2: self.wire.slot(), 3: self.wire.slot()}
        self.made = {
            1: self.wire.copy(own, own, at.zn(1)),
            2: self.wire.copy(own, own, at.zn(3), self.middle, self.slots[2]),
            3: self.wire.copy(own, own, at.zn(2), self.outer, self.slots[3]),
        }

    def take(self, step):
        guarded(self.middle, self.made[step].wait_recv)
        part = self.block(self.layer(step))
        self.wire.copy(part, part, self.at.zn(1), self.middle, self.slots[step])

    def wait(self, step):
        guarded(self.outer if step > 1 else None, self.made[step].wait_recv)


class Gather:
    def __init__(self, wire, at, ref, a, b=None):
        self.wire, self.at, self.ref, self.a = wire, at, ref, a
        self.b = ref.shape[-1] if b is None else b
        self.third = self.b < ref.shape[-1]
        self.mid, self.last = {}, {}
        if self.third:
            self.z = Column(wire, at, lambda zz: ref.at[zz, at.y, at.x, :, : self.b], self.layer)
            self.cz = Column(wire, at, lambda zz: ref.at[zz, :, :, :, self.b :], self.layer)
        else:
            self.z = Column(wire, at, lambda zz: ref.at[zz, at.y, at.x], self.layer)

    def layer(self, step):
        z = self.at.z
        if step < 2:
            return self.at.across(step)
        return 2 - z // 2 if step == 2 else (NZ - 1) * (1 - z // 2)

    def pass_mid(self, *steps):
        at, ref = self.at, self.ref
        for step in steps:
            if step:
                self.z.wait(step)
            zz = self.layer(step)
            left = ref.at[zz, at.y, at.x, :, : self.a]
            right = ref.at[zz, at.y, at.x, :, self.a : self.b]
            self.mid[step] = (
                self.wire.copy(left, left, at.xn),
                self.wire.copy(right, right, at.yn),
            )

    def pass_last(self, step):
        at, ref = self.at, self.ref
        zz = self.layer(step)
        self.mid[step][0].wait_recv()
        left = ref.at[zz, at.y, :, :, : self.a]
        one = self.wire.copy(left, left, at.yn)
        self.mid[step][1].wait_recv()
        right = ref.at[zz, :, at.x, :, self.a : self.b]
        self.last[step] = (one, self.wire.copy(right, right, at.xn))

    def third_x(self):
        at = self.at
        part = self.ref.at[at.z, at.y, at.x, :, self.b :]
        self.cx = self.wire.copy(part, part, at.xn)

    def third_y(self):
        at = self.at
        self.cx.wait_recv()
        part = self.ref.at[at.z, at.y, :, :, self.b :]
        self.cy = self.wire.copy(part, part, at.yn)

    def third_z(self):
        self.cy.wait_recv()
        self.cz.start()

    def arrived(self, step):
        for made in self.last[step]:
            made.wait_recv()
        if self.third and step:
            self.cz.wait(step)

    def finish(self):
        for step in range(NZ):
            self.arrived(step)


class Reduce:
    def __init__(self, wire, at, grad, cuts, one_a, one_b, two, three, *third):
        self.wire, self.at, self.grad = wire, at, grad
        self.a, self.b = cuts
        self.one_a, self.one_b, self.two, self.three = one_a, one_b, two, three
        self.third_refs = third

    def add(self, index, more):
        self.grad[index] = (self.grad[index].astype(F32) + more.astype(F32)).astype(BF16)

    def first(self):
        at, grad, a, b = self.at, self.grad, self.a, self.b
        self.sa = self.wire.copy(grad.at[:, 1 - at.y, :, :, :a], self.one_a, at.yn)
        self.sb = self.wire.copy(grad.at[:, :, 1 - at.x, :, a:b], self.one_b, at.xn)
        if self.third_refs:
            self.cz = [
                self.wire.copy(
                    grad.at[at.across(step), :, :, :, b:], self.third_refs[0].at[step - 1], at.zn(step)
                )
                for step in range(1, NZ)
            ]

    def second(self):
        at, grad, a, b = self.at, self.grad, self.a, self.b
        left, right = slice(0, a), slice(a, b)

        def add_a(xx):
            loop(NZ, lambda zz: self.add((zz, at.y, xx, slice(None), left), self.one_a[zz, xx]))

        def add_b(yy):
            loop(NZ, lambda zz: self.add((zz, yy, at.x, slice(None), right), self.one_b[zz, yy]))

        self.sa.wait_recv()
        add_a(1 - at.x)
        self.saa = self.wire.copy(grad.at[:, at.y, 1 - at.x, :, :a], self.two.at[:, :, :a], at.xn)
        self.sb.wait_recv()
        add_b(1 - at.y)
        self.sbb = self.wire.copy(grad.at[:, 1 - at.y, at.x, :, a:b], self.two.at[:, :, a:], at.yn)
        add_a(at.x)
        add_b(at.y)

    def third(self):
        at, grad, b = self.at, self.grad, self.b
        self.saa.wait_recv()
        self.sbb.wait_recv()
        loop(NZ, lambda zz: self.add((zz, at.y, at.x, slice(None), slice(0, b)), self.two[zz]))
        self.sz = []
        for step in range(1, NZ):
            part = grad.at[at.across(step), at.y, at.x, :, :b]
            self.sz.append(self.wire.copy(part, self.three.at[step - 1], at.zn(step)))

    def third_y(self):
        at, grad, b = self.at, self.grad, self.b
        for made in self.cz:
            made.wait_recv()
        ref = self.third_refs[0]

        def body(yx):
            y, x = yx // NX, yx % NX
            more = ref[0, y, x].astype(F32) + ref[1, y, x].astype(F32) + ref[2, y, x].astype(F32)
            self.add((at.z, y, x, slice(None), slice(b, None)), more)

        loop(NY * NX, body)
        self.cy = self.wire.copy(grad.at[at.z, 1 - at.y, :, :, b:], self.third_refs[1], at.yn)

    def third_x(self):
        at, grad, b = self.at, self.grad, self.b
        self.cy.wait_recv()
        ref = self.third_refs[1]
        loop(NX, lambda x: self.add((at.z, at.y, x, slice(None), slice(b, None)), ref[x]))
        self.cx = self.wire.copy(grad.at[at.z, at.y, 1 - at.x, :, b:], self.third_refs[2], at.xn)

    def result(self):
        at, b = self.at, self.b
        total = self.grad[at.z, at.y, at.x, :, :b].astype(F32)
        for step in range(1, NZ):
            self.sz[step - 1].wait_recv()
            total = total + self.three[step - 1].astype(F32)
        return total

    def third_result(self):
        at = self.at
        self.cx.wait_recv()
        return self.grad[at.z, at.y, at.x, :, self.b :].astype(F32) + self.third_refs[2][
            ...
        ].astype(F32)


def layer(unit, names, *refs):
    (
        mix_ref, gain1_ref, gain2_ref, seg_any, in_any, cot_any,
        q_any, k_any, v_any, o_any, up_any, down_any, hist_ref,
        out_ref, gin_ref, pack_ref, gdown_ref, small_ref,
    ) = refs[:18]
    s = dict(zip(names, refs[18:]))
    seg_ref, in_ref, cot_ref = s["seg"], s["in"], s["cot"]
    q_ref, k_ref, v_ref, o_ref, up_ref, down_ref = (s[n] for n in ("w0", "w1", "w2", "w3", "w4", "w5"))
    tokens, width = in_ref.shape
    length = 2 * tokens
    half = width // 2
    ff_half = up_ref.shape[1] // 2
    pairs = half // 128
    share = q_ref.shape[0]
    down_rows = down_ref.shape[0]
    blocks = length // BLOCK
    hist = hist_ref.shape[0]
    at = Place(unit)
    k, o = at.k, at.o
    wire = Wire(s["send"], s["recv"])

    barrier = pltpu.get_barrier_semaphore()
    for device in (*at.block, at.zn(1), at.zn(2), at.zn(3)):
        pl.semaphore_signal(barrier, inc=1, device_id=device, device_id_type=MESH)
    gets = []
    for src, dst in (
        (q_any, q_ref), (k_any, k_ref), (v_any, v_ref), (o_any, o_ref), (up_any, up_ref),
        (down_any, down_ref), (seg_any, seg_ref), (in_any, in_ref), (cot_any, cot_ref),
    ):
        gets.append(pltpu.make_async_copy(src, dst, s["isem"].at[len(gets)]))
        gets[-1].start()
    hist_rows = s["hbuf"].shape[2]
    hist_chunks = tokens // hist_rows

    def fetch(i):
        return pltpu.make_async_copy(
            hist_ref.at[:, pl.ds(i * hist_rows, hist_rows)],
            s["hbuf"].at[i % HBUF],
            s["hsem"].at[i % HBUF],
        )

    for i in range(HBUF - 1):
        fetch(i).start()

    for made in gets[:3]:
        made.wait()

    xs, xr = s["xs"], s["xr"]
    qkv_cols = 3 * half
    blk = down_rows
    for h in range(2):
        c = h * half
        for i in range(pairs):
            for j, ref in enumerate((q_ref, k_ref, v_ref)):
                xs[h, :, 384 * i + 128 * j : 384 * i + 128 * j + 128] = ref[
                    :, c + 128 * i : c + 128 * i + 128
                ].astype(F32)
    ga = s["ga"]
    ga[k, at.z, at.y, at.x] = jnp.zeros((8, 128), F32)
    ga[k, at.z, at.y, at.x, 0:1, :share] = gain1_ref[...].astype(F32)
    ga[k, at.z, at.y, at.x, 1:2, :share] = gain2_ref[...].astype(F32)

    pl.semaphore_wait(barrier, 10)

    swap = [wire.copy(xs.at[o, :, :qkv_cols], xr.at[:, :qkv_cols], at.core)]
    gain_z = [
        wire.copy(ga.at[k, at.z, at.y, at.x], ga.at[k, at.z, at.y, at.x], at.zn(step))
        for step in range(1, NZ)
    ]
    for made in gets[3:6]:
        made.wait()
    s["wdown"][at.z, at.y, at.x] = down_ref[...]
    gather_down = Gather(wire, at, s["wdown"], width // 3, 2 * width // 3)
    gather_down.third_x()
    gather_down.pass_mid(0)
    wide = up_ref[...].astype(F32)
    for h in range(2):
        c = h * half
        xs[h, :, qkv_cols : qkv_cols + half] = o_ref[:, c : c + half].astype(F32)
        xs[h, :, qkv_cols + half :] = jnp.concatenate(
            [
                wide[:, 2 * blk * i + blk * h : 2 * blk * i + blk * h + blk]
                for i in range(GROUPS)
            ],
            axis=1,
        )
    swap.append(wire.copy(xs.at[o, :, qkv_cols:], xr.at[:, qkv_cols:], at.core))

    own0 = pl.multiple_of(k * tokens, tokens)
    other0 = pl.multiple_of(o * tokens, tokens)

    def own(i, size):
        return pl.ds(pl.multiple_of(own0 + i * size, size), size)

    def other(i, size):
        return pl.ds(pl.multiple_of(other0 + i * size, size), size)

    mix_last = mix_ref[hist]
    gbl, norm, sec, gfl = s["gbl"], s["norm"], s["sec"], s["gfl"]

    def own_block(cols):
        mine = xs[k, :, cols]
        theirs = xr[:, cols]
        upper = jnp.where(k == 0, mine, theirs)
        lower = jnp.where(k == 0, theirs, mine)
        return jnp.concatenate([upper, lower], axis=0).astype(BF16)

    gather_qkv = Gather(wire, at, s["wqkv"], 640)
    gather_o = Gather(wire, at, s["wo"], 128)
    gather_up = Gather(wire, at, s["wup"], UP_CUTS[0] * ff_half // 12, UP_CUTS[1] * ff_half // 12)
    swap[0].wait_recv()
    s["wqkv"][at.z, at.y, at.x] = own_block(slice(0, qkv_cols))
    gather_qkv.z.start()
    gather_qkv.pass_mid(0)
    swap[1].wait_recv()
    s["wo"][at.z, at.y, at.x] = own_block(slice(qkv_cols, qkv_cols + half))
    s["wup"][at.z, at.y, at.x] = own_block(slice(qkv_cols + half, qkv_cols + half + ff_half))
    gather_up.third_x()
    gather_up.pass_mid(0)
    todo = [
        lambda: (gather_qkv.pass_last(0), gather_o.z.start()),
        lambda: (
            gather_qkv.z.take(2),
            gather_qkv.pass_mid(1),
            gather_o.pass_mid(0),
            gather_up.pass_last(0),
            gather_up.z.start(),
        ),
        lambda: (
            gather_qkv.z.take(3),
            gather_qkv.pass_mid(2),
            gather_up.third_y(),
            gather_down.third_y(),
        ),
        lambda: (
            gather_qkv.pass_mid(3),
            gather_o.z.take(2),
            gather_o.z.take(3),
        ),
        lambda: (
            gather_qkv.pass_last(1),
            gather_qkv.pass_last(2),
            gather_up.z.take(2),
        ),
        lambda: (
            gather_qkv.pass_last(3),
            gather_up.z.take(3),
            gather_up.third_z(),
            gather_down.z.start(),
            gather_o.pass_last(0),
        ),
        lambda: (gather_up.pass_mid(1), gather_o.pass_mid(1, 2, 3)),
    ]
    later = [
        lambda: (gather_up.pass_mid(2, 3), gather_up.cz.take(2), gather_up.cz.take(3)),
        lambda: (gather_o.pass_last(1), gather_o.pass_last(2), gather_down.z.take(2)),
        lambda: (gather_o.pass_last(3), gather_up.pass_last(1), gather_down.z.take(3)),
        lambda: gather_down.third_z(),
        lambda: gather_up.pass_last(2),
        lambda: (gather_up.pass_last(3), gather_down.cz.take(2)),
        lambda: (gather_down.pass_mid(1, 2), gather_down.cz.take(3)),
        lambda: (gather_down.pass_last(0), gather_down.pass_mid(3)),
        lambda: gather_down.pass_last(1),
        lambda: gather_down.pass_last(2),
        lambda: gather_down.pass_last(3),
    ]

    def pump(count=1):
        for _ in range(count):
            if todo:
                todo.pop(0)()

    for made in gets[6:]:
        made.wait()
    seg = seg_ref[...].astype(F32)
    seg_col = jnp.transpose(jnp.broadcast_to(seg, (128, length)))
    start_row = jnp.zeros((1, length), F32)
    start_col = jnp.zeros((length, 128), F32)
    for d in range(7):
        count = jnp.sum(jnp.where(seg == d, 1.0, 0.0), axis=1, keepdims=True)
        start_row = start_row + jnp.where(seg > d, count, 0.0)
        start_col = start_col + jnp.where(seg_col > d, count, 0.0)
    s["start_row"][...] = jnp.broadcast_to(start_row, (8, length))
    s["start_col"][...] = start_col
    lane = lax.broadcasted_iota(jnp.int32, (1, 128), 1)
    first_half = (lane % HD) < (HD // 2)

    def rope_tables(i):
        rows = rows_of(i, 64)
        order = (lax.broadcasted_iota(jnp.int32, (64, 128), 0) + i * 64).astype(F32)
        angles = (order - s["start_col"][rows, :]) * freq
        s["cos"][rows, :] = jnp.cos(angles)
        sine = jnp.sin(angles)
        s["sin"][rows, :] = jnp.where(first_half, -sine, sine)

    freq = jnp.zeros((1, 128), F32)
    for i in range(HD // 2):
        rate = float(np.float32(10000.0 ** (-2.0 * i / HD)))
        freq = jnp.where(lane % (HD // 2) == i, rate, freq)
    loop(length // 64, rope_tables)
    for step in range(1, NZ):
        gain_z[step - 1].wait_recv()
    gain_x = wire.copy(ga.at[k, :, at.y, at.x], ga.at[k, :, at.y, at.x], at.xn)
    pump()

    def low_block(i):
        gbl[own(i, 32), :] = (mix_last * cot_ref[rows_of(i, 32), :].astype(F32)).astype(BF16)

    loop(tokens // 32, low_block)
    send_gbl = wire.copy(
        gbl.at[pl.ds(own0, tokens)], gbl.at[pl.ds(own0, tokens)], at.core
    )
    pump()

    def history_chunk(i):
        if i + HBUF - 1 < hist_chunks:
            fetch(i + HBUF - 1).start()
        fetch(i).wait()

        def group(r, sums):
            rows = rows_of(r, 16)
            whole = pl.ds(pl.multiple_of(i * hist_rows + r * 16, 16), 16)
            cot = cot_ref[whole, :].astype(F32)
            total = jnp.zeros((16, width), F32)
            out = []
            for j in range(hist):
                earlier = s["hbuf"][i % HBUF, j, rows, :].astype(F32)
                total = total + mix_ref[j] * earlier
                term = fold_rows(earlier * cot)
                part = sums[j]
                for c in range(0, width, 128):
                    part = part + term[:, c : c + 128]
                out.append(part)
            s["acc"][whole, :] = total
            return tuple(out)

        sums = lax.fori_loop(
            0, hist_rows // 16, group, tuple(s["mixacc"][j] for j in range(hist))
        )
        for j in range(hist):
            s["mixacc"][j] = sums[j]

    s["mixacc"][...] = jnp.zeros_like(s["mixacc"])
    history_chunk(0)
    history_chunk(1)
    gain_x.wait_recv()
    gain_y = wire.copy(ga.at[k, :, at.y], ga.at[k, :, at.y], at.yn)
    pump()
    history_chunk(2)
    history_chunk(3)
    pump()
    history_chunk(4)
    gain_y.wait_recv()
    gain_c = wire.copy(ga.at[k], ga.at[k], at.core)
    pump()
    gain_c.wait_recv()

    lanes = lax.broadcasted_iota(jnp.int32, (128, width), 1).astype(F32)
    rows_i = lax.broadcasted_iota(jnp.int32, (128, width), 0)
    owner = jnp.floor((lanes + 0.5) * (1.0 / share))
    spread = jnp.where(lanes - share * owner == rows_i.astype(F32), 1.0, 0.0).astype(BF16)
    gain_rows = [jnp.zeros((1, width), F32), jnp.zeros((1, width), F32)]
    for kk in range(2):
        tiles = ga[kk].reshape(GROUPS * 8, 128).astype(BF16)
        wide = mm(tiles, spread)
        for r in range(2):
            hit = ((rows_i % 8) == r) & (owner == (2 * (rows_i // 8) + kk).astype(F32))
            gain_rows[r] = gain_rows[r] + jnp.sum(
                jnp.where(hit, wide, 0.0), axis=0, keepdims=True
            )
    s["gain"][...] = jnp.concatenate([gain_rows[0], gain_rows[1], jnp.zeros((6, width), F32)], axis=0)

    def norm_one(i):
        xhat, s["kept_one"][rows_of(i, 128), :] = normalize(in_ref[rows_of(i, 128), :].astype(F32))
        norm[own(i, 128), :] = (xhat * s["gain"][0:1, :]).astype(BF16)

    loop(tokens // 128, norm_one)
    send_norm = wire.copy(norm.at[pl.ds(own0, tokens)], norm.at[pl.ds(own0, tokens)], at.core)
    pump()
    for i in range(5, hist_chunks):
        history_chunk(i)
        if i % 3 == 1:
            pump()
    while len(todo) > 0:
        pump()
    todo.extend(later)
    send_norm.wait_recv()
    send_gbl.wait_recv()
    gather_qkv.finish()

    qs, ks, vs = s["q"], s["kk"], s["v"]

    def turn(value, rows, sign):
        partner = jnp.where(first_half, pltpu.roll(value, 96, 1), pltpu.roll(value, 32, 1))
        return value * s["cos"][rows, :] + (sign * partner) * s["sin"][rows, :]

    def project(i):
        rows = rows_of(i, BLOCK)
        left = norm[rows, :]
        both_pairs = mm(left, s["wqkv"][:, :, :, :, :768].reshape(width, 768))
        for p in range(pairs):
            if p < 2:
                wide = both_pairs[:, 384 * p : 384 * p + 384]
            else:
                wide = mm(left, s["wqkv"][:, :, :, :, 768:].reshape(width, qkv_cols - 768))
            cols = slice(128 * p, 128 * p + 128)
            qs[rows, cols] = (turn(wide[:, :128], rows, 1.0).astype(BF16) * HD**-0.5).astype(BF16)
            ks[rows, cols] = turn(wide[:, 128:256], rows, 1.0).astype(BF16)
            vs[rows, cols] = wide[:, 256:].astype(BF16)

    for i in range(blocks):
        project(i)
        pump()

    lane_low = lane < HD
    ones = [
        jnp.where(lane_low, 1.0, 0.0).astype(BF16),
        jnp.where(lane_low, 0.0, 1.0).astype(BF16),
    ]

    def attend(p, b):
        cols = slice(128 * p, 128 * p + 128)
        r0 = b * tokens
        rows = slice(r0, r0 + tokens)
        here_q = lax.broadcasted_iota(jnp.int32, (tokens, tokens), 0)
        here_k = lax.broadcasted_iota(jnp.int32, (tokens, tokens), 1)
        start = s["start_col"][rows, 0:1]
        outs, tops = [], []
        for h in range(2):
            query = qs[rows, cols] * ones[h]
            near = mm_nt(query, ks[rows, cols])
            near = jnp.where(
                (here_k <= here_q) & ((here_k + r0).astype(F32) >= start), near, MASKED
            )
            top = jnp.max(near, axis=1, keepdims=True)
            if b:
                far = mm_nt(query, ks[0:r0, cols])
                far_k = lax.broadcasted_iota(jnp.int32, (1, r0), 1).astype(F32)
                far = jnp.where(far_k >= start, far, MASKED)
                top = jnp.maximum(top, jnp.max(far, axis=1, keepdims=True))
            raw = jnp.exp(near - top).astype(BF16)
            out = mm(raw, vs[rows, cols] * ones[h] + ones[1 - h])
            if b:
                raw = jnp.exp(far - top).astype(BF16)
                out = out + mm(raw, vs[0:r0, cols] * ones[h] + ones[1 - h])
            outs.append(out)
            tops.append(top)
        total = jnp.where(lane_low, pltpu.roll(outs[0], HD, 1), pltpu.roll(outs[1], HD, 1))
        mixed = jnp.where(lane_low, outs[0], outs[1]) / total
        s["mix"][rows, cols] = mixed.astype(BF16)
        s["mixf"][rows, cols] = mixed
        log_total = jnp.transpose(jnp.where(lane_low, tops[0], tops[1]) + jnp.log(total))
        s["lse"][p, 0:1, rows] = log_total[0:1]
        s["lse"][p, 1:2, rows] = log_total[HD : HD + 1]

    wo, wof = s["wo"], s["wof"]
    my_cols = lane_cut(k * half, half)
    for p in range(pairs):
        for b in range(2):
            attend(p, b)
        pump()
        if p == 1:
            gather_o.finish()
            swap_o = wire.copy(wo.at[pl.ds(2 * o, 2)], wof.at[:, :, :, :, my_cols], at.core)
            wof[:, :, :, :, my_cols] = wo[pl.ds(2 * k, 2)]

    swap_o.wait_recv()

    def output_weight():
        return wof[...].reshape(half, width)

    part_s, part_r = s["part_s"], s["part_r"]
    quarter = tokens // 2

    def send_parts(make, store, recv, pieces=1):
        made = []
        size = tokens // pieces
        for i in range(pieces):
            make(other(i, size), rows_of(i, size), store)
            for j in range(2 // pieces):
                to = pl.ds((i * (2 // pieces) + j) * quarter, quarter)
                made.append(wire.copy(store.at[to], recv.at[to], at.core))
        return made

    def attended(rows, to, store):
        store[to, :] = mm(s["mix"][rows, :], output_weight()).astype(store.dtype)

    arrive = send_parts(attended, gfl.at[pl.ds(0, tokens)], gfl.at[pl.ds(tokens, tokens)], 2)
    first = s["first"]
    for i in range(2):
        attended(own(i, quarter), rows_of(i, quarter), first)
    send_sec = []
    for i in range(2):
        arrive[i].wait_recv()

        def norm_two(j):
            rows = pl.ds(pl.multiple_of(i * quarter + j * 128, 128), 128)
            there = pl.ds(pl.multiple_of(tokens + i * quarter + j * 128, 128), 128)
            value = in_ref[rows, :].astype(F32) + (first[rows, :] + gfl[there, :].astype(F32))
            first[rows, :] = value
            xhat, s["kept_two"][rows, :] = normalize(value)
            to = pl.ds(pl.multiple_of(own0 + i * quarter + j * 128, 128), 128)
            sec[to, :] = (xhat * s["gain"][1:2, :]).astype(BF16)

        loop(quarter // 128, norm_two)
        send_sec.append(wire.copy(sec.at[own(i, quarter)], sec.at[own(i, quarter)], at.core))
    pump()
    gather_up.finish()
    hid, dgelu = s["hid"], s["dgelu"]
    wup, wdown = s["wup"], s["wdown"]
    root_2_pi = float(np.sqrt(2.0 / np.pi).astype(np.float32))

    def expand(start):
        rows = pl.ds(start, tokens)

        def part(cols):
            v = mm(sec[rows, :], wup[:, :, :, :, cols].reshape(width, 256))
            vv = v * v
            t = jnp.tanh(v * (root_2_pi + (0.044715 * root_2_pi) * vv))
            a = 0.5 * t + 0.5
            out = v * a
            hid[rows, cols] = out.astype(BF16)
            slope = 2.0 * root_2_pi + (6.0 * 0.044715 * root_2_pi) * vv
            dgelu[rows, cols] = (a + out * (1.0 - a) * slope).astype(BF16)

        def body(j):
            for c in range(3):
                part(lane_cut(j * 768 + c * 256, 256))

        loop(ff_half // 768, body)
        pump()

    expand(own0)
    for made in send_sec:
        made.wait_recv()
    expand(other0)

    gdown = s["gdown"]

    def grad_down(zz):
        left = hid[:, 384 * zz : 384 * zz + 384]
        wide = mm_tn(left, gbl[...]).astype(BF16)
        for i in range(2):
            gdown[i][zz] = wide[:, i * half : (i + 1) * half].reshape(NY, NX, down_rows, half)

    for zz in range(NZ):
        grad_down(zz)
        if zz % 2:
            pump()
    reduce_down = [
        Reduce(wire, at, gdown[i], (half // 3, 2 * half // 3), *s["rdown"][i]) for i in range(2)
    ]
    for r in reduce_down:
        r.first()

    def back_hidden(step):
        gather_down.arrived(step)
        zz = gather_down.layer(step)
        weight = wdown[zz].reshape(NY * NX * down_rows, width)
        cols = lane_cut(zz * 384, 384)
        for start in (0, tokens):
            rows = slice(start, start + tokens)
            grad = mm_nt(gbl[rows, :], weight)
            dgelu[rows, cols] = (grad * dgelu[rows, cols].astype(F32)).astype(BF16)

    back_hidden(0)
    pump()
    back_hidden(1)
    pump()
    back_hidden(2)
    assert not todo
    back_hidden(3)

    def back_second(rows, to, store):
        store[to, :] = mm_nt(dgelu[rows, :], wup[...].reshape(width, ff_half))

    wire.sent(*arrive)
    arrive = send_parts(back_second, part_s, part_r)
    reduce_down[0].second()
    gsec = s["gfirst"]
    back_second(own(0, tokens), slice(0, tokens), gsec)
    gup = s["gup"]
    small = s["small"]
    small[...] = jnp.zeros_like(small)

    def grad_up(j, i):
        left = sec[:, 384 * j : 384 * j + 384]
        wide = mm_tn(left, dgelu[:, i * width : (i + 1) * width]).astype(BF16)
        gup[i][2 * j : 2 * j + 2] = wide.reshape(2, NY, NX, 2 * share, width)

    def norm_two_back(i):
        arrive[i].wait_recv()

        def body(j, total):
            rows = pl.ds(pl.multiple_of(i * quarter + j * 64, 64), 64)
            grad = gsec[rows, :] + part_r[rows, :]
            xhat, root = normalize_again(first[rows, :], s["kept_two"][rows, :])
            part = norm_back(xhat, root, s["gain"][1:2, :], grad)
            full = mix_last * cot_ref[rows, :].astype(F32) + part
            gsec[rows, :] = full
            to = pl.ds(pl.multiple_of(own0 + i * quarter + j * 64, 64), 64)
            gfl[to, :] = full.astype(BF16)
            return total + fold_rows(grad * xhat)

        total = lax.fori_loop(0, quarter // 64, body, jnp.zeros((8, width), F32))
        small[1:2, :] = small[1:2, :] + jnp.sum(total, axis=0, keepdims=True)
        return wire.copy(gfl.at[own(i, quarter)], gfl.at[own(i, quarter)], at.core)

    reduce_up = [
        Reduce(wire, at, gup[i], (width // 2, width), *s["rup"][i]) for i in range(2)
    ]

    def start_up(i):
        for j in range(2):
            grad_up(j, i)
        reduce_up[i].first()

    start_up(0)
    reduce_down[1].second()
    send_gfl = [norm_two_back(0), norm_two_back(1)]
    start_up(1)
    reduce_down[0].third()

    gm = s["gm"]

    def back_mixed(rows):
        gm[rows, :] = mm_nt(gfl[rows, :], output_weight()).astype(BF16)

    back_mixed(own(0, tokens))
    for made in send_gfl:
        made.wait_recv()
    back_mixed(other(0, tokens))
    go = s["go"]
    wide = mm_tn(s["mix"][...], gfl[...])
    left, right = wide[:, :half], wide[:, half:]
    blocks_o = (2, NY, NX, 2 * share, half)
    s["gox"][...] = jnp.where(k == 0, right, left).astype(BF16).reshape(blocks_o)
    swap_go = wire.copy(s["gox"], go.at[pl.ds(2 * k, 2)], at.core)
    go[pl.ds(2 * k, 2)] = jnp.where(k == 0, left, right).astype(BF16).reshape(blocks_o)
    reduce_o = Reduce(wire, at, go, (128, half), *s["ro"])

    lse, delta = s["lse"], s["delta"]
    wire.sent(send_gbl, *send_sec)
    heads_in = [(gbl, 0), (gbl, 384), (sec, 0)]
    gpair = s["gqkv"]
    grad_query = s["dq"]
    reduce_qkv = [
        Reduce(wire, at, gpair[p], (CUTS[p % 3], 384), *s["rqkv"][p]) for p in range(pairs)
    ]

    nothing = lambda: None
    todo.extend(
        [
            reduce_up[0].second,
            reduce_down[1].third,
            reduce_down[0].third_y,
            nothing,
            nothing,
            reduce_up[1].second,
            lambda: (swap_go.wait_recv(), reduce_o.first()),
            reduce_down[1].third_y,
            reduce_up[0].third,
            nothing,
            reduce_down[0].third_x,
            reduce_qkv[0].second,
            reduce_up[1].third,
            reduce_o.second,
            nothing,
            lambda: (reduce_qkv[0].third(), reduce_o.third()),
            lambda: (reduce_qkv[1].second(), reduce_down[1].third_x()),
            reduce_qkv[2].second,
            reduce_qkv[1].third,
            reduce_qkv[2].third,
        ]
    )

    def attend_back(p, b):
        cols = slice(128 * p, 128 * p + 128)
        r0 = b * BLOCK
        rows = slice(r0, r0 + BLOCK)
        after = slice(r0, length)
        count = length - r0
        here_k = lax.broadcasted_iota(jnp.int32, (BLOCK, count), 0)
        here_q = lax.broadcasted_iota(jnp.int32, (BLOCK, count), 1)
        allowed = (here_k <= here_q) & (
            (here_k + r0).astype(F32) >= s["start_row"][0:1, after]
        )
        key, value = ks[rows, cols], vs[rows, cols]
        query, grad = qs[after, cols], gm[after, cols]
        dk = jnp.zeros((BLOCK, 128), F32)
        dv = jnp.zeros((BLOCK, 128), F32)
        dq = jnp.zeros((count, 128), F32)
        for h in range(2):
            key_h = key * ones[h]
            scores = mm_nt(key_h, query)
            weights = jnp.exp(jnp.where(allowed, scores - lse[p, h : h + 1, after], MASKED))
            grad_w = mm_nt(value * ones[h], grad)
            grad_s = (weights * (grad_w - delta[p, h : h + 1, after])).astype(BF16)
            dv = dv + mm(weights.astype(BF16), grad * ones[h])
            dk = dk + mm(grad_s, query * ones[h])
            dq = dq + mm_tn(grad_s, key_h)
        gqkv, base = heads_in[p]
        gqkv[rows, base + 256 : base + 384] = dv.astype(BF16)
        gqkv[rows, base + 128 : base + 256] = turn(
            dk.astype(BF16).astype(F32), rows, -1.0
        ).astype(BF16)
        if b == 0:
            grad_query[...] = dq
        else:
            grad_query[after, :] = grad_query[after, :] + dq

    out_s, out_r = s["out_s"], s["out_r"]

    def contract(rows, to, store):
        store[to, :] = mm(hid[rows, :], wdown[...].reshape(ff_half, width))

    outb = gfl.at[pl.ds(0, tokens)]
    put_out = pltpu.make_async_copy(outb, out_ref, s["osem"].at[0])

    def write_output(arrive_out):
        wire.sent(*send_gfl)
        mine = s["mixf"]
        for h in range(2):
            weight = wdown[...].reshape(ff_half, width)[:, h * half : h * half + half]
            mine[h * tokens : h * tokens + tokens, :] = mm(hid[own(0, tokens), :], weight)
        for made in arrive_out:
            made.wait_recv()

        def finish_out(j, total):
            rows = rows_of(j, 64)
            below = pl.ds(pl.multiple_of(tokens + j * 64, 64), 64)
            part = jnp.concatenate([mine[rows, :], mine[below, :]], axis=1)
            block = first[rows, :] + (part + out_r[rows, :])
            outb[rows, :] = (s["acc"][rows, :] + mix_last * block).astype(BF16)
            return total + fold_rows(block * cot_ref[rows, :].astype(F32))

        block_sum = lax.fori_loop(0, tokens // 64, finish_out, jnp.zeros((8, width), F32))
        put_out.start()
        terms = jnp.zeros((1, width), F32)
        wide_lane = lax.broadcasted_iota(jnp.int32, (1, width), 1)
        for j in range(hist):
            terms = jnp.where(wide_lane == j, jnp.sum(s["mixacc"][j]), terms)
        small[2:3, :] = jnp.where(wide_lane == hist, jnp.sum(block_sum), terms)

    for p in range(pairs):
        cols = slice(128 * p, 128 * p + 128)

        def inner(i):
            rows = rows_of(i, BLOCK)
            both = jnp.transpose(s["mixf"][rows, cols] * gm[rows, cols].astype(F32))
            delta[p, 0:1, rows] = jnp.sum(both[:HD], axis=0, keepdims=True)
            delta[p, 1:2, rows] = jnp.sum(both[HD:], axis=0, keepdims=True)

        loop(blocks, inner)
        for b in range(blocks):
            attend_back(p, b)
            pump()

        gqkv, base = heads_in[p]

        def turn_query(i):
            rows = rows_of(i, BLOCK)
            low = (grad_query[rows, :] * HD**-0.5).astype(BF16).astype(F32)
            gqkv[rows, base : base + 128] = turn(low, rows, -1.0).astype(BF16)

        loop(blocks, turn_query)

        def grad_qkv(j):
            left = norm[:, pl.ds(pl.multiple_of(j * 384, 128), 384)]
            wide = mm_tn(left, gqkv[:, base : base + 384]).astype(BF16)
            gpair[p][pl.ds(2 * j, 2)] = wide.reshape(2, NY, NX, 2 * share, 384)

        loop(2, grad_qkv)
        reduce_qkv[p].first()
        pump()

    wire.sent(*arrive)

    def normed_grad(rows):
        weight = s["wqkv"][...].reshape(width, qkv_cols)
        return mm_nt(gbl[rows, :], weight[:, :768]) + mm_nt(sec[rows, :384], weight[:, 768:])

    def back_normed(rows, to, store):
        store[to, :] = normed_grad(rows)

    arrive = send_parts(back_normed, part_s, part_r)
    arrive_out = send_parts(contract, out_s, out_r)
    pump(2)
    write_output(arrive_out)
    own_s = first
    back_normed(own(0, tokens), slice(0, tokens), own_s)
    pump()
    total = jnp.zeros((8, width), F32)
    for i in range(2):
        arrive[i].wait_recv()

        def norm_one_back(j, total):
            rows = pl.ds(pl.multiple_of(i * quarter + j * 64, 64), 64)
            grad = own_s[rows, :] + part_r[rows, :]
            xhat, root = normalize_again(in_ref[rows, :].astype(F32), s["kept_one"][rows, :])
            gsec[rows, :] = gsec[rows, :] + norm_back(xhat, root, s["gain"][0:1, :], grad)
            return total + fold_rows(grad * xhat)

        total = lax.fori_loop(0, quarter // 64, norm_one_back, total)
        if i == 0:
            pump()
    put_gin = pltpu.make_async_copy(gsec, gin_ref, s["osem"].at[1])
    put_gin.start()
    small[0:1, :] = jnp.sum(total, axis=0, keepdims=True)

    sp, sz = s["small_p"], s["small_z"]
    sp[k, at.y, at.x] = small[...]
    mine = sp.at[k, at.y, at.x]
    step_p = [wire.copy(mine, mine, device) for device in at.block]
    pump()

    wire.sent(*swap)
    fin, fin_r = xs, xr
    def settle(reduce, c, size):
        total = reduce.result()
        fin[0, :, c : c + size] = total[:share]
        fin[1, :, c : c + size] = total[share:]
        return wire.copy(fin.at[o, :, pl.ds(c, size)], fin_r.at[:, pl.ds(c, size)], at.core)

    up0 = qkv_cols + half
    settled = [settle(reduce_up[i], up0 + i * width, width) for i in range(2)]
    settled.append(settle(reduce_o, qkv_cols, half))
    for i in range(2):
        c = i * half + 2 * half // 3
        s["fin_d"][:, i * half : c] = reduce_down[i].result()
        s["fin_d"][:, c : (i + 1) * half] = reduce_down[i].third_result()
    put_down = pltpu.make_async_copy(s["fin_d"], gdown_ref, s["osem"].at[2])
    put_down.start()
    settled.append(settle(reduce_qkv[0], 0, 384))
    for made in step_p:
        made.wait_recv()
    both = sp[0] + sp[1]
    sz[at.z] = (both[0, 0] + both[0, 1]) + (both[1, 0] + both[1, 1])
    step_z = [wire.copy(sz.at[at.z], sz.at[at.z], at.zn(step)) for step in range(1, NZ)]
    for p in range(1, pairs):
        settled.append(settle(reduce_qkv[p], 384 * p, 384))
    assert not todo
    put_mine = pltpu.make_async_copy(fin.at[k], pack_ref.at[k], s["osem"].at[3])
    put_mine.start()
    for made in settled:
        made.wait_recv()
    put_other = pltpu.make_async_copy(fin_r, pack_ref.at[o], s["osem"].at[4])
    put_other.start()
    for made in step_z:
        made.wait_recv()
    small[...] = ((sz[0] + sz[1]) + sz[2]) + sz[3]
    put_small = pltpu.make_async_copy(small, small_ref, s["osem"].at[5])
    put_small.start()
    for made in (put_down, put_mine, put_other, put_small):
        made.wait()
    put_out.wait()
    put_gin.wait()
    wire.close()


def finish(unit, *refs):
    mix_ref, cot_ref, small_ref, pack_ref, gdown_ref, out_ref, gin_ref = refs[:7]
    out_o, gin_o, ghist_o, gdown_o = refs[7:11]
    rest_o = refs[11:19]
    cot, small, pack, buffer, out, gin, gdown = refs[19:26]
    rest = refs[26:34]
    sems, hsems = refs[34:]
    hist = ghist_o.shape[0]
    tokens, width = cot.shape
    share = pack.shape[1]
    half = width // 2
    gets = [
        pltpu.make_async_copy(src, dst, sems.at[i])
        for i, (src, dst) in enumerate(
            (
                (cot_ref, cot),
                (pack_ref, pack),
                (small_ref, small),
                (out_ref, out),
                (gin_ref, gin),
                (gdown_ref, gdown),
            )
        )
    ]
    for made in gets:
        made.start()
    gets[0].wait()
    puts = []
    rows = 128
    for j in range(hist):

        def scale(i):
            part = rows_of(i, rows)
            buffer[j, part, :] = (mix_ref[j] * cot[part, :].astype(F32)).astype(BF16)

        loop(tokens // rows, scale)
        puts.append(pltpu.make_async_copy(buffer.at[j], ghist_o.at[j], hsems.at[j]))
        puts[j].start()
    for made in gets[1:]:
        made.wait()
    moves = [
        pltpu.make_async_copy(src, dst, sems.at[i])
        for i, (src, dst) in enumerate(((out, out_o), (gin, gin_o), (gdown, gdown_o)))
    ]
    for made in moves:
        made.start()
    gain1, gain2, mix, gq, gk, gv, go, gup = rest
    device = (lax.axis_index("batch") // unit) * 2 + lax.axis_index("seq")
    own = pltpu.roll(small[...], width - device * share, 1)
    gain1[...] = own[0:1, :share]
    gain2[...] = own[1:2, :share]
    mix[...] = small[2:3, : hist + 1]
    for h in range(2):
        for p in range(half // 128):
            for j, ref in enumerate((gq, gk, gv)):
                c = 384 * p + 128 * j
                ref[:, h * half + 128 * p : h * half + 128 * p + 128] = pack[h, :, c : c + 128]
        go[:, h * half : h * half + half] = pack[h, :, 3 * half : 4 * half]
    blk = gdown_o.shape[0]
    gup[...] = jnp.concatenate(
        [
            pack[h, :, 4 * half + blk * i : 4 * half + blk * i + blk]
            for i in range(GROUPS)
            for h in range(2)
        ],
        axis=1,
    )
    for i, (src, dst) in enumerate(zip(rest, rest_o)):
        puts.append(pltpu.make_async_copy(src, dst, sems.at[6 + i]))
        puts[-1].start()
    for made in puts + moves:
        made.wait()


def local(
    unit,
    inputs,
    history,
    segment_ids,
    cotangent,
    mix_weights,
    attn_gain,
    query_weight,
    key_weight,
    value_weight,
    output_weight,
    mlp_gain,
    up_weight,
    down_weight,
):
    rows, tokens, width = inputs.shape
    hist = history.shape[0]
    length = segment_ids.shape[1]
    half = width // 2
    ff_half = up_weight.shape[1] // 2
    share = width // (2 * GROUPS)
    both = 2 * share
    down_share = 2 * ff_half // (2 * GROUPS)
    pairs = half // 128
    seq = lax.axis_index("seq")
    batch = lax.axis_index("batch")
    group_device = (batch // unit) * 2 + seq
    weights = [query_weight, key_weight, value_weight, output_weight, up_weight, down_weight]
    gains = [attn_gain, mlp_gain]
    if unit > 1:
        def widen(value):
            whole = lax.all_gather(value, ("batch", "seq"), axis=0, tiled=True)
            size = value.shape[0] * unit
            return lax.dynamic_slice_in_dim(whole, group_device * size, size)

        weights = [widen(value) for value in weights]
        gains = [widen(value) for value in gains]
    sizes = []

    def scratch(name, shape, dtype=BF16):
        sizes.append((name, pltpu.VMEM(shape, dtype)))

    dims = (NZ, NY, NX)

    def reduction(rows_in, columns, a, b):
        rest = columns - b
        third = [
            pltpu.VMEM((NZ - 1, NY, NX, rows_in, rest), BF16),
            pltpu.VMEM((NX, rows_in, rest), BF16),
            pltpu.VMEM((rows_in, rest), BF16),
        ]
        return [
            pltpu.VMEM((NZ, NX, rows_in, a), BF16),
            pltpu.VMEM((NZ, NY, rows_in, b - a), BF16),
            pltpu.VMEM((NZ, rows_in, b), BF16),
            pltpu.VMEM((NZ - 1, rows_in, b), BF16),
        ] + (third if rest else [])

    sizes.append(("send", pltpu.SemaphoreType.DMA((SENDS,))))
    sizes.append(("recv", pltpu.SemaphoreType.DMA((COPIES,))))
    sizes.append(("hsem", pltpu.SemaphoreType.DMA((HBUF,))))
    sizes.append(("osem", pltpu.SemaphoreType.DMA((6,))))
    scratch("fin_d", (down_share, width), F32)
    sizes.append(("isem", pltpu.SemaphoreType.DMA((9,))))
    scratch("seg", (1, length), jnp.int32)
    scratch("in", (tokens, width))
    scratch("cot", (tokens, width))
    for i, value in enumerate(weights):
        scratch("w%d" % i, value.shape)
    scratch("hbuf", (HBUF, hist, 32, width))
    scratch("xs", (2, share, 2 * half + 2 * half + ff_half), F32)
    scratch("xr", (share, 2 * half + 2 * half + ff_half), F32)
    scratch("ga", (2,) + dims + (8, 128), F32)
    scratch("gain", (8, width), F32)
    scratch("wqkv", dims + (both, 3 * half))
    scratch("wo", dims + (both, half))
    scratch("wof", (2, NY, NX, both, width))
    scratch("wup", dims + (both, ff_half))
    scratch("wdown", dims + (down_share, width))
    for name in ("gbl", "norm", "sec", "gfl"):
        scratch(name, (length, width))
    scratch("kept_one", (tokens, 128), F32)
    scratch("kept_two", (tokens, 128), F32)
    scratch("start_row", (8, length), F32)
    scratch("start_col", (length, 128), F32)
    scratch("cos", (length, 128), F32)
    scratch("sin", (length, 128), F32)
    scratch("acc", (tokens, width), F32)
    scratch("mixacc", (hist, 8, 128), F32)
    for name in ("q", "kk", "v", "mix", "gm"):
        scratch(name, (length, half))
    scratch("mixf", (length, half), F32)
    scratch("lse", (pairs, 8, length), F32)
    scratch("delta", (pairs, 8, length), F32)
    scratch("dq", (length, 128), F32)
    for name in ("part_s", "part_r", "out_s", "out_r", "first", "gfirst"):
        scratch(name, (tokens, width), F32)
    scratch("hid", (length, ff_half))
    scratch("dgelu", (length, ff_half))
    scratch("gox", (2, NY, NX, both, half))
    scratch("small", (8, width), F32)
    scratch("small_p", (2, NY, NX, 8, width), F32)
    scratch("small_z", (NZ, 8, width), F32)
    sizes.append(("gdown", [pltpu.VMEM(dims + (down_share, half), BF16) for _ in range(2)]))
    sizes.append(("gup", [pltpu.VMEM(dims + (both, width), BF16) for _ in range(2)]))
    scratch("go", dims + (both, half))
    sizes.append(("gqkv", [pltpu.VMEM(dims + (both, 384), BF16) for _ in range(pairs)]))
    sizes.append(("rdown", [reduction(down_share, half, half // 3, 2 * half // 3) for _ in range(2)]))
    sizes.append(("rup", [reduction(both, width, width // 2, width) for _ in range(2)]))
    sizes.append(("ro", reduction(both, half, 128, half)))
    sizes.append(("rqkv", [reduction(both, 384, CUTS[p % 3], 384) for p in range(pairs)]))
    names = [name for name, _ in sizes]

    vmem = pl.BlockSpec(memory_space=pltpu.VMEM)
    anywhere = pl.BlockSpec(memory_space=pl.ANY)
    smem = pl.BlockSpec(memory_space=pltpu.SMEM)
    shape = jax.ShapeDtypeStruct
    outs = pl.pallas_call(
        functools.partial(layer, unit, names),
        out_shape=(
            shape((tokens, width), BF16),
            shape((tokens, width), F32),
            shape((2, share, 4 * half + ff_half), F32),
            shape((down_share, width), F32),
            shape((8, width), F32),
        ),
        in_specs=[smem, vmem, vmem] + [anywhere] * 10,
        out_specs=[anywhere] * 5,
        scratch_shapes=[size for _, size in sizes],
        compiler_params=pltpu.CompilerParams(
            collective_id=0, has_side_effects=True, vmem_limit_bytes=64 * 1024 * 1024 - 64 * 1024
        ),
    )(
        mix_weights,
        gains[0].reshape(1, share),
        gains[1].reshape(1, share),
        segment_ids,
        inputs.reshape(tokens, width),
        cotangent.reshape(tokens, width),
        *weights,
        history.reshape(hist, tokens, width),
    )
    partial_out, partial_gin, pack, gdown, small = outs
    rest = [
        shape((1, share), F32),
        shape((1, share), F32),
        shape((1, hist + 1), F32),
        shape((share, width), F32),
        shape((share, width), F32),
        shape((share, width), F32),
        shape((share, width), F32),
        shape((share, 2 * ff_half), F32),
    ]
    ends = pl.pallas_call(
        functools.partial(finish, unit),
        out_shape=[
            shape((tokens, width), BF16),
            shape((tokens, width), F32),
            shape((hist, tokens, width), BF16),
            shape((down_share, width), F32),
        ]
        + rest,
        in_specs=[smem] + [anywhere] * 6,
        out_specs=[anywhere] * 12,
        scratch_shapes=[
            pltpu.VMEM((tokens, width), BF16),
            pltpu.VMEM((8, width), F32),
            pltpu.VMEM((2, share, 4 * half + ff_half), F32),
            pltpu.VMEM((hist, tokens, width), BF16),
            pltpu.VMEM((tokens, width), BF16),
            pltpu.VMEM((tokens, width), F32),
            pltpu.VMEM((down_share, width), F32),
        ]
        + [pltpu.VMEM(one.shape, F32) for one in rest]
        + [pltpu.SemaphoreType.DMA((14,)), pltpu.SemaphoreType.DMA((hist,))],
        compiler_params=pltpu.CompilerParams(vmem_limit_bytes=64 * 1024 * 1024 - 64 * 1024),
    )(
        mix_weights,
        cotangent.reshape(tokens, width),
        small,
        pack,
        gdown,
        partial_out,
        partial_gin,
    )
    output, grad_inputs, grad_history, gdown, gain_one, gain_two, mix_grad = ends[:7]
    grads = list(ends[7:]) + [gdown, gain_one.reshape(share), gain_two.reshape(share)]
    mix_grad = mix_grad.reshape(hist + 1)
    if unit > 1:
        def narrow(value):
            whole = jnp.zeros((value.shape[0] * 2 * GROUPS,) + value.shape[1:], F32)
            whole = lax.dynamic_update_slice_in_dim(whole, value, group_device * value.shape[0], 0)
            return lax.psum_scatter(whole, ("batch", "seq"), scatter_dimension=0, tiled=True)

        grads = [narrow(value) for value in grads]
        mix_grad = lax.psum(mix_grad, ("batch", "seq")) / (2 * GROUPS)
    gq, gk, gv, go, gup, gdown, gain_one, gain_two = grads
    return (
        output.reshape(rows, tokens, width),
        grad_inputs.reshape(rows, tokens, width),
        grad_history.reshape(hist, rows, tokens, width),
        mix_grad,
        gain_one,
        gq,
        gk,
        gv,
        go,
        gain_two,
        gup,
        gdown,
    )


def solution(mesh):
    batch = mesh.shape["batch"]
    split = P(("batch", "seq"), None)
    gain = P(("batch", "seq"))
    placed = (
        P("batch", "seq", None),
        P(None, "batch", "seq", None),
        P("batch", None),
        P("batch", "seq", None),
        P(),
        gain,
        split,
        split,
        split,
        split,
        gain,
        split,
        split,
    )
    return jax.shard_map(
        functools.partial(local, batch // GROUPS),
        mesh=mesh,
        in_specs=placed,
        out_specs=(
            P("batch", "seq", None),
            P("batch", "seq", None),
            P(None, "batch", "seq", None),
            P(),
            gain,
            split,
            split,
            split,
            split,
            gain,
            split,
            split,
        ),
        check_vma=False,
    )
```

```python
import functools

import jax
import jax.numpy as jnp
import numpy as np
from jax import lax
from jax.experimental import pallas as pl
from jax.experimental.pallas import tpu as pltpu
from jax.sharding import PartitionSpec as P

HD = 64
EPSILON = 1e-05
MASKED = -1000000000.0
MESH = pl.DeviceIdType.MESH
F32 = jnp.float32
BF16 = jnp.bfloat16
NZ, NY, NX = 4, 2, 2
GROUPS = NZ * NY * NX
COPIES = 192
SENDS = 32
UP_CUTS = (5, 10)
CUTS = (256, 128, 256)
HBUF = 3
BLOCK = 256


def mm(a, b):
    return lax.dot_general(a, b, (((1,), (0,)), ((), ())), preferred_element_type=F32)


def mm_nt(a, b):
    return lax.dot_general(a, b, (((1,), (1,)), ((), ())), preferred_element_type=F32)


def mm_tn(a, b):
    return lax.dot_general(a, b, (((0,), (0,)), ((), ())), preferred_element_type=F32)


def loop(count, body):
    def step(i, carry):
        body(i)
        return carry

    lax.fori_loop(0, count, step, 0)


def rows_of(i, size):
    return pl.ds(pl.multiple_of(i * size, size), size)


def lane_cut(start, size):
    return pl.ds(pl.multiple_of(start, 128), size)


def normalize(value):
    mean = jnp.mean(value, axis=-1, keepdims=True)
    centred = value - mean
    variance = jnp.mean(centred * centred, axis=-1, keepdims=True)
    root = lax.rsqrt(variance + EPSILON)
    return centred * root, jnp.where(lax.broadcasted_iota(jnp.int32, (1, 128), 1) == 0, mean, root)


def normalize_again(value, kept):
    root = kept[:, 1:2]
    return (value - kept[:, 0:1]) * root, root


def norm_back(xhat, root, gain, grad):
    g = grad * gain
    return root * (
        g - jnp.mean(g, axis=-1, keepdims=True) - xhat * jnp.mean(g * xhat, axis=-1, keepdims=True)
    )


def fold_rows(value):
    total = value[0:8]
    for r in range(8, value.shape[0], 8):
        total = total + value[r : r + 8]
    return total


class Place:
    def __init__(self, unit):
        batch = lax.axis_index("batch")
        self.k = lax.axis_index("seq")
        self.o = 1 - self.k
        group = batch // unit
        self.unit = unit
        self.u = batch % unit
        self.z = group // (NY * NX)
        self.y = (group // NX) % NY
        self.x = group % NX
        self.core = (batch, self.o)
        self.xn = self.device(self.z, self.y, 1 - self.x)
        self.yn = self.device(self.z, 1 - self.y, self.x)
        self.diagonal = self.device(self.z, 1 - self.y, 1 - self.x)
        self.block = [self.xn, self.yn, self.diagonal, self.core] + [
            (batch_of, self.o) for batch_of, _ in (self.xn, self.yn, self.diagonal)
        ]

    def device(self, z, y, x):
        return (((z * NY + y) * NX + x) * self.unit + self.u, self.k)

    def across(self, step):
        if step == 0:
            return self.z
        if step == 2:
            return (self.z + 2) % NZ
        flip = self.z + 1 - 2 * (self.z % 2)
        return flip if step == 1 else (flip + 2) % NZ

    def zn(self, step):
        return self.device(self.across(step), self.y, self.x)


def guarded(condition, action):
    if condition is None:
        action()
    else:
        pl.when(condition)(action)


class Wire:
    def __init__(self, send, recv):
        self.send = send
        self.recv = recv
        self.open = []
        self.count = 0
        self.slots = 0

    def slot(self):
        self.slots += 1
        return self.slots - 1

    def copy(self, src, dst, device, condition=None, slot=None):
        i = self.count
        self.count += 1
        while self.open and self.open[0][0] <= i - SENDS:
            _, made, held = self.open.pop(0)
            guarded(held, made.wait_send)
        made = pltpu.make_async_remote_copy(
            src_ref=src,
            dst_ref=dst,
            send_sem=self.send.at[i % SENDS],
            recv_sem=self.recv.at[self.slot() if slot is None else slot],
            device_id=device,
            device_id_type=MESH,
        )
        guarded(condition, made.start)
        self.open.append((i, made, condition))
        return made

    def sent(self, *copies):
        for made in copies:
            if any(one is made for _, one, _ in self.open):
                made.wait_send()
                self.open = [entry for entry in self.open if entry[1] is not made]

    def close(self):
        for _, made, held in self.open:
            guarded(held, made.wait_send)


class Column:
    def __init__(self, wire, at, block, layer):
        self.wire, self.at, self.block, self.layer = wire, at, block, layer
        self.middle = (at.z == 1) | (at.z == 2)
        self.outer = (at.z == 0) | (at.z == 3)

    def start(self):
        at = self.at
        own = self.block(at.z)
        self.slots = {2: self.wire.slot(), 3: self.wire.slot()}
        self.made = {
            1: self.wire.copy(own, own, at.zn(1)),
            2: self.wire.copy(own, own, at.zn(3), self.middle, self.slots[2]),
            3: self.wire.copy(own, own, at.zn(2), self.outer, self.slots[3]),
        }

    def take(self, step):
        guarded(self.middle, self.made[step].wait_recv)
        part = self.block(self.layer(step))
        self.wire.copy(part, part, self.at.zn(1), self.middle, self.slots[step])

    def wait(self, step):
        guarded(self.outer if step > 1 else None, self.made[step].wait_recv)


class Gather:
    def __init__(self, wire, at, ref, a, b=None):
        self.wire, self.at, self.ref, self.a = wire, at, ref, a
        self.b = ref.shape[-1] if b is None else b
        self.third = self.b < ref.shape[-1]
        self.mid, self.last = {}, {}
        if self.third:
            self.z = Column(wire, at, lambda zz: ref.at[zz, at.y, at.x, :, : self.b], self.layer)
            self.cz = Column(wire, at, lambda zz: ref.at[zz, :, :, :, self.b :], self.layer)
        else:
            self.z = Column(wire, at, lambda zz: ref.at[zz, at.y, at.x], self.layer)

    def layer(self, step):
        z = self.at.z
        if step < 2:
            return self.at.across(step)
        return 2 - z // 2 if step == 2 else (NZ - 1) * (1 - z // 2)

    def pass_mid(self, *steps):
        at, ref = self.at, self.ref
        for step in steps:
            if step:
                self.z.wait(step)
            zz = self.layer(step)
            left = ref.at[zz, at.y, at.x, :, : self.a]
            right = ref.at[zz, at.y, at.x, :, self.a : self.b]
            self.mid[step] = (
                self.wire.copy(left, left, at.xn),
                self.wire.copy(right, right, at.yn),
            )

    def pass_last(self, step):
        at, ref = self.at, self.ref
        zz = self.layer(step)
        self.mid[step][0].wait_recv()
        left = ref.at[zz, at.y, :, :, : self.a]
        one = self.wire.copy(left, left, at.yn)
        self.mid[step][1].wait_recv()
        right = ref.at[zz, :, at.x, :, self.a : self.b]
        self.last[step] = (one, self.wire.copy(right, right, at.xn))

    def third_x(self):
        at = self.at
        part = self.ref.at[at.z, at.y, at.x, :, self.b :]
        self.cx = self.wire.copy(part, part, at.xn)

    def third_y(self):
        at = self.at
        self.cx.wait_recv()
        part = self.ref.at[at.z, at.y, :, :, self.b :]
        self.cy = self.wire.copy(part, part, at.yn)

    def third_z(self):
        self.cy.wait_recv()
        self.cz.start()

    def arrived(self, step):
        for made in self.last[step]:
            made.wait_recv()
        if self.third and step:
            self.cz.wait(step)

    def finish(self):
        for step in range(NZ):
            self.arrived(step)


class Reduce:
    def __init__(self, wire, at, grad, cuts, one_a, one_b, two, three, *third):
        self.wire, self.at, self.grad = wire, at, grad
        self.a, self.b = cuts
        self.one_a, self.one_b, self.two, self.three = one_a, one_b, two, three
        self.third_refs = third

    def add(self, index, more):
        self.grad[index] = (self.grad[index].astype(F32) + more.astype(F32)).astype(BF16)

    def first(self):
        at, grad, a, b = self.at, self.grad, self.a, self.b
        self.sa = self.wire.copy(grad.at[:, 1 - at.y, :, :, :a], self.one_a, at.yn)
        self.sb = self.wire.copy(grad.at[:, :, 1 - at.x, :, a:b], self.one_b, at.xn)
        if self.third_refs:
            self.cz = [
                self.wire.copy(
                    grad.at[at.across(step), :, :, :, b:], self.third_refs[0].at[step - 1], at.zn(step)
                )
                for step in range(1, NZ)
            ]

    def second(self):
        at, grad, a, b = self.at, self.grad, self.a, self.b
        left, right = slice(0, a), slice(a, b)

        def add_a(xx):
            loop(NZ, lambda zz: self.add((zz, at.y, xx, slice(None), left), self.one_a[zz, xx]))

        def add_b(yy):
            loop(NZ, lambda zz: self.add((zz, yy, at.x, slice(None), right), self.one_b[zz, yy]))

        self.sa.wait_recv()
        add_a(1 - at.x)
        self.saa = self.wire.copy(grad.at[:, at.y, 1 - at.x, :, :a], self.two.at[:, :, :a], at.xn)
        self.sb.wait_recv()
        add_b(1 - at.y)
        self.sbb = self.wire.copy(grad.at[:, 1 - at.y, at.x, :, a:b], self.two.at[:, :, a:], at.yn)
        add_a(at.x)
        add_b(at.y)

    def third(self):
        at, grad, b = self.at, self.grad, self.b
        self.saa.wait_recv()
        self.sbb.wait_recv()
        loop(NZ, lambda zz: self.add((zz, at.y, at.x, slice(None), slice(0, b)), self.two[zz]))
        self.sz = []
        for step in range(1, NZ):
            part = grad.at[at.across(step), at.y, at.x, :, :b]
            self.sz.append(self.wire.copy(part, self.three.at[step - 1], at.zn(step)))

    def third_y(self):
        at, grad, b = self.at, self.grad, self.b
        for made in self.cz:
            made.wait_recv()
        ref = self.third_refs[0]

        def body(yx):
            y, x = yx // NX, yx % NX
            more = ref[0, y, x].astype(F32) + ref[1, y, x].astype(F32) + ref[2, y, x].astype(F32)
            self.add((at.z, y, x, slice(None), slice(b, None)), more)

        loop(NY * NX, body)
        self.cy = self.wire.copy(grad.at[at.z, 1 - at.y, :, :, b:], self.third_refs[1], at.yn)

    def third_x(self):
        at, grad, b = self.at, self.grad, self.b
        self.cy.wait_recv()
        ref = self.third_refs[1]
        loop(NX, lambda x: self.add((at.z, at.y, x, slice(None), slice(b, None)), ref[x]))
        self.cx = self.wire.copy(grad.at[at.z, at.y, 1 - at.x, :, b:], self.third_refs[2], at.xn)

    def result(self):
        at, b = self.at, self.b
        total = self.grad[at.z, at.y, at.x, :, :b].astype(F32)
        for step in range(1, NZ):
            self.sz[step - 1].wait_recv()
            total = total + self.three[step - 1].astype(F32)
        return total

    def third_result(self):
        at = self.at
        self.cx.wait_recv()
        return self.grad[at.z, at.y, at.x, :, self.b :].astype(F32) + self.third_refs[2][
            ...
        ].astype(F32)


def layer(unit, names, *refs):
    (
        mix_ref, gain1_ref, gain2_ref, seg_any, in_any, cot_any,
        q_any, k_any, v_any, o_any, up_any, down_any, hist_ref,
        out_ref, gin_ref, pack_ref, gdown_ref, small_ref,
    ) = refs[:18]
    s = dict(zip(names, refs[18:]))
    seg_ref, in_ref, cot_ref = s["seg"], s["in"], s["cot"]
    q_ref, k_ref, v_ref, o_ref, up_ref, down_ref = (s[n] for n in ("w0", "w1", "w2", "w3", "w4", "w5"))
    tokens, width = in_ref.shape
    length = 2 * tokens
    half = width // 2
    ff_half = up_ref.shape[1] // 2
    pairs = half // 128
    share = q_ref.shape[0]
    down_rows = down_ref.shape[0]
    blocks = length // BLOCK
    hist = hist_ref.shape[0]
    at = Place(unit)
    k, o = at.k, at.o
    wire = Wire(s["send"], s["recv"])

    barrier = pltpu.get_barrier_semaphore()
    for device in (*at.block, at.zn(1), at.zn(2), at.zn(3)):
        pl.semaphore_signal(barrier, inc=1, device_id=device, device_id_type=MESH)
    gets = []
    for src, dst in (
        (q_any, q_ref), (k_any, k_ref), (v_any, v_ref), (o_any, o_ref), (up_any, up_ref),
        (down_any, down_ref), (seg_any, seg_ref), (in_any, in_ref), (cot_any, cot_ref),
    ):
        gets.append(pltpu.make_async_copy(src, dst, s["isem"].at[len(gets)]))
        gets[-1].start()
    hist_rows = s["hbuf"].shape[2]
    hist_chunks = tokens // hist_rows

    def fetch(i):
        return pltpu.make_async_copy(
            hist_ref.at[:, pl.ds(i * hist_rows, hist_rows)],
            s["hbuf"].at[i % HBUF],
            s["hsem"].at[i % HBUF],
        )

    for i in range(HBUF - 1):
        fetch(i).start()

    for made in gets[:3]:
        made.wait()

    xs, xr = s["xs"], s["xr"]
    qkv_cols = 3 * half
    blk = down_rows
    for h in range(2):
        c = h * half
        for i in range(pairs):
            for j, ref in enumerate((q_ref, k_ref, v_ref)):
                xs[h, :, 384 * i + 128 * j : 384 * i + 128 * j + 128] = ref[
                    :, c + 128 * i : c + 128 * i + 128
                ].astype(F32)
    ga = s["ga"]
    ga[k, at.z, at.y, at.x] = jnp.zeros((8, 128), F32)
    ga[k, at.z, at.y, at.x, 0:1, :share] = gain1_ref[...].astype(F32)
    ga[k, at.z, at.y, at.x, 1:2, :share] = gain2_ref[...].astype(F32)

    pl.semaphore_wait(barrier, 10)

    swap = [wire.copy(xs.at[o, :, :qkv_cols], xr.at[:, :qkv_cols], at.core)]
    gain_z = [
        wire.copy(ga.at[k, at.z, at.y, at.x], ga.at[k, at.z, at.y, at.x], at.zn(step))
        for step in range(1, NZ)
    ]
    for made in gets[3:6]:
        made.wait()
    s["wdown"][at.z, at.y, at.x] = down_ref[...]
    gather_down = Gather(wire, at, s["wdown"], width // 3, 2 * width // 3)
    gather_down.third_x()
    gather_down.pass_mid(0)
    wide = up_ref[...].astype(F32)
    for h in range(2):
        c = h * half
        xs[h, :, qkv_cols : qkv_cols + half] = o_ref[:, c : c + half].astype(F32)
        xs[h, :, qkv_cols + half :] = jnp.concatenate(
            [
                wide[:, 2 * blk * i + blk * h : 2 * blk * i + blk * h + blk]
                for i in range(GROUPS)
            ],
            axis=1,
        )
    swap.append(wire.copy(xs.at[o, :, qkv_cols:], xr.at[:, qkv_cols:], at.core))

    own0 = pl.multiple_of(k * tokens, tokens)
    other0 = pl.multiple_of(o * tokens, tokens)

    def own(i, size):
        return pl.ds(pl.multiple_of(own0 + i * size, size), size)

    def other(i, size):
        return pl.ds(pl.multiple_of(other0 + i * size, size), size)

    mix_last = mix_ref[hist]
    gbl, norm, sec, gfl = s["gbl"], s["norm"], s["sec"], s["gfl"]

    def own_block(cols):
        mine = xs[k, :, cols]
        theirs = xr[:, cols]
        upper = jnp.where(k == 0, mine, theirs)
        lower = jnp.where(k == 0, theirs, mine)
        return jnp.concatenate([upper, lower], axis=0).astype(BF16)

    gather_qkv = Gather(wire, at, s["wqkv"], 640)
    gather_o = Gather(wire, at, s["wo"], 128)
    gather_up = Gather(wire, at, s["wup"], UP_CUTS[0] * ff_half // 12, UP_CUTS[1] * ff_half // 12)
    swap[0].wait_recv()
    s["wqkv"][at.z, at.y, at.x] = own_block(slice(0, qkv_cols))
    gather_qkv.z.start()
    gather_qkv.pass_mid(0)
    swap[1].wait_recv()
    s["wo"][at.z, at.y, at.x] = own_block(slice(qkv_cols, qkv_cols + half))
    s["wup"][at.z, at.y, at.x] = own_block(slice(qkv_cols + half, qkv_cols + half + ff_half))
    gather_up.third_x()
    gather_up.pass_mid(0)
    todo = [
        lambda: (gather_qkv.pass_last(0), gather_o.z.start()),
        lambda: (
            gather_qkv.z.take(2),
            gather_qkv.pass_mid(1),
            gather_o.pass_mid(0),
            gather_up.pass_last(0),
            gather_up.z.start(),
        ),
        lambda: (
            gather_qkv.z.take(3),
            gather_qkv.pass_mid(2),
            gather_up.third_y(),
            gather_down.third_y(),
        ),
        lambda: (
            gather_qkv.pass_mid(3),
            gather_o.z.take(2),
            gather_o.z.take(3),
        ),
        lambda: (
            gather_qkv.pass_last(1),
            gather_qkv.pass_last(2),
            gather_up.z.take(2),
        ),
        lambda: (
            gather_qkv.pass_last(3),
            gather_up.z.take(3),
            gather_up.third_z(),
            gather_down.z.start(),
            gather_o.pass_last(0),
        ),
        lambda: (gather_up.pass_mid(1), gather_o.pass_mid(1, 2, 3)),
    ]
    later = [
        lambda: (gather_up.pass_mid(2, 3), gather_up.cz.take(2), gather_up.cz.take(3)),
        lambda: (gather_o.pass_last(1), gather_o.pass_last(2), gather_down.z.take(2)),
        lambda: (gather_o.pass_last(3), gather_up.pass_last(1), gather_down.z.take(3)),
        lambda: gather_down.third_z(),
        lambda: gather_up.pass_last(2),
        lambda: (gather_up.pass_last(3), gather_down.cz.take(2)),
        lambda: (gather_down.pass_mid(1, 2), gather_down.cz.take(3)),
        lambda: (gather_down.pass_last(0), gather_down.pass_mid(3)),
        lambda: gather_down.pass_last(1),
        lambda: gather_down.pass_last(2),
        lambda: gather_down.pass_last(3),
    ]

    def pump(count=1):
        for _ in range(count):
            if todo:
                todo.pop(0)()

    for made in gets[6:]:
        made.wait()
    seg = seg_ref[...].astype(F32)
    seg_col = jnp.transpose(jnp.broadcast_to(seg, (128, length)))
    start_row = jnp.zeros((1, length), F32)
    start_col = jnp.zeros((length, 128), F32)
    for d in range(7):
        count = jnp.sum(jnp.where(seg == d, 1.0, 0.0), axis=1, keepdims=True)
        start_row = start_row + jnp.where(seg > d, count, 0.0)
        start_col = start_col + jnp.where(seg_col > d, count, 0.0)
    s["start_row"][...] = jnp.broadcast_to(start_row, (8, length))
    s["start_col"][...] = start_col
    lane = lax.broadcasted_iota(jnp.int32, (1, 128), 1)
    first_half = (lane % HD) < (HD // 2)

    def rope_tables(i):
        rows = rows_of(i, 64)
        order = (lax.broadcasted_iota(jnp.int32, (64, 128), 0) + i * 64).astype(F32)
        angles = (order - s["start_col"][rows, :]) * freq
        s["cos"][rows, :] = jnp.cos(angles)
        sine = jnp.sin(angles)
        s["sin"][rows, :] = jnp.where(first_half, -sine, sine)

    freq = jnp.zeros((1, 128), F32)
    for i in range(HD // 2):
        rate = float(np.float32(10000.0 ** (-2.0 * i / HD)))
        freq = jnp.where(lane % (HD // 2) == i, rate, freq)
    loop(length // 64, rope_tables)
    for step in range(1, NZ):
        gain_z[step - 1].wait_recv()
    gain_x = wire.copy(ga.at[k, :, at.y, at.x], ga.at[k, :, at.y, at.x], at.xn)
    pump()

    def low_block(i):
        gbl[own(i, 32), :] = (mix_last * cot_ref[rows_of(i, 32), :].astype(F32)).astype(BF16)

    loop(tokens // 32, low_block)
    send_gbl = wire.copy(
        gbl.at[pl.ds(own0, tokens)], gbl.at[pl.ds(own0, tokens)], at.core
    )
    pump()

    def history_chunk(i):
        if i + HBUF - 1 < hist_chunks:
            fetch(i + HBUF - 1).start()
        fetch(i).wait()

        def group(r, sums):
            rows = rows_of(r, 16)
            whole = pl.ds(pl.multiple_of(i * hist_rows + r * 16, 16), 16)
            cot = cot_ref[whole, :].astype(F32)
            total = jnp.zeros((16, width), F32)
            out = []
            for j in range(hist):
                earlier = s["hbuf"][i % HBUF, j, rows, :].astype(F32)
                total = total + mix_ref[j] * earlier
                term = fold_rows(earlier * cot)
                part = sums[j]
                for c in range(0, width, 128):
                    part = part + term[:, c : c + 128]
                out.append(part)
            s["acc"][whole, :] = total
            return tuple(out)

        sums = lax.fori_loop(
            0, hist_rows // 16, group, tuple(s["mixacc"][j] for j in range(hist))
        )
        for j in range(hist):
            s["mixacc"][j] = sums[j]

    s["mixacc"][...] = jnp.zeros_like(s["mixacc"])
    history_chunk(0)
    history_chunk(1)
    gain_x.wait_recv()
    gain_y = wire.copy(ga.at[k, :, at.y], ga.at[k, :, at.y], at.yn)
    pump()
    history_chunk(2)
    history_chunk(3)
    pump()
    history_chunk(4)
    gain_y.wait_recv()
    gain_c = wire.copy(ga.at[k], ga.at[k], at.core)
    pump()
    gain_c.wait_recv()

    lanes = lax.broadcasted_iota(jnp.int32, (128, width), 1).astype(F32)
    rows_i = lax.broadcasted_iota(jnp.int32, (128, width), 0)
    owner = jnp.floor((lanes + 0.5) * (1.0 / share))
    spread = jnp.where(lanes - share * owner == rows_i.astype(F32), 1.0, 0.0).astype(BF16)
    gain_rows = [jnp.zeros((1, width), F32), jnp.zeros((1, width), F32)]
    for kk in range(2):
        tiles = ga[kk].reshape(GROUPS * 8, 128).astype(BF16)
        wide = mm(tiles, spread)
        for r in range(2):
            hit = ((rows_i % 8) == r) & (owner == (2 * (rows_i // 8) + kk).astype(F32))
            gain_rows[r] = gain_rows[r] + jnp.sum(
                jnp.where(hit, wide, 0.0), axis=0, keepdims=True
            )
    s["gain"][...] = jnp.concatenate([gain_rows[0], gain_rows[1], jnp.zeros((6, width), F32)], axis=0)

    def norm_one(i):
        xhat, s["kept_one"][rows_of(i, 128), :] = normalize(in_ref[rows_of(i, 128), :].astype(F32))
        norm[own(i, 128), :] = (xhat * s["gain"][0:1, :]).astype(BF16)

    loop(tokens // 128, norm_one)
    send_norm = wire.copy(norm.at[pl.ds(own0, tokens)], norm.at[pl.ds(own0, tokens)], at.core)
    pump()
    for i in range(5, hist_chunks):
        history_chunk(i)
        if i % 3 == 1:
            pump()
    while len(todo) > 0:
        pump()
    todo.extend(later)
    send_norm.wait_recv()
    send_gbl.wait_recv()
    gather_qkv.finish()

    qs, ks, vs = s["q"], s["kk"], s["v"]

    def turn(value, rows, sign):
        partner = jnp.where(first_half, pltpu.roll(value, 96, 1), pltpu.roll(value, 32, 1))
        return value * s["cos"][rows, :] + (sign * partner) * s["sin"][rows, :]

    def project(i):
        rows = rows_of(i, BLOCK)
        left = norm[rows, :]
        both_pairs = mm(left, s["wqkv"][:, :, :, :, :768].reshape(width, 768))
        for p in range(pairs):
            if p < 2:
                wide = both_pairs[:, 384 * p : 384 * p + 384]
            else:
                wide = mm(left, s["wqkv"][:, :, :, :, 768:].reshape(width, qkv_cols - 768))
            cols = slice(128 * p, 128 * p + 128)
            qs[rows, cols] = (turn(wide[:, :128], rows, 1.0).astype(BF16) * HD**-0.5).astype(BF16)
            ks[rows, cols] = turn(wide[:, 128:256], rows, 1.0).astype(BF16)
            vs[rows, cols] = wide[:, 256:].astype(BF16)

    for i in range(blocks):
        project(i)
        pump()

    lane_low = lane < HD
    ones = [
        jnp.where(lane_low, 1.0, 0.0).astype(BF16),
        jnp.where(lane_low, 0.0, 1.0).astype(BF16),
    ]

    def attend(p, b):
        cols = slice(128 * p, 128 * p + 128)
        r0 = b * tokens
        rows = slice(r0, r0 + tokens)
        here_q = lax.broadcasted_iota(jnp.int32, (tokens, tokens), 0)
        here_k = lax.broadcasted_iota(jnp.int32, (tokens, tokens), 1)
        start = s["start_col"][rows, 0:1]
        outs, tops = [], []
        for h in range(2):
            query = qs[rows, cols] * ones[h]
            near = mm_nt(query, ks[rows, cols])
            near = jnp.where(
                (here_k <= here_q) & ((here_k + r0).astype(F32) >= start), near, MASKED
            )
            top = jnp.max(near, axis=1, keepdims=True)
            if b:
                far = mm_nt(query, ks[0:r0, cols])
                far_k = lax.broadcasted_iota(jnp.int32, (1, r0), 1).astype(F32)
                far = jnp.where(far_k >= start, far, MASKED)
                top = jnp.maximum(top, jnp.max(far, axis=1, keepdims=True))
            raw = jnp.exp(near - top).astype(BF16)
            out = mm(raw, vs[rows, cols] * ones[h] + ones[1 - h])
            if b:
                raw = jnp.exp(far - top).astype(BF16)
                out = out + mm(raw, vs[0:r0, cols] * ones[h] + ones[1 - h])
            outs.append(out)
            tops.append(top)
        total = jnp.where(lane_low, pltpu.roll(outs[0], HD, 1), pltpu.roll(outs[1], HD, 1))
        mixed = jnp.where(lane_low, outs[0], outs[1]) / total
        s["mix"][rows, cols] = mixed.astype(BF16)
        s["mixf"][rows, cols] = mixed
        log_total = jnp.transpose(jnp.where(lane_low, tops[0], tops[1]) + jnp.log(total))
        s["lse"][p, 0:1, rows] = log_total[0:1]
        s["lse"][p, 1:2, rows] = log_total[HD : HD + 1]

    wo, wof = s["wo"], s["wof"]
    my_cols = lane_cut(k * half, half)
    for p in range(pairs):
        for b in range(2):
            attend(p, b)
        pump()
        if p == 1:
            gather_o.finish()
            swap_o = wire.copy(wo.at[pl.ds(2 * o, 2)], wof.at[:, :, :, :, my_cols], at.core)
            wof[:, :, :, :, my_cols] = wo[pl.ds(2 * k, 2)]

    swap_o.wait_recv()

    def output_weight():
        return wof[...].reshape(half, width)

    part_s, part_r = s["part_s"], s["part_r"]
    quarter = tokens // 2

    def send_parts(make, store, recv, pieces=1):
        made = []
        size = tokens // pieces
        for i in range(pieces):
            make(other(i, size), rows_of(i, size), store)
            for j in range(2 // pieces):
                to = pl.ds((i * (2 // pieces) + j) * quarter, quarter)
                made.append(wire.copy(store.at[to], recv.at[to], at.core))
        return made

    def attended(rows, to, store):
        store[to, :] = mm(s["mix"][rows, :], output_weight()).astype(store.dtype)

    arrive = send_parts(attended, gfl.at[pl.ds(0, tokens)], gfl.at[pl.ds(tokens, tokens)], 2)
    first = s["first"]
    for i in range(2):
        attended(own(i, quarter), rows_of(i, quarter), first)
    send_sec = []
    for i in range(2):
        arrive[i].wait_recv()

        def norm_two(j):
            rows = pl.ds(pl.multiple_of(i * quarter + j * 128, 128), 128)
            there = pl.ds(pl.multiple_of(tokens + i * quarter + j * 128, 128), 128)
            value = in_ref[rows, :].astype(F32) + (first[rows, :] + gfl[there, :].astype(F32))
            first[rows, :] = value
            xhat, s["kept_two"][rows, :] = normalize(value)
            to = pl.ds(pl.multiple_of(own0 + i * quarter + j * 128, 128), 128)
            sec[to, :] = (xhat * s["gain"][1:2, :]).astype(BF16)

        loop(quarter // 128, norm_two)
        send_sec.append(wire.copy(sec.at[own(i, quarter)], sec.at[own(i, quarter)], at.core))
    pump()
    gather_up.finish()
    hid, dgelu = s["hid"], s["dgelu"]
    wup, wdown = s["wup"], s["wdown"]
    root_2_pi = float(np.sqrt(2.0 / np.pi).astype(np.float32))

    def expand(start):
        rows = pl.ds(start, tokens)

        def part(cols):
            v = mm(sec[rows, :], wup[:, :, :, :, cols].reshape(width, 256))
            vv = v * v
            t = jnp.tanh(v * (root_2_pi + (0.044715 * root_2_pi) * vv))
            a = 0.5 * t + 0.5
            out = v * a
            hid[rows, cols] = out.astype(BF16)
            slope = 2.0 * root_2_pi + (6.0 * 0.044715 * root_2_pi) * vv
            dgelu[rows, cols] = (a + out * (1.0 - a) * slope).astype(BF16)

        def body(j):
            for c in range(3):
                part(lane_cut(j * 768 + c * 256, 256))

        loop(ff_half // 768, body)
        pump()

    expand(own0)
    for made in send_sec:
        made.wait_recv()
    expand(other0)

    gdown = s["gdown"]

    def grad_down(zz):
        left = hid[:, 384 * zz : 384 * zz + 384]
        wide = mm_tn(left, gbl[...]).astype(BF16)
        for i in range(2):
            gdown[i][zz] = wide[:, i * half : (i + 1) * half].reshape(NY, NX, down_rows, half)

    for zz in range(NZ):
        grad_down(zz)
        if zz % 2:
            pump()
    reduce_down = [
        Reduce(wire, at, gdown[i], (half // 3, 2 * half // 3), *s["rdown"][i]) for i in range(2)
    ]
    for r in reduce_down:
        r.first()

    def back_hidden(step):
        gather_down.arrived(step)
        zz = gather_down.layer(step)
        weight = wdown[zz].reshape(NY * NX * down_rows, width)
        cols = lane_cut(zz * 384, 384)
        for start in (0, tokens):
            rows = slice(start, start + tokens)
            grad = mm_nt(gbl[rows, :], weight)
            dgelu[rows, cols] = (grad * dgelu[rows, cols].astype(F32)).astype(BF16)

    back_hidden(0)
    pump()
    back_hidden(1)
    pump()
    back_hidden(2)
    assert not todo
    back_hidden(3)

    def back_second(rows, to, store):
        store[to, :] = mm_nt(dgelu[rows, :], wup[...].reshape(width, ff_half))

    wire.sent(*arrive)
    arrive = send_parts(back_second, part_s, part_r)
    reduce_down[0].second()
    gsec = s["gfirst"]
    back_second(own(0, tokens), slice(0, tokens), gsec)
    gup = s["gup"]
    small = s["small"]
    small[...] = jnp.zeros_like(small)

    def grad_up(j, i):
        left = sec[:, 384 * j : 384 * j + 384]
        wide = mm_tn(left, dgelu[:, i * width : (i + 1) * width]).astype(BF16)
        gup[i][2 * j : 2 * j + 2] = wide.reshape(2, NY, NX, 2 * share, width)

    def norm_two_back(i):
        arrive[i].wait_recv()

        def body(j, total):
            rows = pl.ds(pl.multiple_of(i * quarter + j * 64, 64), 64)
            grad = gsec[rows, :] + part_r[rows, :]
            xhat, root = normalize_again(first[rows, :], s["kept_two"][rows, :])
            part = norm_back(xhat, root, s["gain"][1:2, :], grad)
            full = mix_last * cot_ref[rows, :].astype(F32) + part
            gsec[rows, :] = full
            to = pl.ds(pl.multiple_of(own0 + i * quarter + j * 64, 64), 64)
            gfl[to, :] = full.astype(BF16)
            return total + fold_rows(grad * xhat)

        total = lax.fori_loop(0, quarter // 64, body, jnp.zeros((8, width), F32))
        small[1:2, :] = small[1:2, :] + jnp.sum(total, axis=0, keepdims=True)
        return wire.copy(gfl.at[own(i, quarter)], gfl.at[own(i, quarter)], at.core)

    reduce_up = [
        Reduce(wire, at, gup[i], (width // 2, width), *s["rup"][i]) for i in range(2)
    ]

    def start_up(i):
        for j in range(2):
            grad_up(j, i)
        reduce_up[i].first()

    start_up(0)
    reduce_down[1].second()
    send_gfl = [norm_two_back(0), norm_two_back(1)]
    start_up(1)
    reduce_down[0].third()

    gm = s["gm"]

    def back_mixed(rows):
        gm[rows, :] = mm_nt(gfl[rows, :], output_weight()).astype(BF16)

    back_mixed(own(0, tokens))
    for made in send_gfl:
        made.wait_recv()
    back_mixed(other(0, tokens))
    go = s["go"]
    wide = mm_tn(s["mix"][...], gfl[...])
    left, right = wide[:, :half], wide[:, half:]
    blocks_o = (2, NY, NX, 2 * share, half)
    s["gox"][...] = jnp.where(k == 0, right, left).astype(BF16).reshape(blocks_o)
    swap_go = wire.copy(s["gox"], go.at[pl.ds(2 * k, 2)], at.core)
    go[pl.ds(2 * k, 2)] = jnp.where(k == 0, left, right).astype(BF16).reshape(blocks_o)
    reduce_o = Reduce(wire, at, go, (128, half), *s["ro"])

    lse, delta = s["lse"], s["delta"]
    wire.sent(send_gbl, *send_sec)
    heads_in = [(gbl, 0), (gbl, 384), (sec, 0)]
    gpair = s["gqkv"]
    grad_query = s["dq"]
    reduce_qkv = [
        Reduce(wire, at, gpair[p], (CUTS[p % 3], 384), *s["rqkv"][p]) for p in range(pairs)
    ]

    nothing = lambda: None
    todo.extend(
        [
            reduce_up[0].second,
            reduce_down[1].third,
            reduce_down[0].third_y,
            nothing,
            nothing,
            reduce_up[1].second,
            lambda: (swap_go.wait_recv(), reduce_o.first()),
            reduce_down[1].third_y,
            reduce_up[0].third,
            nothing,
            reduce_down[0].third_x,
            reduce_qkv[0].second,
            reduce_up[1].third,
            reduce_o.second,
            nothing,
            lambda: (reduce_qkv[0].third(), reduce_o.third()),
            lambda: (reduce_qkv[1].second(), reduce_down[1].third_x()),
            reduce_qkv[2].second,
            reduce_qkv[1].third,
            reduce_qkv[2].third,
        ]
    )

    def attend_back(p, b):
        cols = slice(128 * p, 128 * p + 128)
        r0 = b * BLOCK
        rows = slice(r0, r0 + BLOCK)
        after = slice(r0, length)
        count = length - r0
        here_k = lax.broadcasted_iota(jnp.int32, (BLOCK, count), 0)
        here_q = lax.broadcasted_iota(jnp.int32, (BLOCK, count), 1)
        allowed = (here_k <= here_q) & (
            (here_k + r0).astype(F32) >= s["start_row"][0:1, after]
        )
        key, value = ks[rows, cols], vs[rows, cols]
        query, grad = qs[after, cols], gm[after, cols]
        dk = jnp.zeros((BLOCK, 128), F32)
        dv = jnp.zeros((BLOCK, 128), F32)
        dq = jnp.zeros((count, 128), F32)
        for h in range(2):
            key_h = key * ones[h]
            scores = mm_nt(key_h, query)
            weights = jnp.exp(jnp.where(allowed, scores - lse[p, h : h + 1, after], MASKED))
            grad_w = mm_nt(value * ones[h], grad)
            grad_s = (weights * (grad_w - delta[p, h : h + 1, after])).astype(BF16)
            dv = dv + mm(weights.astype(BF16), grad * ones[h])
            dk = dk + mm(grad_s, query * ones[h])
            dq = dq + mm_tn(grad_s, key_h)
        gqkv, base = heads_in[p]
        gqkv[rows, base + 256 : base + 384] = dv.astype(BF16)
        gqkv[rows, base + 128 : base + 256] = turn(
            dk.astype(BF16).astype(F32), rows, -1.0
        ).astype(BF16)
        if b == 0:
            grad_query[...] = dq
        else:
            grad_query[after, :] = grad_query[after, :] + dq

    out_s, out_r = s["out_s"], s["out_r"]

    def contract(rows, to, store):
        store[to, :] = mm(hid[rows, :], wdown[...].reshape(ff_half, width)).astype(BF16)

    outb = gfl.at[pl.ds(0, tokens)]
    put_out = pltpu.make_async_copy(outb, out_ref, s["osem"].at[0])

    def write_output(arrive_out):
        wire.sent(*send_gfl)
        mine = s["mixf"]
        for h in range(2):
            weight = wdown[...].reshape(ff_half, width)[:, h * half : h * half + half]
            mine[h * tokens : h * tokens + tokens, :] = mm(hid[own(0, tokens), :], weight)
        for made in arrive_out:
            made.wait_recv()

        def finish_out(j, total):
            rows = rows_of(j, 64)
            below = pl.ds(pl.multiple_of(tokens + j * 64, 64), 64)
            part = jnp.concatenate([mine[rows, :], mine[below, :]], axis=1)
            block = first[rows, :] + (part + out_r[rows, :].astype(F32))
            outb[rows, :] = (s["acc"][rows, :] + mix_last * block).astype(BF16)
            return total + fold_rows(block * cot_ref[rows, :].astype(F32))

        block_sum = lax.fori_loop(0, tokens // 64, finish_out, jnp.zeros((8, width), F32))
        put_out.start()
        terms = jnp.zeros((1, width), F32)
        wide_lane = lax.broadcasted_iota(jnp.int32, (1, width), 1)
        for j in range(hist):
            terms = jnp.where(wide_lane == j, jnp.sum(s["mixacc"][j]), terms)
        small[2:3, :] = jnp.where(wide_lane == hist, jnp.sum(block_sum), terms)

    for p in range(pairs):
        cols = slice(128 * p, 128 * p + 128)

        def inner(i):
            rows = rows_of(i, BLOCK)
            both = jnp.transpose(s["mixf"][rows, cols] * gm[rows, cols].astype(F32))
            delta[p, 0:1, rows] = jnp.sum(both[:HD], axis=0, keepdims=True)
            delta[p, 1:2, rows] = jnp.sum(both[HD:], axis=0, keepdims=True)

        loop(blocks, inner)
        for b in range(blocks):
            attend_back(p, b)
            pump()

        gqkv, base = heads_in[p]

        def turn_query(i):
            rows = rows_of(i, BLOCK)
            low = (grad_query[rows, :] * HD**-0.5).astype(BF16).astype(F32)
            gqkv[rows, base : base + 128] = turn(low, rows, -1.0).astype(BF16)

        loop(blocks, turn_query)

        def grad_qkv(j):
            left = norm[:, pl.ds(pl.multiple_of(j * 384, 128), 384)]
            wide = mm_tn(left, gqkv[:, base : base + 384]).astype(BF16)
            gpair[p][pl.ds(2 * j, 2)] = wide.reshape(2, NY, NX, 2 * share, 384)

        loop(2, grad_qkv)
        reduce_qkv[p].first()
        pump()

    wire.sent(*arrive)

    def normed_grad(rows):
        weight = s["wqkv"][...].reshape(width, qkv_cols)
        return mm_nt(gbl[rows, :], weight[:, :768]) + mm_nt(sec[rows, :384], weight[:, 768:])

    def back_normed(rows, to, store):
        store[to, :] = normed_grad(rows)

    arrive = send_parts(back_normed, part_s, part_r)
    arrive_out = send_parts(contract, out_s, out_r)
    pump(2)
    write_output(arrive_out)
    own_s = first
    back_normed(own(0, tokens), slice(0, tokens), own_s)
    pump()
    total = jnp.zeros((8, width), F32)
    for i in range(2):
        arrive[i].wait_recv()

        def norm_one_back(j, total):
            rows = pl.ds(pl.multiple_of(i * quarter + j * 64, 64), 64)
            grad = own_s[rows, :] + part_r[rows, :]
            xhat, root = normalize_again(in_ref[rows, :].astype(F32), s["kept_one"][rows, :])
            gsec[rows, :] = gsec[rows, :] + norm_back(xhat, root, s["gain"][0:1, :], grad)
            return total + fold_rows(grad * xhat)

        total = lax.fori_loop(0, quarter // 64, norm_one_back, total)
        if i == 0:
            pump()
    put_gin = pltpu.make_async_copy(gsec, gin_ref, s["osem"].at[1])
    put_gin.start()
    small[0:1, :] = jnp.sum(total, axis=0, keepdims=True)

    sp, sz = s["small_p"], s["small_z"]
    sp[k, at.y, at.x] = small[...]
    mine = sp.at[k, at.y, at.x]
    step_p = [wire.copy(mine, mine, device) for device in at.block]
    pump()

    wire.sent(*swap)
    fin, fin_r = xs, xr
    def settle(reduce, c, size):
        total = reduce.result()
        fin[0, :, c : c + size] = total[:share]
        fin[1, :, c : c + size] = total[share:]
        return wire.copy(fin.at[o, :, pl.ds(c, size)], fin_r.at[:, pl.ds(c, size)], at.core)

    up0 = qkv_cols + half
    settled = [settle(reduce_up[i], up0 + i * width, width) for i in range(2)]
    settled.append(settle(reduce_o, qkv_cols, half))
    for i in range(2):
        c = i * half + 2 * half // 3
        s["fin_d"][:, i * half : c] = reduce_down[i].result()
        s["fin_d"][:, c : (i + 1) * half] = reduce_down[i].third_result()
    put_down = pltpu.make_async_copy(s["fin_d"], gdown_ref, s["osem"].at[2])
    put_down.start()
    settled.append(settle(reduce_qkv[0], 0, 384))
    for made in step_p:
        made.wait_recv()
    both = sp[0] + sp[1]
    sz[at.z] = (both[0, 0] + both[0, 1]) + (both[1, 0] + both[1, 1])
    step_z = [wire.copy(sz.at[at.z], sz.at[at.z], at.zn(step)) for step in range(1, NZ)]
    for p in range(1, pairs):
        settled.append(settle(reduce_qkv[p], 384 * p, 384))
    assert not todo
    put_mine = pltpu.make_async_copy(fin.at[k], pack_ref.at[k], s["osem"].at[3])
    put_mine.start()
    for made in settled:
        made.wait_recv()
    put_other = pltpu.make_async_copy(fin_r, pack_ref.at[o], s["osem"].at[4])
    put_other.start()
    for made in step_z:
        made.wait_recv()
    small[...] = ((sz[0] + sz[1]) + sz[2]) + sz[3]
    put_small = pltpu.make_async_copy(small, small_ref, s["osem"].at[5])
    put_small.start()
    for made in (put_down, put_mine, put_other, put_small):
        made.wait()
    put_out.wait()
    put_gin.wait()
    wire.close()


def finish(unit, *refs):
    mix_ref, cot_ref, small_ref, pack_ref, gdown_ref, out_ref, gin_ref = refs[:7]
    out_o, gin_o, ghist_o, gdown_o = refs[7:11]
    rest_o = refs[11:19]
    cot, small, pack, buffer, out, gin, gdown = refs[19:26]
    rest = refs[26:34]
    sems, hsems = refs[34:]
    hist = ghist_o.shape[0]
    tokens, width = cot.shape
    share = pack.shape[1]
    half = width // 2
    gets = [
        pltpu.make_async_copy(src, dst, sems.at[i])
        for i, (src, dst) in enumerate(
            (
                (cot_ref, cot),
                (pack_ref, pack),
                (small_ref, small),
                (out_ref, out),
                (gin_ref, gin),
                (gdown_ref, gdown),
            )
        )
    ]
    for made in gets:
        made.start()
    gets[0].wait()
    puts = []
    rows = 128
    for j in range(hist):

        def scale(i):
            part = rows_of(i, rows)
            buffer[j, part, :] = (mix_ref[j] * cot[part, :].astype(F32)).astype(BF16)

        loop(tokens // rows, scale)
        puts.append(pltpu.make_async_copy(buffer.at[j], ghist_o.at[j], hsems.at[j]))
        puts[j].start()
    for made in gets[1:]:
        made.wait()
    moves = [
        pltpu.make_async_copy(src, dst, sems.at[i])
        for i, (src, dst) in enumerate(((out, out_o), (gin, gin_o), (gdown, gdown_o)))
    ]
    for made in moves:
        made.start()
    gain1, gain2, mix, gq, gk, gv, go, gup = rest
    device = (lax.axis_index("batch") // unit) * 2 + lax.axis_index("seq")
    own = pltpu.roll(small[...], width - device * share, 1)
    gain1[...] = own[0:1, :share]
    gain2[...] = own[1:2, :share]
    mix[...] = small[2:3, : hist + 1]
    for h in range(2):
        for p in range(half // 128):
            for j, ref in enumerate((gq, gk, gv)):
                c = 384 * p + 128 * j
                ref[:, h * half + 128 * p : h * half + 128 * p + 128] = pack[h, :, c : c + 128]
        go[:, h * half : h * half + half] = pack[h, :, 3 * half : 4 * half]
    blk = gdown_o.shape[0]
    gup[...] = jnp.concatenate(
        [
            pack[h, :, 4 * half + blk * i : 4 * half + blk * i + blk]
            for i in range(GROUPS)
            for h in range(2)
        ],
        axis=1,
    )
    for i, (src, dst) in enumerate(zip(rest, rest_o)):
        puts.append(pltpu.make_async_copy(src, dst, sems.at[6 + i]))
        puts[-1].start()
    for made in puts + moves:
        made.wait()


def local(
    unit,
    inputs,
    history,
    segment_ids,
    cotangent,
    mix_weights,
    attn_gain,
    query_weight,
    key_weight,
    value_weight,
    output_weight,
    mlp_gain,
    up_weight,
    down_weight,
):
    rows, tokens, width = inputs.shape
    hist = history.shape[0]
    length = segment_ids.shape[1]
    half = width // 2
    ff_half = up_weight.shape[1] // 2
    share = width // (2 * GROUPS)
    both = 2 * share
    down_share = 2 * ff_half // (2 * GROUPS)
    pairs = half // 128
    seq = lax.axis_index("seq")
    batch = lax.axis_index("batch")
    group_device = (batch // unit) * 2 + seq
    weights = [query_weight, key_weight, value_weight, output_weight, up_weight, down_weight]
    gains = [attn_gain, mlp_gain]
    if unit > 1:
        def widen(value):
            whole = lax.all_gather(value, ("batch", "seq"), axis=0, tiled=True)
            size = value.shape[0] * unit
            return lax.dynamic_slice_in_dim(whole, group_device * size, size)

        weights = [widen(value) for value in weights]
        gains = [widen(value) for value in gains]
    sizes = []

    def scratch(name, shape, dtype=BF16):
        sizes.append((name, pltpu.VMEM(shape, dtype)))

    dims = (NZ, NY, NX)

    def reduction(rows_in, columns, a, b):
        rest = columns - b
        third = [
            pltpu.VMEM((NZ - 1, NY, NX, rows_in, rest), BF16),
            pltpu.VMEM((NX, rows_in, rest), BF16),
            pltpu.VMEM((rows_in, rest), BF16),
        ]
        return [
            pltpu.VMEM((NZ, NX, rows_in, a), BF16),
            pltpu.VMEM((NZ, NY, rows_in, b - a), BF16),
            pltpu.VMEM((NZ, rows_in, b), BF16),
            pltpu.VMEM((NZ - 1, rows_in, b), BF16),
        ] + (third if rest else [])

    sizes.append(("send", pltpu.SemaphoreType.DMA((SENDS,))))
    sizes.append(("recv", pltpu.SemaphoreType.DMA((COPIES,))))
    sizes.append(("hsem", pltpu.SemaphoreType.DMA((HBUF,))))
    sizes.append(("osem", pltpu.SemaphoreType.DMA((6,))))
    scratch("fin_d", (down_share, width), F32)
    sizes.append(("isem", pltpu.SemaphoreType.DMA((9,))))
    scratch("seg", (1, length), jnp.int32)
    scratch("in", (tokens, width))
    scratch("cot", (tokens, width))
    for i, value in enumerate(weights):
        scratch("w%d" % i, value.shape)
    scratch("hbuf", (HBUF, hist, 32, width))
    scratch("xs", (2, share, 2 * half + 2 * half + ff_half), F32)
    scratch("xr", (share, 2 * half + 2 * half + ff_half), F32)
    scratch("ga", (2,) + dims + (8, 128), F32)
    scratch("gain", (8, width), F32)
    scratch("wqkv", dims + (both, 3 * half))
    scratch("wo", dims + (both, half))
    scratch("wof", (2, NY, NX, both, width))
    scratch("wup", dims + (both, ff_half))
    scratch("wdown", dims + (down_share, width))
    for name in ("gbl", "norm", "sec", "gfl"):
        scratch(name, (length, width))
    scratch("kept_one", (tokens, 128), F32)
    scratch("kept_two", (tokens, 128), F32)
    scratch("start_row", (8, length), F32)
    scratch("start_col", (length, 128), F32)
    scratch("cos", (length, 128), F32)
    scratch("sin", (length, 128), F32)
    scratch("acc", (tokens, width), F32)
    scratch("mixacc", (hist, 8, 128), F32)
    for name in ("q", "kk", "v", "mix", "gm"):
        scratch(name, (length, half))
    scratch("mixf", (length, half), F32)
    scratch("lse", (pairs, 8, length), F32)
    scratch("delta", (pairs, 8, length), F32)
    scratch("dq", (length, 128), F32)
    for name in ("part_s", "part_r", "first", "gfirst"):
        scratch(name, (tokens, width), F32)
    for name in ("out_s", "out_r"):
        scratch(name, (tokens, width))
    scratch("hid", (length, ff_half))
    scratch("dgelu", (length, ff_half))
    scratch("gox", (2, NY, NX, both, half))
    scratch("small", (8, width), F32)
    scratch("small_p", (2, NY, NX, 8, width), F32)
    scratch("small_z", (NZ, 8, width), F32)
    sizes.append(("gdown", [pltpu.VMEM(dims + (down_share, half), BF16) for _ in range(2)]))
    sizes.append(("gup", [pltpu.VMEM(dims + (both, width), BF16) for _ in range(2)]))
    scratch("go", dims + (both, half))
    sizes.append(("gqkv", [pltpu.VMEM(dims + (both, 384), BF16) for _ in range(pairs)]))
    sizes.append(("rdown", [reduction(down_share, half, half // 3, 2 * half // 3) for _ in range(2)]))
    sizes.append(("rup", [reduction(both, width, width // 2, width) for _ in range(2)]))
    sizes.append(("ro", reduction(both, half, 128, half)))
    sizes.append(("rqkv", [reduction(both, 384, CUTS[p % 3], 384) for p in range(pairs)]))
    names = [name for name, _ in sizes]

    vmem = pl.BlockSpec(memory_space=pltpu.VMEM)
    anywhere = pl.BlockSpec(memory_space=pl.ANY)
    smem = pl.BlockSpec(memory_space=pltpu.SMEM)
    shape = jax.ShapeDtypeStruct
    outs = pl.pallas_call(
        functools.partial(layer, unit, names),
        out_shape=(
            shape((tokens, width), BF16),
            shape((tokens, width), F32),
            shape((2, share, 4 * half + ff_half), F32),
            shape((down_share, width), F32),
            shape((8, width), F32),
        ),
        in_specs=[smem, vmem, vmem] + [anywhere] * 10,
        out_specs=[anywhere] * 5,
        scratch_shapes=[size for _, size in sizes],
        compiler_params=pltpu.CompilerParams(
            collective_id=0, has_side_effects=True, vmem_limit_bytes=64 * 1024 * 1024 - 64 * 1024
        ),
    )(
        mix_weights,
        gains[0].reshape(1, share),
        gains[1].reshape(1, share),
        segment_ids,
        inputs.reshape(tokens, width),
        cotangent.reshape(tokens, width),
        *weights,
        history.reshape(hist, tokens, width),
    )
    partial_out, partial_gin, pack, gdown, small = outs
    rest = [
        shape((1, share), F32),
        shape((1, share), F32),
        shape((1, hist + 1), F32),
        shape((share, width), F32),
        shape((share, width), F32),
        shape((share, width), F32),
        shape((share, width), F32),
        shape((share, 2 * ff_half), F32),
    ]
    ends = pl.pallas_call(
        functools.partial(finish, unit),
        out_shape=[
            shape((tokens, width), BF16),
            shape((tokens, width), F32),
            shape((hist, tokens, width), BF16),
            shape((down_share, width), F32),
        ]
        + rest,
        in_specs=[smem] + [anywhere] * 6,
        out_specs=[anywhere] * 12,
        scratch_shapes=[
            pltpu.VMEM((tokens, width), BF16),
            pltpu.VMEM((8, width), F32),
            pltpu.VMEM((2, share, 4 * half + ff_half), F32),
            pltpu.VMEM((hist, tokens, width), BF16),
            pltpu.VMEM((tokens, width), BF16),
            pltpu.VMEM((tokens, width), F32),
            pltpu.VMEM((down_share, width), F32),
        ]
        + [pltpu.VMEM(one.shape, F32) for one in rest]
        + [pltpu.SemaphoreType.DMA((14,)), pltpu.SemaphoreType.DMA((hist,))],
        compiler_params=pltpu.CompilerParams(vmem_limit_bytes=64 * 1024 * 1024 - 64 * 1024),
    )(
        mix_weights,
        cotangent.reshape(tokens, width),
        small,
        pack,
        gdown,
        partial_out,
        partial_gin,
    )
    output, grad_inputs, grad_history, gdown, gain_one, gain_two, mix_grad = ends[:7]
    grads = list(ends[7:]) + [gdown, gain_one.reshape(share), gain_two.reshape(share)]
    mix_grad = mix_grad.reshape(hist + 1)
    if unit > 1:
        def narrow(value):
            whole = jnp.zeros((value.shape[0] * 2 * GROUPS,) + value.shape[1:], F32)
            whole = lax.dynamic_update_slice_in_dim(whole, value, group_device * value.shape[0], 0)
            return lax.psum_scatter(whole, ("batch", "seq"), scatter_dimension=0, tiled=True)

        grads = [narrow(value) for value in grads]
        mix_grad = lax.psum(mix_grad, ("batch", "seq")) / (2 * GROUPS)
    gq, gk, gv, go, gup, gdown, gain_one, gain_two = grads
    return (
        output.reshape(rows, tokens, width),
        grad_inputs.reshape(rows, tokens, width),
        grad_history.reshape(hist, rows, tokens, width),
        mix_grad,
        gain_one,
        gq,
        gk,
        gv,
        go,
        gain_two,
        gup,
        gdown,
    )


def solution(mesh):
    batch = mesh.shape["batch"]
    split = P(("batch", "seq"), None)
    gain = P(("batch", "seq"))
    placed = (
        P("batch", "seq", None),
        P(None, "batch", "seq", None),
        P("batch", None),
        P("batch", "seq", None),
        P(),
        gain,
        split,
        split,
        split,
        split,
        gain,
        split,
        split,
    )
    return jax.shard_map(
        functools.partial(local, batch // GROUPS),
        mesh=mesh,
        in_specs=placed,
        out_specs=(
            P("batch", "seq", None),
            P("batch", "seq", None),
            P(None, "batch", "seq", None),
            P(),
            gain,
            split,
            split,
            split,
            split,
            gain,
            split,
            split,
        ),
        check_vma=False,
    )
```
